256 devices in a mesh: seq: 64 (over z, y, core), head: 4 (over x).
Axes of the slice: x: 4, y: 4, z: 8, core: 2. Of those that a mesh axis runs over, the one named last changes fastest.
Arguments:
- q_res: bfloat16 [49152, 4096], P('seq', 'head'), may hold values from -6 to 6
- k_res: bfloat16 [49152, 4096], P('seq', 'head'), may hold values from -0.5 to 0.5
- v_res: bfloat16 [49152, 4096], P('seq', 'head'), may hold values from -6 to 6
- q_new: bfloat16 [16384, 4096], P('seq', 'head'), may hold values from -6 to 6
- k_new: bfloat16 [16384, 4096], P('seq', 'head'), may hold values from -0.5 to 0.5
- v_new: bfloat16 [16384, 4096], P('seq', 'head'), may hold values from -6 to 6
- admit_dest: int32 [2048], P('seq'), may hold values from 0 to 63, as said below
- admit_slot: int32 [2048], P('seq'), may hold values from 0 to 31, as said below
- boundaries: int32 [32], replicated, may hold values from 1 to 65535, as said below
- rate: float32 [32], P('head'), may hold values from 0 to 1, as said below
Outputs:
- attended: bfloat16 [65536, 4096], P('seq', 'head')
The draws below stay inside these ranges and needn't reach their ends.
Inputs may be any that keep to these rules, and one draw needn't show every extreme that they name: `admit_dest`: each shard is named by exactly 32 blocks; the blocks of one shard's new rows name at most 1 times one shard, and exactly 1 times every shard they name. `admit_slot`: every pair of shard and slot is named by exactly one block. `boundaries`: distinct and increasing. `rate`: Positive.
All inputs are finite; a program needn't handle non-finite values.
Results may differ from the reference program's by a relative error of at most 0.0035.
Values may be sent and summed in bfloat16 or wider, within the bound.
A program may use at most 128 MiB of HBM per device.

```python
import jax
import jax.numpy as jnp
from jax import lax

HEADS = 32
HD = 128
UNIT = 8
BLOCK = 512
RES_DEV = 768
ADM_DEV = 256
NB = 32
MOST = 1
TOKENS = 65536
UNITS = 2048
NEWROWS = 16384
NBOUND = 32
N_SEQ = 64


def admission_plan(key):
    keys = jax.random.split(key, 5)
    groups = NB // MOST
    shifts = jax.random.permutation(keys[0], N_SEQ)[:groups]
    sigma = jax.random.permutation(keys[1], N_SEQ)
    tau = jax.random.permutation(keys[2], N_SEQ)
    unit_index = jnp.arange(NB)
    dest = sigma[(tau[:, None] + shifts[unit_index // MOST][None, :]) % N_SEQ]
    omega = jax.vmap(lambda part_key: jax.random.permutation(part_key, NB))(jax.random.split(keys[3], N_SEQ))
    slot = omega[dest, unit_index[None, :]]
    order = jax.vmap(lambda part_key: jax.random.permutation(part_key, NB))(jax.random.split(keys[4], N_SEQ))
    dest = jnp.take_along_axis(dest, order, axis=1)
    slot = jnp.take_along_axis(slot, order, axis=1)
    return (dest.reshape(UNITS).astype(jnp.int32), slot.reshape(UNITS).astype(jnp.int32))


def draw_admit_dest(key, part):
    return admission_plan(key)[0]


def draw_admit_slot(key, part):
    return admission_plan(key)[1]


def draw_boundaries(key, part):
    key = jax.random.fold_in(key, 11)
    pick_key, side_key = jax.random.split(key, 2)
    inner = jax.random.choice(pick_key, TOKENS // 4, (NBOUND - 2,), replace=False).astype(jnp.int32) + 2
    mirror = jax.random.randint(side_key, (), 0, 2).astype(jnp.int32)
    inner = jnp.where(mirror == 1, TOKENS - inner, inner).astype(jnp.int32)
    inner = jnp.sort(inner).astype(jnp.int32)
    first = jnp.array([1], jnp.int32)
    last = jnp.array([TOKENS - 1], jnp.int32)
    return jnp.concatenate([first, inner, last]).astype(jnp.int32)


def spread_log(key, low, high):
    level = jax.random.uniform(key, (HEADS,), jnp.float32)
    return jnp.exp(jnp.log(low) + level * (jnp.log(high) - jnp.log(low)))


def draw_rate(key, part):
    key = jax.random.fold_in(key, 7)
    first, second, third = jax.random.split(key, 3)
    share = 0.5
    slow = jax.random.uniform(first, (HEADS,), jnp.float32) < share
    slow_rate = spread_log(second, 0.2 / TOKENS, 2.0 / TOKENS)
    fast_rate = spread_log(third, 2.0 / TOKENS, 0.05)
    return jnp.where(slow, slow_rate, fast_rate).astype(jnp.float32)


def shard_levels(stream_key, shape, shards, low, high):
    gain, own = 1.0, jax.random.fold_in(stream_key, 6)
    for position, parts in shards:
        draws = jnp.exp(jax.random.uniform(jax.random.fold_in(own, position), (parts,), jnp.float32, low / len(shards), high / len(shards)))
        gain = gain * jnp.repeat(draws, shape[position] // parts).reshape([-1 if axis == position else 1 for axis in range(len(shape))])
    return gain


def centred(own_key, dims, scale, reach, cuts=(), held_as=jnp.bfloat16):
    loudness = shard_levels(own_key, dims, cuts, -0.22, 0.18) if cuts else 1.0
    values = jax.random.normal(own_key, dims, jnp.float32) * scale * loudness
    return jnp.minimum(jnp.maximum(values, -reach), reach).astype(held_as)


def setup_inputs(seed: int = 0) -> dict:
    key_of = jax.random.split(jax.random.key(seed), 11)
    return {
        "q_res": centred(key_of[0], (N_SEQ * RES_DEV, HEADS * HD), 1.0, 6.0, ((0, 64), (1, 4))),
        "k_res": centred(key_of[1], (N_SEQ * RES_DEV, HEADS * HD), HD ** -0.5, 0.5, ((0, 64), (1, 4))),
        "v_res": centred(key_of[2], (N_SEQ * RES_DEV, HEADS * HD), 1.0, 6.0, ((0, 64), (1, 4))),
        "q_new": centred(key_of[3], (NEWROWS, HEADS * HD), 1.0, 6.0, ((0, 64), (1, 4))),
        "k_new": centred(key_of[4], (NEWROWS, HEADS * HD), HD ** -0.5, 0.5, ((0, 64), (1, 4))),
        "v_new": centred(key_of[5], (NEWROWS, HEADS * HD), 1.0, 6.0, ((0, 64), (1, 4))),
        "admit_dest": draw_admit_dest(jax.random.fold_in(key_of[10], 71), 0),
        "admit_slot": draw_admit_slot(jax.random.fold_in(key_of[10], 71), 0),
        "boundaries": draw_boundaries(jax.random.fold_in(key_of[10], 71), 0),
        "rate": draw_rate(jax.random.fold_in(key_of[10], 71), 0),
    }


def block_pass(carry_state, block, rate):
    q_blk, k_blk, v_blk, r_blk = block
    length = q_blk.shape[0]
    count = jnp.cumsum(r_blk)
    spots = jnp.arange(length).astype(jnp.float32)
    gap = spots[:, None] - spots[None, :]
    linked = (gap >= 0.0) & (count[:, None] == count[None, :])
    decay_mat = jnp.exp(-rate[:, None, None] * jnp.maximum(gap, 0.0)[None, :, :])
    scores = jnp.einsum('ihd,jhd->hij', q_blk, k_blk, preferred_element_type=jnp.float32)
    weights = jnp.where(linked[None, :, :], scores * decay_mat, 0.0).astype(jnp.bfloat16)
    local = jnp.einsum('hij,jhd->ihd', weights, v_blk, preferred_element_type=jnp.float32)
    alive = (count == 0).astype(jnp.float32)
    into = jnp.exp(-rate[None, :] * (spots[:, None] + 1.0)) * alive[:, None]
    carried = jnp.einsum('ihd,hde->ihe', q_blk.astype(jnp.float32) * into[:, :, None], carry_state, precision=lax.Precision.HIGHEST)
    keep = jnp.exp(-rate[None, :] * (length - 1.0 - spots)[:, None]) * (count == count[-1]).astype(jnp.float32)[:, None]
    fresh = jnp.einsum('jhd,jhe->hde', k_blk.astype(jnp.float32) * keep[:, :, None], v_blk.astype(jnp.float32), precision=lax.Precision.HIGHEST)
    whole = jnp.exp(-rate * length) * alive[-1]
    return (whole[:, None, None] * carry_state + fresh, local + carried)

def attend(q_all, k_all, v_all, reset, rate, start_state, block):
    total, heads, width = q_all.shape
    blocks = total // block
    pieces = (q_all.reshape(blocks, block, heads, width), k_all.reshape(blocks, block, heads, width), v_all.reshape(blocks, block, heads, width), reset.reshape(blocks, block))
    end_state, outputs = lax.scan(lambda carry, piece: block_pass(carry, piece, rate), start_state, pieces)
    return (end_state, outputs.reshape(total, heads, width))

def normalize(output):
    scale = 1.0 / jnp.sqrt(lax.optimization_barrier(jnp.mean(output * output, axis=-1, keepdims=True)) + 1e-06)
    return output * scale

def reference(q_res, k_res, v_res, q_new, k_new, v_new, admit_dest, admit_slot, boundaries, rate):
    index = admit_dest * NB + admit_slot

    def arrange(resident, fresh_rows):
        units = fresh_rows.reshape(UNITS, UNIT, HEADS * HD)
        placed = jnp.zeros_like(units).at[index].set(units).reshape(N_SEQ, ADM_DEV, HEADS * HD)
        whole = jnp.concatenate([resident.reshape(N_SEQ, RES_DEV, HEADS * HD), placed], axis=1)
        return whole.reshape(TOKENS, HEADS, HD)
    q_all = arrange(q_res, q_new)
    k_all = arrange(k_res, k_new)
    v_all = arrange(v_res, v_new)
    where_at = jnp.arange(TOKENS).astype(jnp.int32)
    reset = jnp.any(where_at[:, None] == boundaries[None, :], axis=1).astype(jnp.int32)
    start_state = jnp.zeros((HEADS, HD, HD), jnp.float32)
    end_state, output = attend(q_all, k_all, v_all, reset, rate, start_state, BLOCK)
    return normalize(output).reshape(TOKENS, HEADS * HD).astype(jnp.bfloat16)
```

```python
import functools

import jax
import jax.numpy as jnp
from jax import lax
from jax.experimental import pallas as pl
from jax.experimental.pallas import tpu as pltpu
from jax.sharding import PartitionSpec as P

MESH = pl.DeviceIdType.MESH
UNIT = 8
PAIR = 2 * UNIT
CHUNK = 256
HD = 128
F32 = jnp.float32
BF16 = jnp.bfloat16
UNFILLED = 4096


def dot(a, b):
    return jnp.dot(a, b, preferred_element_type=F32)


def dot_t(a, b):
    return lax.dot_general(a, b, (((1,), (1,)), ((), ())), preferred_element_type=F32)


def t_dot(a, b):
    return lax.dot_general(a, b, (((0,), (0,)), ((), ())), preferred_element_type=F32)


def two_terms(x):
    high = x.astype(BF16)
    low = (x - high.astype(F32)).astype(BF16)
    return jnp.concatenate([high, low], axis=1)


def fold(x):
    return x[:, :HD] + x[:, HD:]


def kernel(
    n, plane, q_res, k_res, v_res, q_new, k_new, v_new, send_row, labels, b_row, b_col, rate_ref, out,
    q_all, k_all, v_all, kv_stack, q_stack, pay_kv, pay_q, got_kv, got_q, got_labels, place,
    mask, alive, keep, o_local, s_local, end, in1, total, in2, out3, in3,
    load_sem, send_sem, recv_sem, send2, recv2,
):
    me = lax.axis_index("seq")
    z, p = me // plane, lax.rem(me, plane)
    depth = n // plane
    resident = q_res.shape[0]
    length = resident + CHUNK
    chunks = length // CHUNK
    last = chunks - 1
    slots = CHUNK
    columns = q_res.shape[1]
    half = columns // 2

    loads = [
        pltpu.make_async_copy(k_new, kv_stack.at[pl.ds(0, slots)], load_sem.at[0]),
        pltpu.make_async_copy(v_new, kv_stack.at[pl.ds(slots, slots)], load_sem.at[1]),
        pltpu.make_async_copy(q_new.at[:, pl.ds(0, half)], q_stack.at[pl.ds(0, slots)], load_sem.at[2]),
        pltpu.make_async_copy(q_new.at[:, pl.ds(half, half)], q_stack.at[pl.ds(slots, slots)], load_sem.at[3]),
        pltpu.make_async_copy(q_res, q_all.at[pl.ds(0, resident)], load_sem.at[4]),
        pltpu.make_async_copy(k_res, k_all.at[pl.ds(0, resident)], load_sem.at[5]),
        pltpu.make_async_copy(v_res, v_all.at[pl.ds(0, resident)], load_sem.at[6]),
    ]
    for load in loads:
        load.start()

    barrier = pltpu.get_barrier_semaphore()

    def greet(step, carry):
        pl.semaphore_signal(
            barrier, inc=1, device_id={"seq": lax.rem(me + step, n)}, device_id_type=MESH
        )
        return carry

    lax.fori_loop(1, n, greet, 0)

    for load in loads[:4]:
        load.wait()

    def pack(step, carry):
        base = pl.multiple_of(step * 256, 256)
        rows = base + lax.broadcasted_iota(jnp.int32, (256, 2 * slots), 0)
        pick = jnp.where(rows == send_row[...], 1.0, 0.0).astype(BF16)
        for c in range(columns // 256):
            pay_kv[pl.ds(base, 256), pl.ds(c * 256, 256)] = dot(
                pick, kv_stack[:, pl.ds(c * 256, 256)]
            ).astype(BF16)
        for c in range(half // 256):
            pay_q[pl.ds(base, 256), pl.ds(c * 256, 256)] = dot(
                pick, q_stack[:, pl.ds(c * 256, 256)]
            ).astype(BF16)
        return carry

    lax.fori_loop(0, n * PAIR // 256, pack, 0)
    got_kv[pl.ds(0, PAIR)] = pay_kv[pl.ds(0, PAIR)]
    got_q[pl.ds(0, PAIR)] = pay_q[pl.ds(0, PAIR)]
    got_labels[0] = labels[0]

    pl.semaphore_wait(barrier, n - 1)

    def label_copy(step):
        off = lax.rem(step * 37, n)
        return pltpu.make_async_remote_copy(
            src_ref=labels.at[off], dst_ref=got_labels.at[off],
            send_sem=send_sem.at[0], recv_sem=recv_sem.at[0],
            device_id={"seq": lax.rem(me + off, n)}, device_id_type=MESH,
        )

    def kv_copy(step):
        off = lax.rem(step * 37, n)
        rows = pl.ds(pl.multiple_of(off * PAIR, PAIR), PAIR)
        return pltpu.make_async_remote_copy(
            src_ref=pay_kv.at[rows], dst_ref=got_kv.at[rows],
            send_sem=send_sem.at[1], recv_sem=recv_sem.at[1],
            device_id={"seq": lax.rem(me + off, n)}, device_id_type=MESH,
        )

    def q_copy(step):
        off = lax.rem(step * 37, n)
        rows = pl.ds(pl.multiple_of(off * PAIR, PAIR), PAIR)
        return pltpu.make_async_remote_copy(
            src_ref=pay_q.at[rows], dst_ref=got_q.at[rows],
            send_sem=send_sem.at[2], recv_sem=recv_sem.at[2],
            device_id={"seq": lax.rem(me + off, n)}, device_id_type=MESH,
        )

    def start_range(copy, low, high):
        def one(step, carry):
            copy(step).start()
            return carry

        lax.fori_loop(low, high, one, 0)

    start_range(label_copy, 1, n)
    start_range(kv_copy, 1, n)

    rest = pl.ds(PAIR, (n - 1) * PAIR)

    def all_labels():
        return pltpu.make_async_remote_copy(
            src_ref=labels.at[pl.ds(1, n - 1)], dst_ref=got_labels.at[pl.ds(1, n - 1)],
            send_sem=send_sem.at[0], recv_sem=recv_sem.at[0],
            device_id={"seq": lax.rem(me + 1, n)}, device_id_type=MESH,
        )

    def all_kv():
        return pltpu.make_async_remote_copy(
            src_ref=pay_kv.at[rest], dst_ref=got_kv.at[rest],
            send_sem=send_sem.at[1], recv_sem=recv_sem.at[1],
            device_id={"seq": lax.rem(me + 1, n)}, device_id_type=MESH,
        )

    def all_q():
        return pltpu.make_async_remote_copy(
            src_ref=pay_q.at[rest], dst_ref=got_q.at[rest],
            send_sem=send_sem.at[2], recv_sem=recv_sem.at[2],
            device_id={"seq": lax.rem(me + 1, n)}, device_id_type=MESH,
        )

    def clear(low, high):
        inside = (b_row[...] >= low) & (b_row[...] < high)
        found = jnp.sum(jnp.where(inside, 1.0, 0.0), axis=1, keepdims=True)
        return jnp.where(found == 0.0, 1.0, 0.0)

    def starts_upto(position):
        return jnp.sum(jnp.where(b_row[...] <= position, 1.0, 0.0), axis=1, keepdims=True)

    for c in range(chunks):
        base = me * length + c * CHUNK
        spot = base + lax.broadcasted_iota(jnp.int32, (CHUNK, HD), 0)
        count_col = jnp.sum(jnp.where(b_row[...] <= spot, 1.0, 0.0), axis=1, keepdims=True)
        spot_row = base + lax.broadcasted_iota(jnp.int32, (b_col.shape[0], CHUNK), 1)
        b_wide = jnp.concatenate([b_col[...]] * (CHUNK // HD), axis=1)
        count_row = jnp.sum(jnp.where(b_wide <= spot_row, 1.0, 0.0), axis=0, keepdims=True)
        gap = lax.broadcasted_iota(jnp.int32, (CHUNK, CHUNK), 0) - lax.broadcasted_iota(
            jnp.int32, (CHUNK, CHUNK), 1
        )
        mask[c] = jnp.where((gap >= 0) & (count_col == count_row), 1.0, 0.0)
        wide = jnp.broadcast_to(count_col, (CHUNK, HD))
        alive[c] = jnp.where(wide == starts_upto(base - 1), 1.0, 0.0)
        keep[c] = jnp.where(wide == starts_upto(base + CHUNK - 1), 1.0, 0.0)

    def decay_of(x):
        return jnp.exp(jnp.full((1, HD), x, F32))

    def decay_matrix(rate):
        gap = lax.broadcasted_iota(jnp.int32, (CHUNK, CHUNK), 0) - lax.broadcasted_iota(
            jnp.int32, (CHUNK, CHUNK), 1
        )
        return jnp.exp(-rate * jnp.maximum(gap, 0).astype(F32))

    def step_state(c, h, rate, state):
        rows = pl.ds(c * CHUNK, CHUNK)
        cols = pl.ds(pl.multiple_of(h * HD, HD), HD)
        spot = lax.broadcasted_iota(jnp.int32, (CHUNK, HD), 0).astype(F32)
        weight = jnp.exp(-rate * (CHUNK - 1.0 - spot)) * keep[c]
        fresh = fold(t_dot(k_all[rows, cols], two_terms(v_all[rows, cols].astype(F32) * weight)))
        whole = decay_of(-rate * CHUNK) * alive[c, CHUNK - 1 : CHUNK, :]
        return whole * state + fresh

    def local_part(c, h, decay):
        rows = pl.ds(c * CHUNK, CHUNK)
        cols = pl.ds(pl.multiple_of(h * HD, HD), HD)
        scores = dot_t(q_all[rows, cols], k_all[rows, cols])
        weights = (scores * (decay * mask[c])).astype(BF16)
        return dot(weights, v_all[rows, cols])

    for load in loads[4:]:
        load.wait()

    def resident_head(h, carry):
        rate = rate_ref[h]
        decay = decay_matrix(rate)
        cols = pl.ds(pl.multiple_of(h * HD, HD), HD)
        state = jnp.zeros((HD, HD), F32)
        for c in range(last):
            s_local[c, h] = state
            o_local[pl.ds(c * CHUNK, CHUNK), cols] = local_part(c, h, decay)
            state = step_state(c, h, rate, state)
        s_local[last, h] = state
        return carry

    lax.fori_loop(0, plane, resident_head, 0)

    all_labels().wait_recv()
    lane = lax.broadcasted_iota(jnp.int32, (1, HD), 1)
    group = lax.shift_right_logical(lane, 4)
    pieces = []
    for c in range(n * PAIR // HD):
        piece = jnp.zeros((1, HD), jnp.int32)
        for o in range(HD // PAIR):
            piece = piece + jnp.where(group == o, got_labels[c * (HD // PAIR) + o], 0)
        inner = (lane & (UNIT - 1)) + lax.shift_right_logical(lane & UNIT, 3) * slots
        pieces.append(piece + inner)
    for c, piece in enumerate(pieces):
        rows = lax.broadcasted_iota(jnp.int32, (2 * slots, HD), 0)
        place[:, pl.ds(c * HD, HD)] = jnp.where(rows == piece, 1.0, 0.0).astype(BF16)

    start_range(q_copy, 1, n // 4)

    all_kv().wait_recv()

    def arrange_kv(step, carry):
        cols = pl.ds(pl.multiple_of(step * 256, 256), 256)
        whole = dot(place[...], got_kv[:, cols]).astype(BF16)
        k_all[pl.ds(resident, slots), cols] = whole[:slots]
        v_all[pl.ds(resident, slots), cols] = whole[slots:]
        return carry

    lax.fori_loop(0, columns // 256, arrange_kv, 0)

    def end_head(h, carry):
        end[h] = step_state(last, h, rate_ref[h], s_local[last, h])
        return carry

    lax.fori_loop(0, plane, end_head, 0)

    def first_copy(step):
        mate = lax.rem(p + step, plane)
        return pltpu.make_async_remote_copy(
            src_ref=end.at[mate], dst_ref=in1.at[step],
            send_sem=send_sem.at[3], recv_sem=recv_sem.at[3],
            device_id={"seq": z * plane + mate}, device_id_type=MESH,
        )

    def third_copy(step):
        mate = lax.rem(p + step, plane)
        return pltpu.make_async_remote_copy(
            src_ref=out3.at[mate], dst_ref=in3.at[step],
            send_sem=send_sem.at[4], recv_sem=recv_sem.at[4],
            device_id={"seq": z * plane + mate}, device_id_type=MESH,
        )

    def second_copy(step):
        return pltpu.make_async_remote_copy(
            src_ref=total, dst_ref=in2.at[step],
            send_sem=send2.at[step], recv_sem=recv2.at[step],
            device_id={"seq": lax.rem(me + step * plane, n)}, device_id_type=MESH,
        )

    def all_first():
        return pltpu.make_async_remote_copy(
            src_ref=end.at[pl.ds(1, plane - 1)], dst_ref=in1.at[pl.ds(1, plane - 1)],
            send_sem=send_sem.at[3], recv_sem=recv_sem.at[3],
            device_id={"seq": z * plane + lax.rem(p + 1, plane)}, device_id_type=MESH,
        )

    def all_third():
        return pltpu.make_async_remote_copy(
            src_ref=out3.at[pl.ds(1, plane - 1)], dst_ref=in3.at[pl.ds(1, plane - 1)],
            send_sem=send_sem.at[4], recv_sem=recv_sem.at[4],
            device_id={"seq": z * plane + lax.rem(p + 1, plane)}, device_id_type=MESH,
        )

    start_range(first_copy, 1, plane)
    start_range(q_copy, n // 4, n // 2)
    in1[0] = end[p]
    rate_p = rate_ref[p]
    all_first().wait_recv()

    state = jnp.zeros((HD, HD), F32)
    for m in range(plane):
        shard = z * plane + m
        out3[m] = state
        pass_on = decay_of(-rate_p * length) * clear(shard * length, (shard + 1) * length)
        state = pass_on * state + in1[lax.rem(p - m + plane, plane)]
    total[...] = state

    for step in range(1, depth):
        @pl.when(z + step < depth)
        def _(step=step):
            second_copy(step).start()

    start_range(q_copy, n // 2, (3 * n) // 4)

    in2[0] = jnp.zeros((HD, HD), F32)
    span = plane * length
    for step in range(1, depth):
        @pl.when(z - step >= 0)
        def _(step=step):
            second_copy(step).wait_recv()
            factor = decay_of(-rate_p * float(span * (step - 1))) * clear(
                (z - step + 1) * span, z * span
            )
            in2[0] = in2[0] + factor * in2[step]

    before = in2[0]
    for m in range(plane):
        factor = decay_of(-rate_p * float(length * m)) * clear(z * span, z * span + m * length)
        out3[m] = out3[m] + factor * before

    start_range(third_copy, 1, plane)
    start_range(q_copy, (3 * n) // 4, n)
    in3[0] = out3[p]
    all_third().wait_recv()

    def finish(c, h, rate, local):
        rows = pl.ds(c * CHUNK, CHUNK)
        cols = pl.ds(pl.multiple_of(h * HD, HD), HD)
        reach = decay_of(-rate * float(c * CHUNK))
        for m in range(c):
            reach = reach * alive[m, CHUNK - 1 : CHUNK, :]
        carry = s_local[c, h] + reach * in3[lax.rem(p - h + plane, plane)]
        spot = lax.broadcasted_iota(jnp.int32, (CHUNK, HD), 0).astype(F32)
        into = jnp.exp(-rate * (spot + 1.0)) * alive[c]
        whole = local + into * fold(dot(q_all[rows, cols], two_terms(carry)))
        mean = jnp.sum(whole * whole, axis=1, keepdims=True) * (1.0 / HD)
        out[rows, cols] = (whole * lax.rsqrt(mean + 1e-06)).astype(BF16)

    def finish_resident(h, carry):
        rate = rate_ref[h]
        cols = pl.ds(pl.multiple_of(h * HD, HD), HD)
        for c in range(last):
            finish(c, h, rate, o_local[pl.ds(c * CHUNK, CHUNK), cols])
        return carry

    lax.fori_loop(0, plane, finish_resident, 0)

    all_q().wait_recv()

    def arrange_q(step, carry):
        cols = pl.ds(pl.multiple_of(step * 256, 256), 256)
        later = pl.ds(pl.multiple_of(half + step * 256, 256), 256)
        whole = dot(place[...], got_q[:, cols]).astype(BF16)
        q_all[pl.ds(resident, slots), cols] = whole[:slots]
        q_all[pl.ds(resident, slots), later] = whole[slots:]
        return carry

    lax.fori_loop(0, half // 256, arrange_q, 0)

    def finish_admitted(h, carry):
        rate = rate_ref[h]
        finish(last, h, rate, local_part(last, h, decay_matrix(rate)))
        return carry

    lax.fori_loop(0, plane, finish_admitted, 0)

    all_labels().wait_send()
    all_kv().wait_send()
    all_q().wait_send()
    all_first().wait_send()
    all_third().wait_send()
    for step in range(1, depth):
        @pl.when(z + step < depth)
        def _(step=step):
            second_copy(step).wait_send()


def body(q_res, k_res, v_res, q_new, k_new, v_new, admit_dest, admit_slot, boundaries, rate):
    n = lax.axis_size("seq")
    me = lax.axis_index("seq")
    heads = rate.shape[0]
    columns = q_res.shape[1]
    resident, fresh = q_res.shape[0], q_new.shape[0]
    length = resident + fresh
    away = jnp.remainder(admit_dest - me, n)
    inner = jnp.arange(UNIT, dtype=jnp.int32)
    row = (away[:, None] * PAIR + inner[None, :]).reshape(1, fresh)
    send_row = jnp.concatenate([row, row + UNIT], axis=1)
    match = jnp.arange(n, dtype=jnp.int32)[:, None] == away[None, :]
    label = jnp.sum(jnp.where(match, admit_slot[None, :] * UNIT + UNFILLED, 0), axis=1) - UNFILLED
    labels = jnp.broadcast_to(label[:, None, None], (n, 1, HD)).astype(jnp.int32)
    count = boundaries.shape[0]
    b_row = jnp.concatenate([boundaries, jnp.full((HD - count,), 2**30, jnp.int32)]).reshape(1, HD)
    b_col = jnp.broadcast_to(boundaries[:, None], (count, HD))

    any_spec = pl.BlockSpec(memory_space=pl.ANY)
    vmem = pl.BlockSpec(memory_space=pltpu.VMEM)
    smem = pl.BlockSpec(memory_space=pltpu.SMEM)
    chunks = length // CHUNK
    return pl.pallas_call(
        functools.partial(kernel, n, heads),
        out_shape=jax.ShapeDtypeStruct((length, columns), BF16),
        in_specs=[any_spec] * 6 + [vmem] * 4 + [smem],
        out_specs=vmem,
        scratch_shapes=[
            pltpu.VMEM((length, columns), BF16),
            pltpu.VMEM((length, columns), BF16),
            pltpu.VMEM((length, columns), BF16),
            pltpu.VMEM((2 * fresh, columns), BF16),
            pltpu.VMEM((2 * fresh, columns // 2), BF16),
            pltpu.VMEM((n * PAIR, columns), BF16),
            pltpu.VMEM((n * PAIR, columns // 2), BF16),
            pltpu.VMEM((n * PAIR, columns), BF16),
            pltpu.VMEM((n * PAIR, columns // 2), BF16),
            pltpu.VMEM((n, 1, HD), jnp.int32),
            pltpu.VMEM((2 * fresh, n * PAIR), BF16),
            pltpu.VMEM((chunks, CHUNK, CHUNK), F32),
            pltpu.VMEM((chunks, CHUNK, HD), F32),
            pltpu.VMEM((chunks, CHUNK, HD), F32),
            pltpu.VMEM((resident, columns), F32),
            pltpu.VMEM((chunks, heads, HD, HD), F32),
            pltpu.VMEM((heads, HD, HD), F32),
            pltpu.VMEM((heads, HD, HD), F32),
            pltpu.VMEM((HD, HD), F32),
            pltpu.VMEM((n // heads, HD, HD), F32),
            pltpu.VMEM((heads, HD, HD), F32),
            pltpu.VMEM((heads, HD, HD), F32),
            pltpu.SemaphoreType.DMA((7,)),
            pltpu.SemaphoreType.DMA((5,)),
            pltpu.SemaphoreType.DMA((5,)),
            pltpu.SemaphoreType.DMA((n // heads,)),
            pltpu.SemaphoreType.DMA((n // heads,)),
        ],
        compiler_params=pltpu.CompilerParams(
            collective_id=0, has_side_effects=True, vmem_limit_bytes=48 * 1024 * 1024
        ),
    )(q_res, k_res, v_res, q_new, k_new, v_new, send_row, labels, b_row, b_col, rate)


def solution(mesh):
    in_specs = (
        P("seq", "head"),
        P("seq", "head"),
        P("seq", "head"),
        P("seq", "head"),
        P("seq", "head"),
        P("seq", "head"),
        P("seq"),
        P("seq"),
        P(),
        P("head"),
    )
    out_specs = P("seq", "head")
    return jax.shard_map(body, mesh=mesh, in_specs=in_specs, out_specs=out_specs, check_vma=False)
```

```python
import functools

import jax
import jax.numpy as jnp
from jax import lax
from jax.experimental import pallas as pl
from jax.experimental.pallas import tpu as pltpu
from jax.sharding import PartitionSpec as P

MESH = pl.DeviceIdType.MESH
UNIT = 8
PAIR = 2 * UNIT
CHUNK = 256
HD = 128
F32 = jnp.float32
BF16 = jnp.bfloat16
UNFILLED = 4096
STRIDE = 37


def dot(a, b):
    return jnp.dot(a, b, preferred_element_type=F32)


def dot_t(a, b):
    return lax.dot_general(a, b, (((1,), (1,)), ((), ())), preferred_element_type=F32)


def t_dot(a, b):
    return lax.dot_general(a, b, (((0,), (0,)), ((), ())), preferred_element_type=F32)


def two_terms(x):
    high = x.astype(BF16)
    low = (x - high.astype(F32)).astype(BF16)
    return jnp.concatenate([high, low], axis=1)


def fold(x):
    return x[:, :HD] + x[:, HD:]


def kernel(
    n, plane, q_res, k_res, v_res, q_new, k_new, v_new, send_row, labels, b_row, b_col, rate_ref, out,
    q_all, k_all, v_all, kv_stack, q_stack, pay_kv, pay_q, got_kv, got_q, got_labels, place,
    mask, alive, keep, o_local, s_local, end, in1, total, in2, before, out3, in3, done,
    load_sem, send_sem, recv_sem, send2, recv2, out_sem,
):
    me = lax.axis_index("seq")
    z, p = me // plane, lax.rem(me, plane)
    depth = n // plane
    resident = q_res.shape[0]
    length = resident + CHUNK
    chunks = length // CHUNK
    last = chunks - 1
    slots = CHUNK
    columns = q_res.shape[1]
    half = columns // 2

    loads = [
        pltpu.make_async_copy(k_new, kv_stack.at[pl.ds(0, slots)], load_sem.at[0]),
        pltpu.make_async_copy(v_new, kv_stack.at[pl.ds(slots, slots)], load_sem.at[1]),
        pltpu.make_async_copy(q_new.at[:, pl.ds(0, half)], q_stack.at[pl.ds(0, slots)], load_sem.at[2]),
        pltpu.make_async_copy(q_new.at[:, pl.ds(half, half)], q_stack.at[pl.ds(slots, slots)], load_sem.at[3]),
        pltpu.make_async_copy(q_res, q_all.at[pl.ds(0, resident)], load_sem.at[4]),
        pltpu.make_async_copy(k_res, k_all.at[pl.ds(0, resident)], load_sem.at[5]),
        pltpu.make_async_copy(v_res, v_all.at[pl.ds(0, resident)], load_sem.at[6]),
    ]
    for load in loads:
        load.start()

    barrier = pltpu.get_barrier_semaphore()

    def greet(step, carry):
        pl.semaphore_signal(
            barrier, inc=1, device_id={"seq": lax.rem(me + step, n)}, device_id_type=MESH
        )
        return carry

    lax.fori_loop(1, n, greet, 0)

    def ahead(step):
        return lax.rem(me + step * STRIDE, n)

    def label_copy(step):
        return pltpu.make_async_remote_copy(
            src_ref=labels.at[step], dst_ref=got_labels.at[step],
            send_sem=send_sem.at[0], recv_sem=recv_sem.at[0],
            device_id={"seq": ahead(step)}, device_id_type=MESH,
        )

    def kv_copy(step):
        rows = pl.ds(pl.multiple_of(step * PAIR, PAIR), PAIR)
        return pltpu.make_async_remote_copy(
            src_ref=pay_kv.at[rows], dst_ref=got_kv.at[rows],
            send_sem=send_sem.at[1], recv_sem=recv_sem.at[1],
            device_id={"seq": ahead(step)}, device_id_type=MESH,
        )

    def q_copy(step):
        rows = pl.ds(pl.multiple_of(step * PAIR, PAIR), PAIR)
        return pltpu.make_async_remote_copy(
            src_ref=pay_q.at[rows], dst_ref=got_q.at[rows],
            send_sem=send_sem.at[2], recv_sem=recv_sem.at[2],
            device_id={"seq": ahead(step)}, device_id_type=MESH,
        )

    def start_range(copy, low, high):
        def one(step, carry):
            copy(step).start()
            return carry

        lax.fori_loop(low, high, one, 0)

    def pick(base):
        rows = base + lax.broadcasted_iota(jnp.int32, (256, 2 * slots), 0)
        return jnp.where(rows == send_row[...], 1.0, 0.0).astype(BF16)

    def pack_kv(base):
        chosen = pick(base)
        for c in range(columns // 256):
            pay_kv[pl.ds(base, 256), pl.ds(c * 256, 256)] = dot(
                chosen, kv_stack[:, pl.ds(c * 256, 256)]
            ).astype(BF16)

    for load in loads[:2]:
        load.wait()
    pack_kv(0)
    pl.semaphore_wait(barrier, n - 1)
    group = 256 // PAIR
    start_range(kv_copy, 1, group)
    start_range(label_copy, 1, n)
    for part in range(1, n // group):
        pack_kv(part * 256)
        start_range(kv_copy, part * group, (part + 1) * group)

    for load in loads[2:4]:
        load.wait()

    def pack_q(step, carry):
        base = pl.multiple_of(step * 256, 256)
        chosen = pick(base)
        for c in range(half // 256):
            pay_q[pl.ds(base, 256), pl.ds(c * 256, 256)] = dot(
                chosen, q_stack[:, pl.ds(c * 256, 256)]
            ).astype(BF16)
        return carry

    lax.fori_loop(0, n // group, pack_q, 0)
    got_kv[pl.ds(0, PAIR)] = pay_kv[pl.ds(0, PAIR)]
    got_q[pl.ds(0, PAIR)] = pay_q[pl.ds(0, PAIR)]
    got_labels[0] = labels[0]

    rest = pl.ds(PAIR, (n - 1) * PAIR)

    def all_labels():
        return pltpu.make_async_remote_copy(
            src_ref=labels.at[pl.ds(1, n - 1)], dst_ref=got_labels.at[pl.ds(1, n - 1)],
            send_sem=send_sem.at[0], recv_sem=recv_sem.at[0],
            device_id={"seq": lax.rem(me + 1, n)}, device_id_type=MESH,
        )

    def all_kv():
        return pltpu.make_async_remote_copy(
            src_ref=pay_kv.at[rest], dst_ref=got_kv.at[rest],
            send_sem=send_sem.at[1], recv_sem=recv_sem.at[1],
            device_id={"seq": lax.rem(me + 1, n)}, device_id_type=MESH,
        )

    def all_q():
        return pltpu.make_async_remote_copy(
            src_ref=pay_q.at[rest], dst_ref=got_q.at[rest],
            send_sem=send_sem.at[2], recv_sem=recv_sem.at[2],
            device_id={"seq": lax.rem(me + 1, n)}, device_id_type=MESH,
        )

    def clear(low, high):
        inside = (b_row[...] >= low) & (b_row[...] < high)
        found = jnp.sum(jnp.where(inside, 1.0, 0.0), axis=1, keepdims=True)
        return jnp.where(found == 0.0, 1.0, 0.0)

    def starts_upto(position):
        return jnp.sum(jnp.where(b_row[...] <= position, 1.0, 0.0), axis=1, keepdims=True)

    for c in range(chunks):
        base = me * length + c * CHUNK
        spot = base + lax.broadcasted_iota(jnp.int32, (CHUNK, HD), 0)
        count_col = jnp.sum(jnp.where(b_row[...] <= spot, 1.0, 0.0), axis=1, keepdims=True)
        spot_row = base + lax.broadcasted_iota(jnp.int32, (b_col.shape[0], CHUNK), 1)
        b_wide = jnp.concatenate([b_col[...]] * (CHUNK // HD), axis=1)
        count_row = jnp.sum(jnp.where(b_wide <= spot_row, 1.0, 0.0), axis=0, keepdims=True)
        gap = lax.broadcasted_iota(jnp.int32, (CHUNK, CHUNK), 0) - lax.broadcasted_iota(
            jnp.int32, (CHUNK, CHUNK), 1
        )
        mask[c] = jnp.where((gap >= 0) & (count_col == count_row), 1.0, 0.0)
        wide = jnp.broadcast_to(count_col, (CHUNK, HD))
        alive[c] = jnp.where(wide == starts_upto(base - 1), 1.0, 0.0)
        keep[c] = jnp.where(wide == starts_upto(base + CHUNK - 1), 1.0, 0.0)

    def decay_of(x):
        return jnp.exp(jnp.full((1, HD), x, F32))

    def decay_matrix(rate):
        gap = lax.broadcasted_iota(jnp.int32, (CHUNK, CHUNK), 0) - lax.broadcasted_iota(
            jnp.int32, (CHUNK, CHUNK), 1
        )
        return jnp.exp(-rate * jnp.maximum(gap, 0).astype(F32))

    def step_state(c, h, rate, state):
        rows = pl.ds(c * CHUNK, CHUNK)
        cols = pl.ds(pl.multiple_of(h * HD, HD), HD)
        spot = lax.broadcasted_iota(jnp.int32, (CHUNK, HD), 0).astype(F32)
        weight = jnp.exp(-rate * (CHUNK - 1.0 - spot)) * keep[c]
        fresh = fold(t_dot(k_all[rows, cols], two_terms(v_all[rows, cols].astype(F32) * weight)))
        whole = decay_of(-rate * CHUNK) * alive[c, CHUNK - 1 : CHUNK, :]
        return whole * state + fresh

    def local_part(c, h, decay):
        rows = pl.ds(c * CHUNK, CHUNK)
        cols = pl.ds(pl.multiple_of(h * HD, HD), HD)
        scores = dot_t(q_all[rows, cols], k_all[rows, cols])
        weights = (scores * (decay * mask[c])).astype(BF16)
        return dot(weights, v_all[rows, cols])

    for load in loads[4:]:
        load.wait()

    def resident_head(h, carry):
        rate = rate_ref[h]
        decay = decay_matrix(rate)
        cols = pl.ds(pl.multiple_of(h * HD, HD), HD)
        state = jnp.zeros((HD, HD), F32)
        for c in range(last):
            s_local[c, h] = state
            o_local[pl.ds(c * CHUNK, CHUNK), cols] = local_part(c, h, decay)
            state = step_state(c, h, rate, state)
        s_local[last, h] = state
        return carry

    lax.fori_loop(0, plane, resident_head, 0)

    all_labels().wait_recv()
    lane = lax.broadcasted_iota(jnp.int32, (1, HD), 1)
    owner = lax.shift_right_logical(lane, 4)
    pieces = []
    for c in range(n * PAIR // HD):
        piece = jnp.zeros((1, HD), jnp.int32)
        for o in range(HD // PAIR):
            piece = piece + jnp.where(owner == o, got_labels[c * (HD // PAIR) + o], 0)
        inner = (lane & (UNIT - 1)) + lax.shift_right_logical(lane & UNIT, 3) * slots
        pieces.append(piece + inner)
    for c, piece in enumerate(pieces):
        rows = lax.broadcasted_iota(jnp.int32, (2 * slots, HD), 0)
        place[:, pl.ds(c * HD, HD)] = jnp.where(rows == piece, 1.0, 0.0).astype(BF16)

    start_range(q_copy, 1, n // 4)

    all_kv().wait_recv()

    def arrange_kv(step, carry):
        cols = pl.ds(pl.multiple_of(step * 256, 256), 256)
        whole = dot(place[...], got_kv[:, cols]).astype(BF16)
        k_all[pl.ds(resident, slots), cols] = whole[:slots]
        v_all[pl.ds(resident, slots), cols] = whole[slots:]
        return carry

    lax.fori_loop(0, columns // 256, arrange_kv, 0)

    def first_copy(step):
        mate = lax.rem(p + step, plane)
        return pltpu.make_async_remote_copy(
            src_ref=end.at[mate], dst_ref=in1.at[step],
            send_sem=send_sem.at[3], recv_sem=recv_sem.at[3],
            device_id={"seq": z * plane + mate}, device_id_type=MESH,
        )

    def third_copy(step):
        mate = lax.rem(p + step, plane)
        return pltpu.make_async_remote_copy(
            src_ref=out3.at[mate], dst_ref=in3.at[step],
            send_sem=send_sem.at[4], recv_sem=recv_sem.at[4],
            device_id={"seq": z * plane + mate}, device_id_type=MESH,
        )

    def second_copy(step):
        return pltpu.make_async_remote_copy(
            src_ref=total, dst_ref=in2.at[step],
            send_sem=send2.at[step], recv_sem=recv2.at[step],
            device_id={"seq": lax.rem(me + step * plane, n)}, device_id_type=MESH,
        )

    def all_first():
        return pltpu.make_async_remote_copy(
            src_ref=end.at[pl.ds(1, plane - 1)], dst_ref=in1.at[pl.ds(1, plane - 1)],
            send_sem=send_sem.at[3], recv_sem=recv_sem.at[3],
            device_id={"seq": z * plane + lax.rem(p + 1, plane)}, device_id_type=MESH,
        )

    def all_third():
        return pltpu.make_async_remote_copy(
            src_ref=out3.at[pl.ds(1, plane - 1)], dst_ref=in3.at[pl.ds(1, plane - 1)],
            send_sem=send_sem.at[4], recv_sem=recv_sem.at[4],
            device_id={"seq": z * plane + lax.rem(p + 1, plane)}, device_id_type=MESH,
        )

    def end_head(h):
        end[h] = step_state(last, h, rate_ref[h], s_local[last, h])

    def end_mate(step, carry):
        end_head(lax.rem(p + step, plane))
        first_copy(step).start()
        return carry

    lax.fori_loop(1, plane, end_mate, 0)
    start_range(q_copy, n // 4, n // 2)
    end_head(p)
    in1[0] = end[p]
    rate_p = rate_ref[p]
    all_first().wait_recv()

    state = jnp.zeros((HD, HD), F32)
    for m in range(plane):
        shard = z * plane + m
        out3[m] = state
        pass_on = decay_of(-rate_p * length) * clear(shard * length, (shard + 1) * length)
        state = pass_on * state + in1[lax.rem(p - m + plane, plane)]
    total[...] = state.astype(BF16)

    for step in range(1, depth):
        @pl.when(z + step < depth)
        def _(step=step):
            second_copy(step).start()

    start_range(q_copy, n // 2, (3 * n) // 4)

    before[...] = jnp.zeros((HD, HD), F32)
    span = plane * length
    for step in range(1, depth):
        @pl.when(z - step >= 0)
        def _(step=step):
            second_copy(step).wait_recv()
            factor = decay_of(-rate_p * float(span * (step - 1))) * clear(
                (z - step + 1) * span, z * span
            )
            before[...] = before[...] + factor * in2[step].astype(F32)

    earlier = before[...]
    for m in range(plane):
        factor = decay_of(-rate_p * float(length * m)) * clear(z * span, z * span + m * length)
        out3[m] = out3[m] + factor * earlier

    start_range(third_copy, 1, plane)
    start_range(q_copy, (3 * n) // 4, n)
    in3[0] = out3[p]
    all_third().wait_recv()

    def finish(c, h, rate, local):
        rows = pl.ds(c * CHUNK, CHUNK)
        cols = pl.ds(pl.multiple_of(h * HD, HD), HD)
        reach = decay_of(-rate * float(c * CHUNK))
        for m in range(c):
            reach = reach * alive[m, CHUNK - 1 : CHUNK, :]
        carry = s_local[c, h] + reach * in3[lax.rem(p - h + plane, plane)]
        spot = lax.broadcasted_iota(jnp.int32, (CHUNK, HD), 0).astype(F32)
        into = jnp.exp(-rate * (spot + 1.0)) * alive[c]
        whole = local + into * fold(dot(q_all[rows, cols], two_terms(carry)))
        mean = jnp.sum(whole * whole, axis=1, keepdims=True) * (1.0 / HD)
        done[rows, cols] = (whole * lax.rsqrt(mean + 1e-06)).astype(BF16)

    def finish_resident(h, carry):
        rate = rate_ref[h]
        cols = pl.ds(pl.multiple_of(h * HD, HD), HD)
        for c in range(last):
            finish(c, h, rate, o_local[pl.ds(c * CHUNK, CHUNK), cols])
        return carry

    lax.fori_loop(0, plane, finish_resident, 0, unroll=2)
    rows_in = pl.ds(0, resident)
    rows_new = pl.ds(resident, slots)
    store = pltpu.make_async_copy(done.at[rows_in], out.at[rows_in], out_sem.at[0])
    store.start()

    all_q().wait_recv()

    def arrange_q(step, carry):
        cols = pl.ds(pl.multiple_of(step * 256, 256), 256)
        later = pl.ds(pl.multiple_of(half + step * 256, 256), 256)
        whole = dot(place[...], got_q[:, cols]).astype(BF16)
        q_all[pl.ds(resident, slots), cols] = whole[:slots]
        q_all[pl.ds(resident, slots), later] = whole[slots:]
        return carry

    lax.fori_loop(0, half // 256, arrange_q, 0)

    def finish_admitted(h, carry):
        rate = rate_ref[h]
        finish(last, h, rate, local_part(last, h, decay_matrix(rate)))
        return carry

    lax.fori_loop(0, plane, finish_admitted, 0, unroll=2)
    store_new = pltpu.make_async_copy(done.at[rows_new], out.at[rows_new], out_sem.at[1])
    store_new.start()

    all_labels().wait_send()
    all_kv().wait_send()
    all_q().wait_send()
    all_first().wait_send()
    all_third().wait_send()
    for step in range(1, depth):
        @pl.when(z + step < depth)
        def _(step=step):
            second_copy(step).wait_send()
    store.wait()
    store_new.wait()


def hand_over(parts, src, dst, sem):
    size = src.shape[0] // parts
    copies = [
        pltpu.make_async_copy(src.at[pl.ds(i * size, size)], dst.at[pl.ds(i * size, size)], sem.at[i])
        for i in range(parts)
    ]
    for copy in copies:
        copy.start()
    for copy in copies:
        copy.wait()


def body(q_res, k_res, v_res, q_new, k_new, v_new, admit_dest, admit_slot, boundaries, rate):
    n = lax.axis_size("seq")
    me = lax.axis_index("seq")
    heads = rate.shape[0]
    columns = q_res.shape[1]
    resident, fresh = q_res.shape[0], q_new.shape[0]
    length = resident + fresh
    away = jnp.remainder(admit_dest - me, n)
    inner = jnp.arange(UNIT, dtype=jnp.int32)
    slot = jnp.remainder(away * pow(STRIDE, -1, n), n)
    row = (slot[:, None] * PAIR + inner[None, :]).reshape(1, fresh)
    send_row = jnp.concatenate([row, row + UNIT], axis=1)
    match = jnp.arange(n, dtype=jnp.int32)[:, None] == slot[None, :]
    label = jnp.sum(jnp.where(match, admit_slot[None, :] * UNIT + UNFILLED, 0), axis=1) - UNFILLED
    labels = jnp.broadcast_to(label[:, None, None], (n, 1, HD)).astype(jnp.int32)
    count = boundaries.shape[0]
    b_row = jnp.concatenate([boundaries, jnp.full((HD - count,), 2**30, jnp.int32)]).reshape(1, HD)
    b_col = jnp.broadcast_to(boundaries[:, None], (count, HD))

    any_spec = pl.BlockSpec(memory_space=pl.ANY)
    vmem = pl.BlockSpec(memory_space=pltpu.VMEM)
    smem = pl.BlockSpec(memory_space=pltpu.SMEM)
    chunks = length // CHUNK
    result = pl.pallas_call(
        functools.partial(kernel, n, heads),
        out_shape=jax.ShapeDtypeStruct((length, columns), BF16),
        in_specs=[any_spec] * 6 + [vmem] * 4 + [smem],
        out_specs=any_spec,
        scratch_shapes=[
            pltpu.VMEM((length, columns), BF16),
            pltpu.VMEM((length, columns), BF16),
            pltpu.VMEM((length, columns), BF16),
            pltpu.VMEM((2 * fresh, columns), BF16),
            pltpu.VMEM((2 * fresh, columns // 2), BF16),
            pltpu.VMEM((n * PAIR, columns), BF16),
            pltpu.VMEM((n * PAIR, columns // 2), BF16),
            pltpu.VMEM((n * PAIR, columns), BF16),
            pltpu.VMEM((n * PAIR, columns // 2), BF16),
            pltpu.VMEM((n, 1, HD), jnp.int32),
            pltpu.VMEM((2 * fresh, n * PAIR), BF16),
            pltpu.VMEM((chunks, CHUNK, CHUNK), F32),
            pltpu.VMEM((chunks, CHUNK, HD), F32),
            pltpu.VMEM((chunks, CHUNK, HD), F32),
            pltpu.VMEM((resident, columns), F32),
            pltpu.VMEM((chunks, heads, HD, HD), F32),
            pltpu.VMEM((heads, HD, HD), F32),
            pltpu.VMEM((heads, HD, HD), F32),
            pltpu.VMEM((HD, HD), BF16),
            pltpu.VMEM((n // heads, HD, HD), BF16),
            pltpu.VMEM((HD, HD), F32),
            pltpu.VMEM((heads, HD, HD), F32),
            pltpu.VMEM((heads, HD, HD), F32),
            pltpu.VMEM((length, columns), BF16),
            pltpu.SemaphoreType.DMA((7,)),
            pltpu.SemaphoreType.DMA((5,)),
            pltpu.SemaphoreType.DMA((5,)),
            pltpu.SemaphoreType.DMA((n // heads,)),
            pltpu.SemaphoreType.DMA((n // heads,)),
            pltpu.SemaphoreType.DMA((2,)),
        ],
        compiler_params=pltpu.CompilerParams(
            collective_id=0, has_side_effects=True, vmem_limit_bytes=60 * 1024 * 1024
        ),
    )(q_res, k_res, v_res, q_new, k_new, v_new, send_row, labels, b_row, b_col, rate)
    parts = 4
    return pl.pallas_call(
        functools.partial(hand_over, parts),
        out_shape=jax.ShapeDtypeStruct((length, columns), BF16),
        in_specs=[any_spec],
        out_specs=any_spec,
        scratch_shapes=[pltpu.SemaphoreType.DMA((parts,))],
        compiler_params=pltpu.CompilerParams(vmem_limit_bytes=60 * 1024 * 1024),
    )(result)


def solution(mesh):
    in_specs = (
        P("seq", "head"),
        P("seq", "head"),
        P("seq", "head"),
        P("seq", "head"),
        P("seq", "head"),
        P("seq", "head"),
        P("seq"),
        P("seq"),
        P(),
        P("head"),
    )
    out_specs = P("seq", "head")
    return jax.shard_map(body, mesh=mesh, in_specs=in_specs, out_specs=out_specs, check_vma=False)
```

```python
import functools

import jax
import jax.numpy as jnp
from jax import lax
from jax.experimental import pallas as pl
from jax.experimental.pallas import tpu as pltpu
from jax.sharding import PartitionSpec as P

MESH = pl.DeviceIdType.MESH
UNIT = 8
PAIR = 2 * UNIT
CHUNK = 256
HD = 128
F32 = jnp.float32
BF16 = jnp.bfloat16
UNFILLED = 4096
STRIDE = 37


def dot(a, b):
    return jnp.dot(a, b, preferred_element_type=F32)


def dot_t(a, b):
    return lax.dot_general(a, b, (((1,), (1,)), ((), ())), preferred_element_type=F32)


def t_dot(a, b):
    return lax.dot_general(a, b, (((0,), (0,)), ((), ())), preferred_element_type=F32)


def two_terms(x):
    high = x.astype(BF16)
    low = (x - high.astype(F32)).astype(BF16)
    return jnp.concatenate([high, low], axis=1)


def fold(x):
    return x[:, :HD] + x[:, HD:]


def kernel(
    n, plane, q_res, k_res, v_res, q_new, k_new, v_new, dest_ref, slot_ref, bound_ref, rate_ref, out,
    send_row, labels, b_row, b_col,
    q_all, k_all, v_all, kv_stack, q_stack, pay_kv, pay_q, got_kv, got_q, got_labels, place,
    mask, alive, keep, o_local, s_local, end, in1, total, in2, before, out3, in3, done,
    load_sem, send_sem, recv_sem, send2, recv2, out_sem,
):
    me = lax.axis_index("seq")
    z, p = me // plane, lax.rem(me, plane)
    depth = n // plane
    resident = q_res.shape[0]
    length = resident + CHUNK
    chunks = length // CHUNK
    last = chunks - 1
    slots = CHUNK
    columns = q_res.shape[1]
    half = columns // 2

    loads = [
        pltpu.make_async_copy(k_new, kv_stack.at[pl.ds(0, slots)], load_sem.at[0]),
        pltpu.make_async_copy(v_new, kv_stack.at[pl.ds(slots, slots)], load_sem.at[1]),
        pltpu.make_async_copy(q_new.at[:, pl.ds(0, half)], q_stack.at[pl.ds(0, slots)], load_sem.at[2]),
        pltpu.make_async_copy(q_new.at[:, pl.ds(half, half)], q_stack.at[pl.ds(slots, slots)], load_sem.at[3]),
        pltpu.make_async_copy(q_res, q_all.at[pl.ds(0, resident)], load_sem.at[4]),
        pltpu.make_async_copy(k_res, k_all.at[pl.ds(0, resident)], load_sem.at[5]),
        pltpu.make_async_copy(v_res, v_all.at[pl.ds(0, resident)], load_sem.at[6]),
    ]
    for load in loads:
        load.start()

    barrier = pltpu.get_barrier_semaphore()

    def greet(step, carry):
        pl.semaphore_signal(
            barrier, inc=1, device_id={"seq": lax.rem(me + step, n)}, device_id_type=MESH
        )
        return carry

    lax.fori_loop(1, n, greet, 0)

    side = 1 - 2 * lax.rem(me, 2)

    def ahead(step):
        return lax.rem(me + n * STRIDE + side * step * STRIDE, n)

    blocks_in = dest_ref.shape[0]
    back = pow(STRIDE, -1, n)
    lane = lax.broadcasted_iota(jnp.int32, (1, 2 * slots), 1)
    unit = lax.rem(lax.shift_right_logical(lane, 3), blocks_in)
    row = jnp.zeros((1, 2 * slots), jnp.int32)
    label = jnp.full((n, HD), -UNFILLED, jnp.int32)
    label_row = lax.broadcasted_iota(jnp.int32, (n, HD), 0)
    for u in range(blocks_in):
        slot = lax.rem((dest_ref[u] - me) * side * back + n * n, n)
        row = jnp.where(unit == u, slot * PAIR, row)
        label = jnp.where(label_row == slot, slot_ref[u] * UNIT, label)
    send_row[...] = row + (lane & (UNIT - 1)) + (lane // slots) * UNIT

    def label_copy(step):
        return pltpu.make_async_remote_copy(
            src_ref=labels.at[step], dst_ref=got_labels.at[step],
            send_sem=send_sem.at[0], recv_sem=recv_sem.at[0],
            device_id={"seq": ahead(step)}, device_id_type=MESH,
        )

    def kv_copy(step):
        rows = pl.ds(pl.multiple_of(step * PAIR, PAIR), PAIR)
        return pltpu.make_async_remote_copy(
            src_ref=pay_kv.at[rows], dst_ref=got_kv.at[rows],
            send_sem=send_sem.at[1], recv_sem=recv_sem.at[1],
            device_id={"seq": ahead(step)}, device_id_type=MESH,
        )

    def q_copy(step):
        rows = pl.ds(pl.multiple_of(step * PAIR, PAIR), PAIR)
        return pltpu.make_async_remote_copy(
            src_ref=pay_q.at[rows], dst_ref=got_q.at[rows],
            send_sem=send_sem.at[2], recv_sem=recv_sem.at[2],
            device_id={"seq": ahead(step)}, device_id_type=MESH,
        )

    def start_range(copy, low, high):
        def one(step, carry):
            copy(step).start()
            return carry

        lax.fori_loop(low, high, one, 0)

    def pick(base):
        rows = base + lax.broadcasted_iota(jnp.int32, (256, 2 * slots), 0)
        return jnp.where(rows == send_row[...], 1.0, 0.0).astype(BF16)

    def pack_kv(base):
        chosen = pick(base)
        for c in range(columns // 256):
            pay_kv[pl.ds(base, 256), pl.ds(c * 256, 256)] = dot(
                chosen, kv_stack[:, pl.ds(c * 256, 256)]
            ).astype(BF16)

    for load in loads[:2]:
        load.wait()
    pack_kv(0)
    pl.semaphore_wait(barrier, n - 1)
    group = 256 // PAIR
    start_range(kv_copy, 1, group)
    for step in range(n):
        labels[step] = label[step : step + 1, :]
    start_range(label_copy, 1, n)
    for part in range(1, n // group):
        pack_kv(part * 256)
        start_range(kv_copy, part * group, (part + 1) * group)

    for load in loads[2:4]:
        load.wait()

    def pack_q(step, carry):
        base = pl.multiple_of(step * 256, 256)
        chosen = pick(base)
        for c in range(half // 256):
            pay_q[pl.ds(base, 256), pl.ds(c * 256, 256)] = dot(
                chosen, q_stack[:, pl.ds(c * 256, 256)]
            ).astype(BF16)
        return carry

    lax.fori_loop(0, n // group, pack_q, 0)
    got_kv[pl.ds(0, PAIR)] = pay_kv[pl.ds(0, PAIR)]
    got_q[pl.ds(0, PAIR)] = pay_q[pl.ds(0, PAIR)]
    got_labels[0] = labels[0]

    rest = pl.ds(PAIR, (n - 1) * PAIR)

    def all_labels():
        return pltpu.make_async_remote_copy(
            src_ref=labels.at[pl.ds(1, n - 1)], dst_ref=got_labels.at[pl.ds(1, n - 1)],
            send_sem=send_sem.at[0], recv_sem=recv_sem.at[0],
            device_id={"seq": lax.rem(me + 1, n)}, device_id_type=MESH,
        )

    def all_kv():
        return pltpu.make_async_remote_copy(
            src_ref=pay_kv.at[rest], dst_ref=got_kv.at[rest],
            send_sem=send_sem.at[1], recv_sem=recv_sem.at[1],
            device_id={"seq": lax.rem(me + 1, n)}, device_id_type=MESH,
        )

    def all_q():
        return pltpu.make_async_remote_copy(
            src_ref=pay_q.at[rest], dst_ref=got_q.at[rest],
            send_sem=send_sem.at[2], recv_sem=recv_sem.at[2],
            device_id={"seq": lax.rem(me + 1, n)}, device_id_type=MESH,
        )

    count = bound_ref.shape[0]
    across = lax.broadcasted_iota(jnp.int32, (1, HD), 1)
    down = lax.broadcasted_iota(jnp.int32, (count, HD), 0)
    line = jnp.full((1, HD), 2**30, jnp.int32)
    column = jnp.full((count, HD), 2**30, jnp.int32)
    for j in range(count):
        line = jnp.where(across == j, bound_ref[j], line)
        column = jnp.where(down == j, bound_ref[j], column)
    b_row[...] = line
    b_col[...] = column

    def clear(low, high):
        inside = (b_row[...] >= low) & (b_row[...] < high)
        found = jnp.sum(jnp.where(inside, 1.0, 0.0), axis=1, keepdims=True)
        return jnp.where(found == 0.0, 1.0, 0.0)

    def starts_upto(position):
        return jnp.sum(jnp.where(b_row[...] <= position, 1.0, 0.0), axis=1, keepdims=True)

    for c in range(chunks):
        base = me * length + c * CHUNK
        spot = base + lax.broadcasted_iota(jnp.int32, (CHUNK, HD), 0)
        count_col = jnp.sum(jnp.where(b_row[...] <= spot, 1.0, 0.0), axis=1, keepdims=True)
        spot_row = base + lax.broadcasted_iota(jnp.int32, (b_col.shape[0], CHUNK), 1)
        b_wide = jnp.concatenate([b_col[...]] * (CHUNK // HD), axis=1)
        count_row = jnp.sum(jnp.where(b_wide <= spot_row, 1.0, 0.0), axis=0, keepdims=True)
        gap = lax.broadcasted_iota(jnp.int32, (CHUNK, CHUNK), 0) - lax.broadcasted_iota(
            jnp.int32, (CHUNK, CHUNK), 1
        )
        mask[c] = jnp.where((gap >= 0) & (count_col == count_row), 1.0, 0.0)
        wide = jnp.broadcast_to(count_col, (CHUNK, HD))
        alive[c] = jnp.where(wide == starts_upto(base - 1), 1.0, 0.0)
        keep[c] = jnp.where(wide == starts_upto(base + CHUNK - 1), 1.0, 0.0)

    def decay_of(x):
        return jnp.exp(jnp.full((1, HD), x, F32))

    def decay_matrix(rate):
        gap = lax.broadcasted_iota(jnp.int32, (CHUNK, CHUNK), 0) - lax.broadcasted_iota(
            jnp.int32, (CHUNK, CHUNK), 1
        )
        return jnp.exp(-rate * jnp.maximum(gap, 0).astype(F32))

    def step_state(c, h, rate, state):
        rows = pl.ds(c * CHUNK, CHUNK)
        cols = pl.ds(pl.multiple_of(h * HD, HD), HD)
        spot = lax.broadcasted_iota(jnp.int32, (CHUNK, HD), 0).astype(F32)
        weight = jnp.exp(-rate * (CHUNK - 1.0 - spot)) * keep[c]
        fresh = fold(t_dot(k_all[rows, cols], two_terms(v_all[rows, cols].astype(F32) * weight)))
        whole = decay_of(-rate * CHUNK) * alive[c, CHUNK - 1 : CHUNK, :]
        return whole * state + fresh

    def local_part(c, h, decay):
        rows = pl.ds(c * CHUNK, CHUNK)
        cols = pl.ds(pl.multiple_of(h * HD, HD), HD)
        scores = dot_t(q_all[rows, cols], k_all[rows, cols])
        weights = (scores * (decay * mask[c])).astype(BF16)
        return dot(weights, v_all[rows, cols])

    for load in loads[4:]:
        load.wait()

    def resident_head(h, carry):
        rate = rate_ref[h]
        decay = decay_matrix(rate)
        cols = pl.ds(pl.multiple_of(h * HD, HD), HD)
        state = jnp.zeros((HD, HD), F32)
        for c in range(last):
            s_local[c, h] = state
            o_local[pl.ds(c * CHUNK, CHUNK), cols] = local_part(c, h, decay)
            state = step_state(c, h, rate, state)
        s_local[last, h] = state
        return carry

    lax.fori_loop(0, plane, resident_head, 0)

    all_labels().wait_recv()
    lane = lax.broadcasted_iota(jnp.int32, (1, HD), 1)
    owner = lax.shift_right_logical(lane, 4)
    pieces = []
    for c in range(n * PAIR // HD):
        piece = jnp.zeros((1, HD), jnp.int32)
        for o in range(HD // PAIR):
            piece = piece + jnp.where(owner == o, got_labels[c * (HD // PAIR) + o], 0)
        inner = (lane & (UNIT - 1)) + lax.shift_right_logical(lane & UNIT, 3) * slots
        pieces.append(piece + inner)
    for c, piece in enumerate(pieces):
        rows = lax.broadcasted_iota(jnp.int32, (2 * slots, HD), 0)
        place[:, pl.ds(c * HD, HD)] = jnp.where(rows == piece, 1.0, 0.0).astype(BF16)

    start_range(q_copy, 1, n // 4)

    all_kv().wait_recv()

    def arrange_kv(step, carry):
        cols = pl.ds(pl.multiple_of(step * 256, 256), 256)
        whole = dot(place[...], got_kv[:, cols]).astype(BF16)
        k_all[pl.ds(resident, slots), cols] = whole[:slots]
        v_all[pl.ds(resident, slots), cols] = whole[slots:]
        return carry

    lax.fori_loop(0, columns // 256, arrange_kv, 0)

    def first_copy(step):
        mate = lax.rem(p + step, plane)
        return pltpu.make_async_remote_copy(
            src_ref=end.at[mate], dst_ref=in1.at[step],
            send_sem=send_sem.at[3], recv_sem=recv_sem.at[3],
            device_id={"seq": z * plane + mate}, device_id_type=MESH,
        )

    def third_copy(step):
        mate = lax.rem(p + step, plane)
        return pltpu.make_async_remote_copy(
            src_ref=out3.at[mate], dst_ref=in3.at[step],
            send_sem=send_sem.at[4], recv_sem=recv_sem.at[4],
            device_id={"seq": z * plane + mate}, device_id_type=MESH,
        )

    def second_copy(step):
        return pltpu.make_async_remote_copy(
            src_ref=total, dst_ref=in2.at[step],
            send_sem=send2.at[step], recv_sem=recv2.at[step],
            device_id={"seq": lax.rem(me + step * plane, n)}, device_id_type=MESH,
        )

    def all_first():
        return pltpu.make_async_remote_copy(
            src_ref=end.at[pl.ds(1, plane - 1)], dst_ref=in1.at[pl.ds(1, plane - 1)],
            send_sem=send_sem.at[3], recv_sem=recv_sem.at[3],
            device_id={"seq": z * plane + lax.rem(p + 1, plane)}, device_id_type=MESH,
        )

    def all_third():
        return pltpu.make_async_remote_copy(
            src_ref=out3.at[pl.ds(1, plane - 1)], dst_ref=in3.at[pl.ds(1, plane - 1)],
            send_sem=send_sem.at[4], recv_sem=recv_sem.at[4],
            device_id={"seq": z * plane + lax.rem(p + 1, plane)}, device_id_type=MESH,
        )

    def end_head(h):
        end[h] = step_state(last, h, rate_ref[h], s_local[last, h])

    def end_mate(step, carry):
        end_head(lax.rem(p + step, plane))
        first_copy(step).start()
        return carry

    lax.fori_loop(1, plane, end_mate, 0)
    start_range(q_copy, n // 4, n // 2)
    end_head(p)
    in1[0] = end[p]
    rate_p = rate_ref[p]
    all_first().wait_recv()

    state = jnp.zeros((HD, HD), F32)
    for m in range(plane):
        shard = z * plane + m
        out3[m] = state
        pass_on = decay_of(-rate_p * length) * clear(shard * length, (shard + 1) * length)
        state = pass_on * state + in1[lax.rem(p - m + plane, plane)]
    total[...] = state.astype(BF16)

    for step in range(1, depth):
        @pl.when(z + step < depth)
        def _(step=step):
            second_copy(step).start()

    start_range(q_copy, n // 2, (3 * n) // 4)

    before[...] = jnp.zeros((HD, HD), F32)
    span = plane * length
    for step in range(1, depth):
        @pl.when(z - step >= 0)
        def _(step=step):
            second_copy(step).wait_recv()
            factor = decay_of(-rate_p * float(span * (step - 1))) * clear(
                (z - step + 1) * span, z * span
            )
            before[...] = before[...] + factor * in2[step].astype(F32)

    earlier = before[...]
    for m in range(plane):
        factor = decay_of(-rate_p * float(length * m)) * clear(z * span, z * span + m * length)
        out3[m] = out3[m] + factor * earlier

    start_range(third_copy, 1, plane)
    start_range(q_copy, (3 * n) // 4, n)
    in3[0] = out3[p]
    all_third().wait_recv()

    def finish(c, h, rate, local):
        rows = pl.ds(c * CHUNK, CHUNK)
        cols = pl.ds(pl.multiple_of(h * HD, HD), HD)
        reach = decay_of(-rate * float(c * CHUNK))
        for m in range(c):
            reach = reach * alive[m, CHUNK - 1 : CHUNK, :]
        carry = s_local[c, h] + reach * in3[lax.rem(p - h + plane, plane)]
        spot = lax.broadcasted_iota(jnp.int32, (CHUNK, HD), 0).astype(F32)
        into = jnp.exp(-rate * (spot + 1.0)) * alive[c]
        whole = local + into * fold(dot(q_all[rows, cols], two_terms(carry)))
        mean = jnp.sum(whole * whole, axis=1, keepdims=True) * (1.0 / HD)
        done[rows, cols] = (whole * lax.rsqrt(mean + 1e-06)).astype(BF16)

    def finish_resident(h, carry):
        rate = rate_ref[h]
        cols = pl.ds(pl.multiple_of(h * HD, HD), HD)
        for c in range(last):
            finish(c, h, rate, o_local[pl.ds(c * CHUNK, CHUNK), cols])
        return carry

    lax.fori_loop(0, plane, finish_resident, 0, unroll=2)
    rows_in = pl.ds(0, resident)
    rows_new = pl.ds(resident, slots)
    store = pltpu.make_async_copy(done.at[rows_in], out.at[rows_in], out_sem.at[0])
    store.start()

    all_q().wait_recv()

    def arrange_q(step, carry):
        cols = pl.ds(pl.multiple_of(step * 256, 256), 256)
        later = pl.ds(pl.multiple_of(half + step * 256, 256), 256)
        whole = dot(place[...], got_q[:, cols]).astype(BF16)
        q_all[pl.ds(resident, slots), cols] = whole[:slots]
        q_all[pl.ds(resident, slots), later] = whole[slots:]
        return carry

    lax.fori_loop(0, half // 256, arrange_q, 0)

    def finish_admitted(h, carry):
        rate = rate_ref[h]
        finish(last, h, rate, local_part(last, h, decay_matrix(rate)))
        return carry

    lax.fori_loop(0, plane, finish_admitted, 0, unroll=2)
    store_new = pltpu.make_async_copy(done.at[rows_new], out.at[rows_new], out_sem.at[1])
    store_new.start()

    all_labels().wait_send()
    all_kv().wait_send()
    all_q().wait_send()
    all_first().wait_send()
    all_third().wait_send()
    for step in range(1, depth):
        @pl.when(z + step < depth)
        def _(step=step):
            second_copy(step).wait_send()
    store.wait()
    store_new.wait()


def hand_over(parts, src, dst, hold, load_sem, store_sem):
    size = src.shape[0] // parts
    pieces = [pl.ds(i * size, size) for i in range(parts)]
    loads = [
        pltpu.make_async_copy(src.at[rows], hold.at[rows], load_sem.at[i])
        for i, rows in enumerate(pieces)
    ]
    stores = [
        pltpu.make_async_copy(hold.at[rows], dst.at[rows], store_sem.at[i])
        for i, rows in enumerate(pieces)
    ]
    for load in loads:
        load.start()
    for load, store in zip(loads, stores):
        load.wait()
        store.start()
    for store in stores:
        store.wait()


def body(q_res, k_res, v_res, q_new, k_new, v_new, admit_dest, admit_slot, boundaries, rate):
    n = lax.axis_size("seq")
    heads = rate.shape[0]
    columns = q_res.shape[1]
    resident, fresh = q_res.shape[0], q_new.shape[0]
    length = resident + fresh
    count = boundaries.shape[0]
    any_spec = pl.BlockSpec(memory_space=pl.ANY)
    smem = pl.BlockSpec(memory_space=pltpu.SMEM)
    chunks = length // CHUNK
    result = pl.pallas_call(
        functools.partial(kernel, n, heads),
        out_shape=jax.ShapeDtypeStruct((length, columns), BF16),
        in_specs=[any_spec] * 6 + [smem] * 4,
        out_specs=any_spec,
        scratch_shapes=[
            pltpu.VMEM((1, 2 * fresh), jnp.int32),
            pltpu.VMEM((n, 1, HD), jnp.int32),
            pltpu.VMEM((1, HD), jnp.int32),
            pltpu.VMEM((count, HD), jnp.int32),
            pltpu.VMEM((length, columns), BF16),
            pltpu.VMEM((length, columns), BF16),
            pltpu.VMEM((length, columns), BF16),
            pltpu.VMEM((2 * fresh, columns), BF16),
            pltpu.VMEM((2 * fresh, columns // 2), BF16),
            pltpu.VMEM((n * PAIR, columns), BF16),
            pltpu.VMEM((n * PAIR, columns // 2), BF16),
            pltpu.VMEM((n * PAIR, columns), BF16),
            pltpu.VMEM((n * PAIR, columns // 2), BF16),
            pltpu.VMEM((n, 1, HD), jnp.int32),
            pltpu.VMEM((2 * fresh, n * PAIR), BF16),
            pltpu.VMEM((chunks, CHUNK, CHUNK), F32),
            pltpu.VMEM((chunks, CHUNK, HD), F32),
            pltpu.VMEM((chunks, CHUNK, HD), F32),
            pltpu.VMEM((resident, columns), F32),
            pltpu.VMEM((chunks, heads, HD, HD), F32),
            pltpu.VMEM((heads, HD, HD), F32),
            pltpu.VMEM((heads, HD, HD), F32),
            pltpu.VMEM((HD, HD), BF16),
            pltpu.VMEM((n // heads, HD, HD), BF16),
            pltpu.VMEM((HD, HD), F32),
            pltpu.VMEM((heads, HD, HD), F32),
            pltpu.VMEM((heads, HD, HD), F32),
            pltpu.VMEM((length, columns), BF16),
            pltpu.SemaphoreType.DMA((7,)),
            pltpu.SemaphoreType.DMA((5,)),
            pltpu.SemaphoreType.DMA((5,)),
            pltpu.SemaphoreType.DMA((n // heads,)),
            pltpu.SemaphoreType.DMA((n // heads,)),
            pltpu.SemaphoreType.DMA((2,)),
        ],
        compiler_params=pltpu.CompilerParams(
            collective_id=0, has_side_effects=True, vmem_limit_bytes=60 * 1024 * 1024
        ),
    )(q_res, k_res, v_res, q_new, k_new, v_new, admit_dest, admit_slot, boundaries, rate)
    parts = 8
    return pl.pallas_call(
        functools.partial(hand_over, parts),
        out_shape=jax.ShapeDtypeStruct((length, columns), BF16),
        in_specs=[any_spec],
        out_specs=any_spec,
        scratch_shapes=[
            pltpu.VMEM((length, columns), BF16),
            pltpu.SemaphoreType.DMA((parts,)),
            pltpu.SemaphoreType.DMA((parts,)),
        ],
        compiler_params=pltpu.CompilerParams(vmem_limit_bytes=60 * 1024 * 1024),
    )(result)


def solution(mesh):
    in_specs = (
        P("seq", "head"),
        P("seq", "head"),
        P("seq", "head"),
        P("seq", "head"),
        P("seq", "head"),
        P("seq", "head"),
        P("seq"),
        P("seq"),
        P(),
        P("head"),
    )
    out_specs = P("seq", "head")
    return jax.shard_map(body, mesh=mesh, in_specs=in_specs, out_specs=out_specs, check_vma=False)
```

```python
import functools

import jax
import jax.numpy as jnp
from jax import lax
from jax.experimental import pallas as pl
from jax.experimental.pallas import tpu as pltpu
from jax.sharding import PartitionSpec as P

MESH = pl.DeviceIdType.MESH
UNIT = 8
PAIR = 2 * UNIT
CHUNK = 256
HD = 128
F32 = jnp.float32
BF16 = jnp.bfloat16
UNFILLED = 4096
STRIDE = 37
GROUPS = 2


def dot(a, b):
    return jnp.dot(a, b, preferred_element_type=F32)


def dot_t(a, b):
    return lax.dot_general(a, b, (((1,), (1,)), ((), ())), preferred_element_type=F32)


def t_dot(a, b):
    return lax.dot_general(a, b, (((0,), (0,)), ((), ())), preferred_element_type=F32)


def two_terms(x):
    high = x.astype(BF16)
    low = (x - high.astype(F32)).astype(BF16)
    return jnp.concatenate([high, low], axis=1)


def fold(x):
    return x[:, :HD] + x[:, HD:]


def kernel(
    n, plane, q_res, k_res, v_res, q_new, k_new, v_new, dest_ref, slot_ref, bound_ref, rate_ref, out,
    send_row, labels, b_row, b_col,
    q_all, k_all, v_all, kv_stack, q_stack, pay_kv, pay_q, got_kv, got_q, got_labels, place,
    mask, alive, keep, o_local, s_local, end, in1, total, in2, before, out3, in3, done,
    load_sem, send_sem, recv_sem, send2, recv2, out_sem,
):
    me = lax.axis_index("seq")
    z, p = me // plane, lax.rem(me, plane)
    depth = n // plane
    resident = q_res.shape[0]
    length = resident + CHUNK
    chunks = length // CHUNK
    last = chunks - 1
    slots = CHUNK
    columns = q_res.shape[1]
    half = columns // 2
    span = columns // GROUPS
    heads_in = plane // GROUPS
    piece_rows = HD // GROUPS

    loads = [
        pltpu.make_async_copy(k_new, kv_stack.at[pl.ds(0, slots)], load_sem.at[0]),
        pltpu.make_async_copy(v_new, kv_stack.at[pl.ds(slots, slots)], load_sem.at[1]),
        pltpu.make_async_copy(q_new.at[:, pl.ds(0, half)], q_stack.at[pl.ds(0, slots)], load_sem.at[2]),
        pltpu.make_async_copy(q_new.at[:, pl.ds(half, half)], q_stack.at[pl.ds(slots, slots)], load_sem.at[3]),
        pltpu.make_async_copy(q_res, q_all.at[pl.ds(0, resident)], load_sem.at[4]),
        pltpu.make_async_copy(k_res, k_all.at[pl.ds(0, resident)], load_sem.at[5]),
        pltpu.make_async_copy(v_res, v_all.at[pl.ds(0, resident)], load_sem.at[6]),
    ]
    for load in loads:
        load.start()

    barrier = pltpu.get_barrier_semaphore()

    def greet(step, carry):
        pl.semaphore_signal(
            barrier, inc=1, device_id={"seq": lax.rem(me + step, n)}, device_id_type=MESH
        )
        return carry

    lax.fori_loop(1, n, greet, 0)

    side = 1 - 2 * lax.rem(me, 2)

    def ahead(step):
        return lax.rem(me + n * STRIDE + side * step * STRIDE, n)

    blocks_in = dest_ref.shape[0]
    back = pow(STRIDE, -1, n)
    lane = lax.broadcasted_iota(jnp.int32, (1, 2 * slots), 1)
    unit = lax.rem(lax.shift_right_logical(lane, 3), blocks_in)
    row = jnp.zeros((1, 2 * slots), jnp.int32)
    label = jnp.full((n, HD), -UNFILLED, jnp.int32)
    label_row = lax.broadcasted_iota(jnp.int32, (n, HD), 0)
    for u in range(blocks_in):
        slot = lax.rem((dest_ref[u] - me) * side * back + n * n, n)
        row = jnp.where(unit == u, slot * PAIR, row)
        label = jnp.where(label_row == slot, slot_ref[u] * UNIT, label)
    send_row[...] = row + (lane & (UNIT - 1)) + (lane // slots) * UNIT

    def label_copy(step):
        return pltpu.make_async_remote_copy(
            src_ref=labels.at[step], dst_ref=got_labels.at[step],
            send_sem=send_sem.at[0], recv_sem=recv_sem.at[0],
            device_id={"seq": ahead(step)}, device_id_type=MESH,
        )

    def kv_copy(g, step):
        rows = pl.ds(pl.multiple_of(step * PAIR, PAIR), PAIR)
        return pltpu.make_async_remote_copy(
            src_ref=pay_kv.at[g, rows], dst_ref=got_kv.at[g, rows],
            send_sem=send_sem.at[4 + g], recv_sem=recv_sem.at[4 + g],
            device_id={"seq": ahead(step)}, device_id_type=MESH,
        )

    def q_copy(step):
        rows = pl.ds(pl.multiple_of(step * PAIR, PAIR), PAIR)
        return pltpu.make_async_remote_copy(
            src_ref=pay_q.at[rows], dst_ref=got_q.at[rows],
            send_sem=send_sem.at[1], recv_sem=recv_sem.at[1],
            device_id={"seq": ahead(step)}, device_id_type=MESH,
        )

    def start_range(copy, low, high):
        def one(step, carry):
            copy(step).start()
            return carry

        lax.fori_loop(low, high, one, 0)

    def pick(base):
        rows = base + lax.broadcasted_iota(jnp.int32, (256, 2 * slots), 0)
        return jnp.where(rows == send_row[...], 1.0, 0.0).astype(BF16)

    def pack_kv(g, base):
        chosen = pick(base)
        for c in range(span // 256):
            pay_kv[g, pl.ds(base, 256), pl.ds(c * 256, 256)] = dot(
                chosen, kv_stack[:, pl.ds(g * span + c * 256, 256)]
            ).astype(BF16)

    for load in loads[:2]:
        load.wait()
    pack_kv(0, 0)
    pl.semaphore_wait(barrier, n - 1)
    group = 256 // PAIR
    kv_first = functools.partial(kv_copy, 0)
    kv_second = functools.partial(kv_copy, 1)
    start_range(kv_first, 1, group)
    for step in range(n):
        labels[step] = label[step : step + 1, :]
    start_range(label_copy, 1, n)
    for part in range(1, n // group):
        pack_kv(0, part * 256)
        start_range(kv_first, part * group, (part + 1) * group)

    def pack_later(step, carry):
        pack_kv(1, pl.multiple_of(step * 256, 256))
        return carry

    lax.fori_loop(0, n // group, pack_later, 0)
    start_range(kv_second, 1, (3 * n) // 8)

    for load in loads[2:4]:
        load.wait()

    def pack_q(step, carry):
        base = pl.multiple_of(step * 256, 256)
        chosen = pick(base)
        for c in range(half // 256):
            pay_q[pl.ds(base, 256), pl.ds(c * 256, 256)] = dot(
                chosen, q_stack[:, pl.ds(c * 256, 256)]
            ).astype(BF16)
        return carry

    lax.fori_loop(0, n // group, pack_q, 0)
    for g in range(GROUPS):
        got_kv[g, pl.ds(0, PAIR)] = pay_kv[g, pl.ds(0, PAIR)]
    got_q[pl.ds(0, PAIR)] = pay_q[pl.ds(0, PAIR)]
    got_labels[0] = labels[0]

    rest = pl.ds(PAIR, (n - 1) * PAIR)

    def all_labels():
        return pltpu.make_async_remote_copy(
            src_ref=labels.at[pl.ds(1, n - 1)], dst_ref=got_labels.at[pl.ds(1, n - 1)],
            send_sem=send_sem.at[0], recv_sem=recv_sem.at[0],
            device_id={"seq": lax.rem(me + 1, n)}, device_id_type=MESH,
        )

    def all_kv(g):
        return pltpu.make_async_remote_copy(
            src_ref=pay_kv.at[g, rest], dst_ref=got_kv.at[g, rest],
            send_sem=send_sem.at[4 + g], recv_sem=recv_sem.at[4 + g],
            device_id={"seq": lax.rem(me + 1, n)}, device_id_type=MESH,
        )

    def all_q():
        return pltpu.make_async_remote_copy(
            src_ref=pay_q.at[rest], dst_ref=got_q.at[rest],
            send_sem=send_sem.at[1], recv_sem=recv_sem.at[1],
            device_id={"seq": lax.rem(me + 1, n)}, device_id_type=MESH,
        )

    count = bound_ref.shape[0]
    across = lax.broadcasted_iota(jnp.int32, (1, HD), 1)
    down = lax.broadcasted_iota(jnp.int32, (count, HD), 0)
    line = jnp.full((1, HD), 2**30, jnp.int32)
    column = jnp.full((count, HD), 2**30, jnp.int32)
    for j in range(count):
        line = jnp.where(across == j, bound_ref[j], line)
        column = jnp.where(down == j, bound_ref[j], column)
    b_row[...] = line
    b_col[...] = column

    def clear(low, high):
        inside = (b_row[...] >= low) & (b_row[...] < high)
        found = jnp.sum(jnp.where(inside, 1.0, 0.0), axis=1, keepdims=True)
        return jnp.where(found == 0.0, 1.0, 0.0)

    def starts_upto(position):
        return jnp.sum(jnp.where(b_row[...] <= position, 1.0, 0.0), axis=1, keepdims=True)

    for c in range(chunks):
        base = me * length + c * CHUNK
        spot = base + lax.broadcasted_iota(jnp.int32, (CHUNK, HD), 0)
        count_col = jnp.sum(jnp.where(b_row[...] <= spot, 1.0, 0.0), axis=1, keepdims=True)
        spot_row = base + lax.broadcasted_iota(jnp.int32, (b_col.shape[0], CHUNK), 1)
        b_wide = jnp.concatenate([b_col[...]] * (CHUNK // HD), axis=1)
        count_row = jnp.sum(jnp.where(b_wide <= spot_row, 1.0, 0.0), axis=0, keepdims=True)
        gap = lax.broadcasted_iota(jnp.int32, (CHUNK, CHUNK), 0) - lax.broadcasted_iota(
            jnp.int32, (CHUNK, CHUNK), 1
        )
        mask[c] = jnp.where((gap >= 0) & (count_col == count_row), 1.0, 0.0)
        wide = jnp.broadcast_to(count_col, (CHUNK, HD))
        alive[c] = jnp.where(wide == starts_upto(base - 1), 1.0, 0.0)
        keep[c] = jnp.where(wide == starts_upto(base + CHUNK - 1), 1.0, 0.0)

    def decay_of(x):
        return jnp.exp(jnp.full((1, HD), x, F32))

    def decay_matrix(rate):
        gap = lax.broadcasted_iota(jnp.int32, (CHUNK, CHUNK), 0) - lax.broadcasted_iota(
            jnp.int32, (CHUNK, CHUNK), 1
        )
        return jnp.exp(-rate * jnp.maximum(gap, 0).astype(F32))

    def step_state(c, h, rate, state):
        rows = pl.ds(c * CHUNK, CHUNK)
        cols = pl.ds(pl.multiple_of(h * HD, HD), HD)
        spot = lax.broadcasted_iota(jnp.int32, (CHUNK, HD), 0).astype(F32)
        weight = jnp.exp(-rate * (CHUNK - 1.0 - spot)) * keep[c]
        fresh = fold(t_dot(k_all[rows, cols], two_terms(v_all[rows, cols].astype(F32) * weight)))
        whole = decay_of(-rate * CHUNK) * alive[c, CHUNK - 1 : CHUNK, :]
        return whole * state + fresh

    def local_part(c, h, decay):
        rows = pl.ds(c * CHUNK, CHUNK)
        cols = pl.ds(pl.multiple_of(h * HD, HD), HD)
        scores = dot_t(q_all[rows, cols], k_all[rows, cols])
        weights = (scores * (decay * mask[c])).astype(BF16)
        return dot(weights, v_all[rows, cols])

    for load in loads[4:]:
        load.wait()

    def resident_head(h, carry):
        rate = rate_ref[h]
        decay = decay_matrix(rate)
        cols = pl.ds(pl.multiple_of(h * HD, HD), HD)
        state = jnp.zeros((HD, HD), F32)
        for c in range(last):
            s_local[c, h] = state
            o_local[pl.ds(c * CHUNK, CHUNK), cols] = local_part(c, h, decay)
            state = step_state(c, h, rate, state)
        s_local[last, h] = state
        return carry

    lax.fori_loop(0, plane, resident_head, 0)

    all_labels().wait_recv()
    lane = lax.broadcasted_iota(jnp.int32, (1, HD), 1)
    owner = lax.shift_right_logical(lane, 4)
    pieces = []
    for c in range(n * PAIR // HD):
        piece = jnp.zeros((1, HD), jnp.int32)
        for o in range(HD // PAIR):
            piece = piece + jnp.where(owner == o, got_labels[c * (HD // PAIR) + o], 0)
        inner = (lane & (UNIT - 1)) + lax.shift_right_logical(lane & UNIT, 3) * slots
        pieces.append(piece + inner)
    for c, piece in enumerate(pieces):
        rows = lax.broadcasted_iota(jnp.int32, (2 * slots, HD), 0)
        place[:, pl.ds(c * HD, HD)] = jnp.where(rows == piece, 1.0, 0.0).astype(BF16)

    def arrange_kv(g):
        def one(step, carry):
            cols = pl.ds(pl.multiple_of(step * 256, 256), 256)
            home = pl.ds(pl.multiple_of(g * span + step * 256, 256), 256)
            whole = dot(place[...], got_kv[g, :, cols]).astype(BF16)
            k_all[pl.ds(resident, slots), home] = whole[:slots]
            v_all[pl.ds(resident, slots), home] = whole[slots:]
            return carry

        lax.fori_loop(0, span // 256, one, 0)

    def first_copy(g, step):
        mate = lax.rem(p + step, plane)
        return pltpu.make_async_remote_copy(
            src_ref=end.at[g * plane + mate], dst_ref=in1.at[g * plane + step],
            send_sem=send_sem.at[6 + g], recv_sem=recv_sem.at[6 + g],
            device_id={"seq": z * plane + mate}, device_id_type=MESH,
        )

    def third_copy(g, step):
        mate = lax.rem(p + step, plane)
        return pltpu.make_async_remote_copy(
            src_ref=out3.at[g * plane + mate], dst_ref=in3.at[g * plane + step],
            send_sem=send_sem.at[2 + g], recv_sem=recv_sem.at[2 + g],
            device_id={"seq": z * plane + mate}, device_id_type=MESH,
        )

    def second_copy(g, step):
        return pltpu.make_async_remote_copy(
            src_ref=total.at[g], dst_ref=in2.at[g * depth + step],
            send_sem=send2.at[g * depth + step], recv_sem=recv2.at[g * depth + step],
            device_id={"seq": lax.rem(me + step * plane, n)}, device_id_type=MESH,
        )

    def all_first(g):
        pieces = pl.ds(g * plane + 1, plane - 1)
        return pltpu.make_async_remote_copy(
            src_ref=end.at[pieces], dst_ref=in1.at[pieces],
            send_sem=send_sem.at[6 + g], recv_sem=recv_sem.at[6 + g],
            device_id={"seq": z * plane + lax.rem(p + 1, plane)}, device_id_type=MESH,
        )

    def all_third(g):
        pieces = pl.ds(g * plane + 1, plane - 1)
        return pltpu.make_async_remote_copy(
            src_ref=out3.at[pieces], dst_ref=in3.at[pieces],
            send_sem=send_sem.at[2 + g], recv_sem=recv_sem.at[2 + g],
            device_id={"seq": z * plane + lax.rem(p + 1, plane)}, device_id_type=MESH,
        )

    plane_rows = plane * length

    def ends(g):
        def one(i, carry):
            h = g * heads_in + i
            state = step_state(last, h, rate_ref[h], s_local[last, h])
            for m in range(GROUPS):
                end[h * GROUPS + m] = state[m * piece_rows : (m + 1) * piece_rows]
            return carry

        lax.fori_loop(0, heads_in, one, 0, unroll=2)
        start_range(functools.partial(first_copy, g), 1, plane)
        in1[g * plane] = end[g * plane + p]

    def totals(g, rate_p):
        all_first(g).wait_recv()
        state = jnp.zeros((piece_rows, HD), F32)
        for m in range(plane):
            shard = z * plane + m
            out3[g * plane + m] = state
            pass_on = decay_of(-rate_p * length) * clear(shard * length, (shard + 1) * length)
            state = pass_on * state + in1[g * plane + lax.rem(p - m + plane, plane)]
        total[g] = state.astype(BF16)
        for step in range(1, depth):
            @pl.when(z + step < depth)
            def _(step=step):
                second_copy(g, step).start()

    def prefixes(g, rate_p):
        before[...] = jnp.zeros((piece_rows, HD), F32)
        for step in range(1, depth):
            @pl.when(z - step >= 0)
            def _(step=step):
                second_copy(g, step).wait_recv()
                factor = decay_of(-rate_p * float(plane_rows * (step - 1))) * clear(
                    (z - step + 1) * plane_rows, z * plane_rows
                )
                before[...] = before[...] + factor * in2[g * depth + step].astype(F32)
        earlier = before[...]
        for m in range(plane):
            factor = decay_of(-rate_p * float(length * m)) * clear(
                z * plane_rows, z * plane_rows + m * length
            )
            out3[g * plane + m] = out3[g * plane + m] + factor * earlier
        start_range(functools.partial(third_copy, g), 1, plane)
        in3[g * plane] = out3[g * plane + p]

    def finish(c, h, rate, local):
        rows = pl.ds(c * CHUNK, CHUNK)
        cols = pl.ds(pl.multiple_of(h * HD, HD), HD)
        reach = decay_of(-rate * float(c * CHUNK))
        for m in range(c):
            reach = reach * alive[m, CHUNK - 1 : CHUNK, :]
        g = h // heads_in
        owner = (h - g * heads_in) * GROUPS
        carried = jnp.concatenate(
            [in3[g * plane + lax.rem(p - owner - m + plane, plane)] for m in range(GROUPS)], axis=0
        )
        carry = s_local[c, h] + reach * carried
        spot = lax.broadcasted_iota(jnp.int32, (CHUNK, HD), 0).astype(F32)
        into = jnp.exp(-rate * (spot + 1.0)) * alive[c]
        whole = local + into * fold(dot(q_all[rows, cols], two_terms(carry)))
        mean = jnp.sum(whole * whole, axis=1, keepdims=True) * (1.0 / HD)
        done[rows, cols] = (whole * lax.rsqrt(mean + 1e-06)).astype(BF16)

    def finish_resident(h, carry):
        rate = rate_ref[h]
        cols = pl.ds(pl.multiple_of(h * HD, HD), HD)
        for c in range(last):
            finish(c, h, rate, o_local[pl.ds(c * CHUNK, CHUNK), cols])
        return carry

    def finish_group(g):
        all_third(g).wait_recv()
        lax.fori_loop(g * heads_in, (g + 1) * heads_in, finish_resident, 0, unroll=2)

    rates = [rate_ref[g * heads_in + p // GROUPS] for g in range(GROUPS)]

    all_kv(0).wait_recv()
    arrange_kv(0)
    ends(0)
    start_range(kv_second, (3 * n) // 8, (5 * n) // 8)
    totals(0, rates[0])
    start_range(kv_second, (5 * n) // 8, (13 * n) // 16)
    prefixes(0, rates[0])
    start_range(kv_second, (13 * n) // 16, n)
    start_range(q_copy, 1, n // 4)

    all_kv(1).wait_recv()
    arrange_kv(1)
    ends(1)
    start_range(q_copy, n // 4, n // 2)
    finish_group(0)
    totals(1, rates[1])
    start_range(q_copy, n // 2, (3 * n) // 4)
    prefixes(1, rates[1])
    start_range(q_copy, (3 * n) // 4, n)
    finish_group(1)
    rows_in = pl.ds(0, resident)
    rows_new = pl.ds(resident, slots)
    store = pltpu.make_async_copy(done.at[rows_in], out.at[rows_in], out_sem.at[0])
    store.start()

    all_q().wait_recv()

    def arrange_q(step, carry):
        cols = pl.ds(pl.multiple_of(step * 256, 256), 256)
        later = pl.ds(pl.multiple_of(half + step * 256, 256), 256)
        whole = dot(place[...], got_q[:, cols]).astype(BF16)
        q_all[pl.ds(resident, slots), cols] = whole[:slots]
        q_all[pl.ds(resident, slots), later] = whole[slots:]
        return carry

    lax.fori_loop(0, half // 256, arrange_q, 0)

    def finish_admitted(h, carry):
        rate = rate_ref[h]
        finish(last, h, rate, local_part(last, h, decay_matrix(rate)))
        return carry

    lax.fori_loop(0, plane, finish_admitted, 0, unroll=2)
    store_new = pltpu.make_async_copy(done.at[rows_new], out.at[rows_new], out_sem.at[1])
    store_new.start()

    all_labels().wait_send()
    all_q().wait_send()
    for g in range(GROUPS):
        all_kv(g).wait_send()
        all_first(g).wait_send()
        all_third(g).wait_send()
        for step in range(1, depth):
            @pl.when(z + step < depth)
            def _(g=g, step=step):
                second_copy(g, step).wait_send()
    store.wait()
    store_new.wait()


def hand_over(parts, src, dst, hold, load_sem, store_sem):
    size = src.shape[0] // parts
    pieces = [pl.ds(i * size, size) for i in range(parts)]
    loads = [
        pltpu.make_async_copy(src.at[rows], hold.at[rows], load_sem.at[i])
        for i, rows in enumerate(pieces)
    ]
    stores = [
        pltpu.make_async_copy(hold.at[rows], dst.at[rows], store_sem.at[i])
        for i, rows in enumerate(pieces)
    ]
    for load in loads:
        load.start()
    for load, store in zip(loads, stores):
        load.wait()
        store.start()
    for store in stores:
        store.wait()


def body(q_res, k_res, v_res, q_new, k_new, v_new, admit_dest, admit_slot, boundaries, rate):
    n = lax.axis_size("seq")
    heads = rate.shape[0]
    columns = q_res.shape[1]
    resident, fresh = q_res.shape[0], q_new.shape[0]
    length = resident + fresh
    count = boundaries.shape[0]
    any_spec = pl.BlockSpec(memory_space=pl.ANY)
    smem = pl.BlockSpec(memory_space=pltpu.SMEM)
    chunks = length // CHUNK
    result = pl.pallas_call(
        functools.partial(kernel, n, heads),
        out_shape=jax.ShapeDtypeStruct((length, columns), BF16),
        in_specs=[any_spec] * 6 + [smem] * 4,
        out_specs=any_spec,
        scratch_shapes=[
            pltpu.VMEM((1, 2 * fresh), jnp.int32),
            pltpu.VMEM((n, 1, HD), jnp.int32),
            pltpu.VMEM((1, HD), jnp.int32),
            pltpu.VMEM((count, HD), jnp.int32),
            pltpu.VMEM((length, columns), BF16),
            pltpu.VMEM((length, columns), BF16),
            pltpu.VMEM((length, columns), BF16),
            pltpu.VMEM((2 * fresh, columns), BF16),
            pltpu.VMEM((2 * fresh, columns // 2), BF16),
            pltpu.VMEM((GROUPS, n * PAIR, columns // GROUPS), BF16),
            pltpu.VMEM((n * PAIR, columns // 2), BF16),
            pltpu.VMEM((GROUPS, n * PAIR, columns // GROUPS), BF16),
            pltpu.VMEM((n * PAIR, columns // 2), BF16),
            pltpu.VMEM((n, 1, HD), jnp.int32),
            pltpu.VMEM((2 * fresh, n * PAIR), BF16),
            pltpu.VMEM((chunks, CHUNK, CHUNK), F32),
            pltpu.VMEM((chunks, CHUNK, HD), F32),
            pltpu.VMEM((chunks, CHUNK, HD), F32),
            pltpu.VMEM((resident, columns), F32),
            pltpu.VMEM((chunks, heads, HD, HD), F32),
            pltpu.VMEM((GROUPS * heads, HD // GROUPS, HD), F32),
            pltpu.VMEM((GROUPS * heads, HD // GROUPS, HD), F32),
            pltpu.VMEM((GROUPS, HD // GROUPS, HD), BF16),
            pltpu.VMEM((GROUPS * (n // heads), HD // GROUPS, HD), BF16),
            pltpu.VMEM((HD // GROUPS, HD), F32),
            pltpu.VMEM((GROUPS * heads, HD // GROUPS, HD), F32),
            pltpu.VMEM((GROUPS * heads, HD // GROUPS, HD), F32),
            pltpu.VMEM((length, columns), BF16),
            pltpu.SemaphoreType.DMA((7,)),
            pltpu.SemaphoreType.DMA((4 + 2 * GROUPS,)),
            pltpu.SemaphoreType.DMA((4 + 2 * GROUPS,)),
            pltpu.SemaphoreType.DMA((GROUPS * (n // heads),)),
            pltpu.SemaphoreType.DMA((GROUPS * (n // heads),)),
            pltpu.SemaphoreType.DMA((2,)),
        ],
        compiler_params=pltpu.CompilerParams(
            collective_id=0, has_side_effects=True, vmem_limit_bytes=60 * 1024 * 1024
        ),
    )(q_res, k_res, v_res, q_new, k_new, v_new, admit_dest, admit_slot, boundaries, rate)
    parts = 8
    return pl.pallas_call(
        functools.partial(hand_over, parts),
        out_shape=jax.ShapeDtypeStruct((length, columns), BF16),
        in_specs=[any_spec],
        out_specs=any_spec,
        scratch_shapes=[
            pltpu.VMEM((length, columns), BF16),
            pltpu.SemaphoreType.DMA((parts,)),
            pltpu.SemaphoreType.DMA((parts,)),
        ],
        compiler_params=pltpu.CompilerParams(vmem_limit_bytes=60 * 1024 * 1024),
    )(result)


def solution(mesh):
    in_specs = (
        P("seq", "head"),
        P("seq", "head"),
        P("seq", "head"),
        P("seq", "head"),
        P("seq", "head"),
        P("seq", "head"),
        P("seq"),
        P("seq"),
        P(),
        P("head"),
    )
    out_specs = P("seq", "head")
    return jax.shard_map(body, mesh=mesh, in_specs=in_specs, out_specs=out_specs, check_vma=False)
```

```python
import functools

import jax
import jax.numpy as jnp
from jax import lax
from jax.experimental import pallas as pl
from jax.experimental.pallas import tpu as pltpu
from jax.sharding import PartitionSpec as P

MESH = pl.DeviceIdType.MESH
UNIT = 8
PAIR = 2 * UNIT
CHUNK = 256
HD = 128
F32 = jnp.float32
BF16 = jnp.bfloat16
UNFILLED = 4096
STRIDE = 37
GROUPS = 2


def dot(a, b):
    return jnp.dot(a, b, preferred_element_type=F32)


def dot_t(a, b):
    return lax.dot_general(a, b, (((1,), (1,)), ((), ())), preferred_element_type=F32)


def t_dot(a, b):
    return lax.dot_general(a, b, (((0,), (0,)), ((), ())), preferred_element_type=F32)


def two_terms(x):
    high = x.astype(BF16)
    low = (x - high.astype(F32)).astype(BF16)
    return jnp.concatenate([high, low], axis=1)


def fold(x):
    return x[:, :HD] + x[:, HD:]


def kernel(
    n, plane, q_res, k_res, v_res, q_new, k_new, v_new, dest_ref, slot_ref, bound_ref, rate_ref, out,
    send_row, labels, b_row, b_col,
    q_all, k_all, v_all, kv_stack, q_stack, pay_kv, pay_q, got_kv, got_q, got_labels, place,
    mask, alive, keep, o_local, s_local, end, in1, total, in2, before, out3, in3, done, relay,
    load_sem, send_sem, recv_sem, send2, recv2, out_sem, relay_recv, pass_send,
):
    me = lax.axis_index("seq")
    z, p = me // plane, lax.rem(me, plane)
    depth = n // plane
    resident = q_res.shape[0]
    length = resident + CHUNK
    chunks = length // CHUNK
    last = chunks - 1
    slots = CHUNK
    columns = q_res.shape[1]
    half = columns // 2
    span = columns // GROUPS
    heads_in = plane // GROUPS
    piece_rows = HD // GROUPS

    loads = [
        pltpu.make_async_copy(k_new, kv_stack.at[pl.ds(0, slots)], load_sem.at[0]),
        pltpu.make_async_copy(v_new, kv_stack.at[pl.ds(slots, slots)], load_sem.at[1]),
        pltpu.make_async_copy(q_new.at[:, pl.ds(0, half)], q_stack.at[pl.ds(0, slots)], load_sem.at[2]),
        pltpu.make_async_copy(q_new.at[:, pl.ds(half, half)], q_stack.at[pl.ds(slots, slots)], load_sem.at[3]),
        pltpu.make_async_copy(q_res, q_all.at[pl.ds(0, resident)], load_sem.at[4]),
        pltpu.make_async_copy(k_res, k_all.at[pl.ds(0, resident)], load_sem.at[5]),
        pltpu.make_async_copy(v_res, v_all.at[pl.ds(0, resident)], load_sem.at[6]),
    ]
    for load in loads:
        load.start()

    barrier = pltpu.get_barrier_semaphore()

    def greet(step, carry):
        pl.semaphore_signal(
            barrier, inc=1, device_id={"seq": lax.rem(me + step, n)}, device_id_type=MESH
        )
        return carry

    lax.fori_loop(1, n, greet, 0)

    side = 1 - 2 * lax.rem(me, 2)

    def ahead(step):
        return lax.rem(me + n * STRIDE + side * step * STRIDE, n)

    blocks_in = dest_ref.shape[0]
    back = pow(STRIDE, -1, n)
    lane = lax.broadcasted_iota(jnp.int32, (1, 2 * slots), 1)
    unit = lax.rem(lax.shift_right_logical(lane, 3), blocks_in)
    row = jnp.zeros((1, 2 * slots), jnp.int32)
    label = jnp.full((n, HD), -UNFILLED, jnp.int32)
    label_row = lax.broadcasted_iota(jnp.int32, (n, HD), 0)
    for u in range(blocks_in):
        slot = lax.rem((dest_ref[u] - me) * side * back + n * n, n)
        row = jnp.where(unit == u, slot * PAIR, row)
        label = jnp.where(label_row == slot, slot_ref[u] * UNIT, label)
    send_row[...] = row + (lane & (UNIT - 1)) + (lane // slots) * UNIT

    def label_copy(step):
        return pltpu.make_async_remote_copy(
            src_ref=labels.at[step], dst_ref=got_labels.at[step],
            send_sem=send_sem.at[0], recv_sem=recv_sem.at[0],
            device_id={"seq": ahead(step)}, device_id_type=MESH,
        )

    def kv_copy(g, step):
        rows = pl.ds(pl.multiple_of(step * PAIR, PAIR), PAIR)
        return pltpu.make_async_remote_copy(
            src_ref=pay_kv.at[g, rows], dst_ref=got_kv.at[g, rows],
            send_sem=send_sem.at[4 + g], recv_sem=recv_sem.at[4 + g],
            device_id={"seq": ahead(step)}, device_id_type=MESH,
        )

    def q_copy(step):
        rows = pl.ds(pl.multiple_of(step * PAIR, PAIR), PAIR)
        return pltpu.make_async_remote_copy(
            src_ref=pay_q.at[rows], dst_ref=got_q.at[rows],
            send_sem=send_sem.at[1], recv_sem=recv_sem.at[1],
            device_id={"seq": ahead(step)}, device_id_type=MESH,
        )

    def start_range(copy, low, high):
        def one(step, carry):
            copy(step).start()
            return carry

        lax.fori_loop(low, high, one, 0)

    hop = depth // 4

    def is_far(step):
        return lax.rem(ahead(step) // plane - z + depth, depth) == depth // 2

    def payload(k):
        return pay_q if k == GROUPS else pay_kv.at[k]

    def arrived(k):
        return got_q if k == GROUPS else got_kv.at[k]

    def payload_sem(k):
        return 1 if k == GROUPS else 4 + k

    def direct_copy(k, step):
        return q_copy(step) if k == GROUPS else kv_copy(k, step)

    def relay_copy(k, step):
        place_in = lax.rem(ahead(step), plane)
        way = 1 - 2 * lax.rem(place_in, 2)
        return pltpu.make_async_remote_copy(
            src_ref=payload(k).at[pl.ds(pl.multiple_of(step * PAIR, PAIR), PAIR)],
            dst_ref=relay.at[k, pl.ds(pl.multiple_of(place_in * PAIR, PAIR), PAIR)],
            send_sem=send_sem.at[payload_sem(k)], recv_sem=relay_recv.at[k],
            device_id={"seq": lax.rem(me + way * hop * plane + n, n)}, device_id_type=MESH,
        )

    def pass_copy(k, place_in):
        way = 1 - 2 * lax.rem(place_in, 2)
        source = lax.rem(me - way * hop * plane + n, n)
        target = lax.rem(z + way * hop + depth, depth) * plane + place_in
        slot = lax.rem((target - source) * side * back + n * n, n)
        return pltpu.make_async_remote_copy(
            src_ref=relay.at[k, pl.ds(pl.multiple_of(place_in * PAIR, PAIR), PAIR)],
            dst_ref=arrived(k).at[pl.ds(pl.multiple_of(slot * PAIR, PAIR), PAIR)],
            send_sem=pass_send.at[k], recv_sem=recv_sem.at[payload_sem(k)],
            device_id={"seq": target}, device_id_type=MESH,
        )

    def relayed(k):
        return pltpu.make_async_remote_copy(
            src_ref=relay.at[k], dst_ref=relay.at[k],
            send_sem=pass_send.at[k], recv_sem=relay_recv.at[k],
            device_id={"seq": lax.rem(me + 1, n)}, device_id_type=MESH,
        )

    def start_far(k, low, high):
        def one(step, carry):
            @pl.when(is_far(step))
            def _():
                relay_copy(k, step).start()
            return carry

        lax.fori_loop(low, high, one, 0)

    def start_near(k, low, high):
        def one(step, carry):
            @pl.when(jnp.logical_not(is_far(step)))
            def _():
                direct_copy(k, step).start()
            return carry

        lax.fori_loop(low, high, one, 0)

    def pass_on_all(k):
        relayed(k).wait_recv()

        def one(place_in, carry):
            pass_copy(k, place_in).start()
            return carry

        lax.fori_loop(0, plane, one, 0)

    def pick(base):
        rows = base + lax.broadcasted_iota(jnp.int32, (256, 2 * slots), 0)
        return jnp.where(rows == send_row[...], 1.0, 0.0).astype(BF16)

    def pack_kv(g, base):
        chosen = pick(base)
        for c in range(span // 256):
            pay_kv[g, pl.ds(base, 256), pl.ds(c * 256, 256)] = dot(
                chosen, kv_stack[:, pl.ds(g * span + c * 256, 256)]
            ).astype(BF16)

    for load in loads[:2]:
        load.wait()
    pack_kv(0, 0)
    pl.semaphore_wait(barrier, n - 1)
    group = 256 // PAIR
    start_far(0, 1, group)
    start_near(0, 1, group)
    for step in range(n):
        labels[step] = label[step : step + 1, :]
    start_range(label_copy, 1, n)
    for part in range(1, n // group):
        pack_kv(0, part * 256)
    start_far(0, group, n)
    start_near(0, group, n)

    def pack_later(step, carry):
        pack_kv(1, pl.multiple_of(step * 256, 256))
        return carry

    lax.fori_loop(0, n // group, pack_later, 0)
    start_far(1, 1, n)

    for load in loads[2:4]:
        load.wait()

    def pack_q(step, carry):
        base = pl.multiple_of(step * 256, 256)
        chosen = pick(base)
        for c in range(half // 256):
            pay_q[pl.ds(base, 256), pl.ds(c * 256, 256)] = dot(
                chosen, q_stack[:, pl.ds(c * 256, 256)]
            ).astype(BF16)
        return carry

    lax.fori_loop(0, n // group, pack_q, 0)
    for g in range(GROUPS):
        got_kv[g, pl.ds(0, PAIR)] = pay_kv[g, pl.ds(0, PAIR)]
    got_q[pl.ds(0, PAIR)] = pay_q[pl.ds(0, PAIR)]
    got_labels[0] = labels[0]

    rest = pl.ds(PAIR, (n - 1) * PAIR)

    def all_labels():
        return pltpu.make_async_remote_copy(
            src_ref=labels.at[pl.ds(1, n - 1)], dst_ref=got_labels.at[pl.ds(1, n - 1)],
            send_sem=send_sem.at[0], recv_sem=recv_sem.at[0],
            device_id={"seq": lax.rem(me + 1, n)}, device_id_type=MESH,
        )

    def all_kv(g):
        return pltpu.make_async_remote_copy(
            src_ref=pay_kv.at[g, rest], dst_ref=got_kv.at[g, rest],
            send_sem=send_sem.at[4 + g], recv_sem=recv_sem.at[4 + g],
            device_id={"seq": lax.rem(me + 1, n)}, device_id_type=MESH,
        )

    def all_q():
        return pltpu.make_async_remote_copy(
            src_ref=pay_q.at[rest], dst_ref=got_q.at[rest],
            send_sem=send_sem.at[1], recv_sem=recv_sem.at[1],
            device_id={"seq": lax.rem(me + 1, n)}, device_id_type=MESH,
        )

    count = bound_ref.shape[0]
    across = lax.broadcasted_iota(jnp.int32, (1, HD), 1)
    down = lax.broadcasted_iota(jnp.int32, (count, HD), 0)
    line = jnp.full((1, HD), 2**30, jnp.int32)
    column = jnp.full((count, HD), 2**30, jnp.int32)
    for j in range(count):
        line = jnp.where(across == j, bound_ref[j], line)
        column = jnp.where(down == j, bound_ref[j], column)
    b_row[...] = line
    b_col[...] = column

    def clear(low, high):
        inside = (b_row[...] >= low) & (b_row[...] < high)
        found = jnp.sum(jnp.where(inside, 1.0, 0.0), axis=1, keepdims=True)
        return jnp.where(found == 0.0, 1.0, 0.0)

    def starts_upto(position):
        return jnp.sum(jnp.where(b_row[...] <= position, 1.0, 0.0), axis=1, keepdims=True)

    for c in range(chunks):
        base = me * length + c * CHUNK
        spot = base + lax.broadcasted_iota(jnp.int32, (CHUNK, HD), 0)
        count_col = jnp.sum(jnp.where(b_row[...] <= spot, 1.0, 0.0), axis=1, keepdims=True)
        spot_row = base + lax.broadcasted_iota(jnp.int32, (b_col.shape[0], CHUNK), 1)
        b_wide = jnp.concatenate([b_col[...]] * (CHUNK // HD), axis=1)
        count_row = jnp.sum(jnp.where(b_wide <= spot_row, 1.0, 0.0), axis=0, keepdims=True)
        gap = lax.broadcasted_iota(jnp.int32, (CHUNK, CHUNK), 0) - lax.broadcasted_iota(
            jnp.int32, (CHUNK, CHUNK), 1
        )
        mask[c] = jnp.where((gap >= 0) & (count_col == count_row), 1.0, 0.0)
        wide = jnp.broadcast_to(count_col, (CHUNK, HD))
        alive[c] = jnp.where(wide == starts_upto(base - 1), 1.0, 0.0)
        keep[c] = jnp.where(wide == starts_upto(base + CHUNK - 1), 1.0, 0.0)

    def decay_of(x):
        return jnp.exp(jnp.full((1, HD), x, F32))

    def decay_matrix(rate):
        gap = lax.broadcasted_iota(jnp.int32, (CHUNK, CHUNK), 0) - lax.broadcasted_iota(
            jnp.int32, (CHUNK, CHUNK), 1
        )
        return jnp.exp(-rate * jnp.maximum(gap, 0).astype(F32))

    def step_state(c, h, rate, state):
        rows = pl.ds(c * CHUNK, CHUNK)
        cols = pl.ds(pl.multiple_of(h * HD, HD), HD)
        spot = lax.broadcasted_iota(jnp.int32, (CHUNK, HD), 0).astype(F32)
        weight = jnp.exp(-rate * (CHUNK - 1.0 - spot)) * keep[c]
        fresh = fold(t_dot(k_all[rows, cols], two_terms(v_all[rows, cols].astype(F32) * weight)))
        whole = decay_of(-rate * CHUNK) * alive[c, CHUNK - 1 : CHUNK, :]
        return whole * state + fresh

    def local_part(c, h, decay):
        rows = pl.ds(c * CHUNK, CHUNK)
        cols = pl.ds(pl.multiple_of(h * HD, HD), HD)
        scores = dot_t(q_all[rows, cols], k_all[rows, cols])
        weights = (scores * (decay * mask[c])).astype(BF16)
        return dot(weights, v_all[rows, cols])

    for load in loads[4:]:
        load.wait()

    def resident_head(h, carry):
        rate = rate_ref[h]
        decay = decay_matrix(rate)
        cols = pl.ds(pl.multiple_of(h * HD, HD), HD)
        state = jnp.zeros((HD, HD), F32)
        for c in range(last):
            s_local[c, h] = state
            o_local[pl.ds(c * CHUNK, CHUNK), cols] = local_part(c, h, decay)
            state = step_state(c, h, rate, state)
        s_local[last, h] = state
        return carry

    lax.fori_loop(0, heads_in, resident_head, 0)
    pass_on_all(0)
    start_near(1, 1, (3 * n) // 8)
    lax.fori_loop(heads_in, plane, resident_head, 0)

    all_labels().wait_recv()
    lane = lax.broadcasted_iota(jnp.int32, (1, HD), 1)
    owner = lax.shift_right_logical(lane, 4)
    pieces = []
    for c in range(n * PAIR // HD):
        piece = jnp.zeros((1, HD), jnp.int32)
        for o in range(HD // PAIR):
            piece = piece + jnp.where(owner == o, got_labels[c * (HD // PAIR) + o], 0)
        inner = (lane & (UNIT - 1)) + lax.shift_right_logical(lane & UNIT, 3) * slots
        pieces.append(piece + inner)
    for c, piece in enumerate(pieces):
        rows = lax.broadcasted_iota(jnp.int32, (2 * slots, HD), 0)
        place[:, pl.ds(c * HD, HD)] = jnp.where(rows == piece, 1.0, 0.0).astype(BF16)

    def arrange_kv(g):
        def one(step, carry):
            cols = pl.ds(pl.multiple_of(step * 256, 256), 256)
            home = pl.ds(pl.multiple_of(g * span + step * 256, 256), 256)
            whole = dot(place[...], got_kv[g, :, cols]).astype(BF16)
            k_all[pl.ds(resident, slots), home] = whole[:slots]
            v_all[pl.ds(resident, slots), home] = whole[slots:]
            return carry

        lax.fori_loop(0, span // 256, one, 0)

    def first_copy(g, step):
        mate = lax.rem(p + step, plane)
        return pltpu.make_async_remote_copy(
            src_ref=end.at[g * plane + mate], dst_ref=in1.at[g * plane + step],
            send_sem=send_sem.at[6 + g], recv_sem=recv_sem.at[6 + g],
            device_id={"seq": z * plane + mate}, device_id_type=MESH,
        )

    def third_copy(g, step):
        mate = lax.rem(p + step, plane)
        return pltpu.make_async_remote_copy(
            src_ref=out3.at[g * plane + mate], dst_ref=in3.at[g * plane + step],
            send_sem=send_sem.at[2 + g], recv_sem=recv_sem.at[2 + g],
            device_id={"seq": z * plane + mate}, device_id_type=MESH,
        )

    def second_copy(g, step):
        return pltpu.make_async_remote_copy(
            src_ref=total.at[g], dst_ref=in2.at[g * depth + step],
            send_sem=send2.at[g * depth + step], recv_sem=recv2.at[g * depth + step],
            device_id={"seq": lax.rem(me + step * plane, n)}, device_id_type=MESH,
        )

    def all_first(g):
        pieces = pl.ds(g * plane + 1, plane - 1)
        return pltpu.make_async_remote_copy(
            src_ref=end.at[pieces], dst_ref=in1.at[pieces],
            send_sem=send_sem.at[6 + g], recv_sem=recv_sem.at[6 + g],
            device_id={"seq": z * plane + lax.rem(p + 1, plane)}, device_id_type=MESH,
        )

    def all_third(g):
        pieces = pl.ds(g * plane + 1, plane - 1)
        return pltpu.make_async_remote_copy(
            src_ref=out3.at[pieces], dst_ref=in3.at[pieces],
            send_sem=send_sem.at[2 + g], recv_sem=recv_sem.at[2 + g],
            device_id={"seq": z * plane + lax.rem(p + 1, plane)}, device_id_type=MESH,
        )

    plane_rows = plane * length

    def ends(g):
        def one(i, carry):
            h = g * heads_in + i
            state = step_state(last, h, rate_ref[h], s_local[last, h])
            for m in range(GROUPS):
                end[h * GROUPS + m] = state[m * piece_rows : (m + 1) * piece_rows]
            return carry

        lax.fori_loop(0, heads_in, one, 0, unroll=2)
        start_range(functools.partial(first_copy, g), 1, plane)
        in1[g * plane] = end[g * plane + p]

    def totals(g, rate_p):
        all_first(g).wait_recv()
        state = jnp.zeros((piece_rows, HD), F32)
        for m in range(plane):
            shard = z * plane + m
            out3[g * plane + m] = state
            pass_on = decay_of(-rate_p * length) * clear(shard * length, (shard + 1) * length)
            state = pass_on * state + in1[g * plane + lax.rem(p - m + plane, plane)]
        total[g] = state.astype(BF16)
        for step in range(1, depth):
            @pl.when(z + step < depth)
            def _(step=step):
                second_copy(g, step).start()

    def prefixes(g, rate_p):
        before[...] = jnp.zeros((piece_rows, HD), F32)
        for step in range(1, depth):
            @pl.when(z - step >= 0)
            def _(step=step):
                second_copy(g, step).wait_recv()
                factor = decay_of(-rate_p * float(plane_rows * (step - 1))) * clear(
                    (z - step + 1) * plane_rows, z * plane_rows
                )
                before[...] = before[...] + factor * in2[g * depth + step].astype(F32)
        earlier = before[...]
        for m in range(plane):
            factor = decay_of(-rate_p * float(length * m)) * clear(
                z * plane_rows, z * plane_rows + m * length
            )
            out3[g * plane + m] = out3[g * plane + m] + factor * earlier
        start_range(functools.partial(third_copy, g), 1, plane)
        in3[g * plane] = out3[g * plane + p]

    def finish(c, h, rate, local):
        rows = pl.ds(c * CHUNK, CHUNK)
        cols = pl.ds(pl.multiple_of(h * HD, HD), HD)
        reach = decay_of(-rate * float(c * CHUNK))
        for m in range(c):
            reach = reach * alive[m, CHUNK - 1 : CHUNK, :]
        g = h // heads_in
        owner = (h - g * heads_in) * GROUPS
        carried = jnp.concatenate(
            [in3[g * plane + lax.rem(p - owner - m + plane, plane)] for m in range(GROUPS)], axis=0
        )
        carry = s_local[c, h] + reach * carried
        spot = lax.broadcasted_iota(jnp.int32, (CHUNK, HD), 0).astype(F32)
        into = jnp.exp(-rate * (spot + 1.0)) * alive[c]
        whole = local + into * fold(dot(q_all[rows, cols], two_terms(carry)))
        mean = jnp.sum(whole * whole, axis=1, keepdims=True) * (1.0 / HD)
        done[rows, cols] = (whole * lax.rsqrt(mean + 1e-06)).astype(BF16)

    def finish_resident(h, carry):
        rate = rate_ref[h]
        cols = pl.ds(pl.multiple_of(h * HD, HD), HD)
        for c in range(last):
            finish(c, h, rate, o_local[pl.ds(c * CHUNK, CHUNK), cols])
        return carry

    def finish_group(g):
        all_third(g).wait_recv()
        lax.fori_loop(g * heads_in, (g + 1) * heads_in, finish_resident, 0, unroll=2)

    rates = [rate_ref[g * heads_in + p // GROUPS] for g in range(GROUPS)]

    all_kv(0).wait_recv()
    arrange_kv(0)
    ends(0)
    start_near(1, (3 * n) // 8, (5 * n) // 8)
    totals(0, rates[0])
    pass_on_all(1)
    start_near(1, (5 * n) // 8, (13 * n) // 16)
    prefixes(0, rates[0])
    start_near(1, (13 * n) // 16, n)
    start_far(2, 1, n)
    start_near(2, 1, n // 4)

    all_kv(1).wait_recv()
    arrange_kv(1)
    ends(1)
    start_near(2, n // 4, n // 2)
    finish_group(0)
    totals(1, rates[1])
    pass_on_all(2)
    start_near(2, n // 2, (3 * n) // 4)
    prefixes(1, rates[1])
    start_near(2, (3 * n) // 4, n)
    finish_group(1)
    rows_in = pl.ds(0, resident)
    rows_new = pl.ds(resident, slots)
    store = pltpu.make_async_copy(done.at[rows_in], out.at[rows_in], out_sem.at[0])
    store.start()

    all_q().wait_recv()

    def arrange_q(step, carry):
        cols = pl.ds(pl.multiple_of(step * 256, 256), 256)
        later = pl.ds(pl.multiple_of(half + step * 256, 256), 256)
        whole = dot(place[...], got_q[:, cols]).astype(BF16)
        q_all[pl.ds(resident, slots), cols] = whole[:slots]
        q_all[pl.ds(resident, slots), later] = whole[slots:]
        return carry

    lax.fori_loop(0, half // 256, arrange_q, 0)

    def finish_admitted(h, carry):
        rate = rate_ref[h]
        finish(last, h, rate, local_part(last, h, decay_matrix(rate)))
        return carry

    lax.fori_loop(0, plane, finish_admitted, 0, unroll=2)
    store_new = pltpu.make_async_copy(done.at[rows_new], out.at[rows_new], out_sem.at[1])
    store_new.start()

    all_labels().wait_send()
    all_q().wait_send()
    for k in range(GROUPS + 1):
        relayed(k).wait_send()
    for g in range(GROUPS):
        all_kv(g).wait_send()
        all_first(g).wait_send()
        all_third(g).wait_send()
        for step in range(1, depth):
            @pl.when(z + step < depth)
            def _(g=g, step=step):
                second_copy(g, step).wait_send()
    store.wait()
    store_new.wait()


def hand_over(parts, src, dst, hold, load_sem, store_sem):
    size = src.shape[0] // parts
    pieces = [pl.ds(i * size, size) for i in range(parts)]
    loads = [
        pltpu.make_async_copy(src.at[rows], hold.at[rows], load_sem.at[i])
        for i, rows in enumerate(pieces)
    ]
    stores = [
        pltpu.make_async_copy(hold.at[rows], dst.at[rows], store_sem.at[i])
        for i, rows in enumerate(pieces)
    ]
    for load in loads:
        load.start()
    for load, store in zip(loads, stores):
        load.wait()
        store.start()
    for store in stores:
        store.wait()


def body(q_res, k_res, v_res, q_new, k_new, v_new, admit_dest, admit_slot, boundaries, rate):
    n = lax.axis_size("seq")
    heads = rate.shape[0]
    columns = q_res.shape[1]
    resident, fresh = q_res.shape[0], q_new.shape[0]
    length = resident + fresh
    count = boundaries.shape[0]
    any_spec = pl.BlockSpec(memory_space=pl.ANY)
    smem = pl.BlockSpec(memory_space=pltpu.SMEM)
    chunks = length // CHUNK
    result = pl.pallas_call(
        functools.partial(kernel, n, heads),
        out_shape=jax.ShapeDtypeStruct((length, columns), BF16),
        in_specs=[any_spec] * 6 + [smem] * 4,
        out_specs=any_spec,
        scratch_shapes=[
            pltpu.VMEM((1, 2 * fresh), jnp.int32),
            pltpu.VMEM((n, 1, HD), jnp.int32),
            pltpu.VMEM((1, HD), jnp.int32),
            pltpu.VMEM((count, HD), jnp.int32),
            pltpu.VMEM((length, columns), BF16),
            pltpu.VMEM((length, columns), BF16),
            pltpu.VMEM((length, columns), BF16),
            pltpu.VMEM((2 * fresh, columns), BF16),
            pltpu.VMEM((2 * fresh, columns // 2), BF16),
            pltpu.VMEM((GROUPS, n * PAIR, columns // GROUPS), BF16),
            pltpu.VMEM((n * PAIR, columns // 2), BF16),
            pltpu.VMEM((GROUPS, n * PAIR, columns // GROUPS), BF16),
            pltpu.VMEM((n * PAIR, columns // 2), BF16),
            pltpu.VMEM((n, 1, HD), jnp.int32),
            pltpu.VMEM((2 * fresh, n * PAIR), BF16),
            pltpu.VMEM((chunks, CHUNK, CHUNK), F32),
            pltpu.VMEM((chunks, CHUNK, HD), F32),
            pltpu.VMEM((chunks, CHUNK, HD), F32),
            pltpu.VMEM((resident, columns), F32),
            pltpu.VMEM((chunks, heads, HD, HD), F32),
            pltpu.VMEM((GROUPS * heads, HD // GROUPS, HD), F32),
            pltpu.VMEM((GROUPS * heads, HD // GROUPS, HD), F32),
            pltpu.VMEM((GROUPS, HD // GROUPS, HD), BF16),
            pltpu.VMEM((GROUPS * (n // heads), HD // GROUPS, HD), BF16),
            pltpu.VMEM((HD // GROUPS, HD), F32),
            pltpu.VMEM((GROUPS * heads, HD // GROUPS, HD), F32),
            pltpu.VMEM((GROUPS * heads, HD // GROUPS, HD), F32),
            pltpu.VMEM((length, columns), BF16),
            pltpu.VMEM((GROUPS + 1, heads * PAIR, columns // GROUPS), BF16),
            pltpu.SemaphoreType.DMA((7,)),
            pltpu.SemaphoreType.DMA((4 + 2 * GROUPS,)),
            pltpu.SemaphoreType.DMA((4 + 2 * GROUPS,)),
            pltpu.SemaphoreType.DMA((GROUPS * (n // heads),)),
            pltpu.SemaphoreType.DMA((GROUPS * (n // heads),)),
            pltpu.SemaphoreType.DMA((2,)),
            pltpu.SemaphoreType.DMA((GROUPS + 1,)),
            pltpu.SemaphoreType.DMA((GROUPS + 1,)),
        ],
        compiler_params=pltpu.CompilerParams(
            collective_id=0, has_side_effects=True, vmem_limit_bytes=60 * 1024 * 1024
        ),
    )(q_res, k_res, v_res, q_new, k_new, v_new, admit_dest, admit_slot, boundaries, rate)
    parts = 8
    return pl.pallas_call(
        functools.partial(hand_over, parts),
        out_shape=jax.ShapeDtypeStruct((length, columns), BF16),
        in_specs=[any_spec],
        out_specs=any_spec,
        scratch_shapes=[
            pltpu.VMEM((length, columns), BF16),
            pltpu.SemaphoreType.DMA((parts,)),
            pltpu.SemaphoreType.DMA((parts,)),
        ],
        compiler_params=pltpu.CompilerParams(vmem_limit_bytes=60 * 1024 * 1024),
    )(result)


def solution(mesh):
    in_specs = (
        P("seq", "head"),
        P("seq", "head"),
        P("seq", "head"),
        P("seq", "head"),
        P("seq", "head"),
        P("seq", "head"),
        P("seq"),
        P("seq"),
        P(),
        P("head"),
    )
    out_specs = P("seq", "head")
    return jax.shard_map(body, mesh=mesh, in_specs=in_specs, out_specs=out_specs, check_vma=False)
```

```python
import functools

import jax
import jax.numpy as jnp
from jax import lax
from jax.experimental import pallas as pl
from jax.experimental.pallas import tpu as pltpu
from jax.sharding import PartitionSpec as P

MESH = pl.DeviceIdType.MESH
UNIT = 8
PAIR = 2 * UNIT
CHUNK = 256
HD = 128
F32 = jnp.float32
BF16 = jnp.bfloat16
UNFILLED = 4096
STRIDE = 37
GROUPS = 2


def dot(a, b):
    return jnp.dot(a, b, preferred_element_type=F32)


def dot_t(a, b):
    return lax.dot_general(a, b, (((1,), (1,)), ((), ())), preferred_element_type=F32)


def t_dot(a, b):
    return lax.dot_general(a, b, (((0,), (0,)), ((), ())), preferred_element_type=F32)


def two_terms(x):
    high = x.astype(BF16)
    low = (x - high.astype(F32)).astype(BF16)
    return jnp.concatenate([high, low], axis=1)


def fold(x):
    return x[:, :HD] + x[:, HD:]


def kernel(
    n, plane, q_res, k_res, v_res, q_new, k_new, v_new, dest_ref, slot_ref, bound_ref, rate_ref, out,
    send_row, labels, b_row, b_col,
    q_all, k_all, v_all, kv_stack, q_stack, pay_kv, pay_q, got_kv, got_q, got_labels, place,
    mask, alive, keep, o_local, s_local, end, in1, total, in2, before, out3, in3, done,
    load_sem, send_sem, recv_sem, send2, recv2, out_sem,
):
    me = lax.axis_index("seq")
    z, p = me // plane, lax.rem(me, plane)
    depth = n // plane
    resident = q_res.shape[0]
    length = resident + CHUNK
    chunks = length // CHUNK
    last = chunks - 1
    slots = CHUNK
    columns = q_res.shape[1]
    span = columns // GROUPS
    half = span // 2
    heads_in = plane // GROUPS
    piece_rows = HD // GROUPS

    loads = [
        pltpu.make_async_copy(k_new, kv_stack.at[pl.ds(0, slots)], load_sem.at[0]),
        pltpu.make_async_copy(v_new, kv_stack.at[pl.ds(slots, slots)], load_sem.at[1]),
        pltpu.make_async_copy(q_res, q_all.at[pl.ds(0, resident)], load_sem.at[2]),
        pltpu.make_async_copy(k_res, k_all.at[pl.ds(0, resident)], load_sem.at[3]),
        pltpu.make_async_copy(v_res, v_all.at[pl.ds(0, resident)], load_sem.at[4]),
    ]
    q_loads = [
        pltpu.make_async_copy(
            q_new.at[:, pl.ds(g * span + m * half, half)],
            q_stack.at[g, pl.ds(m * slots, slots)],
            load_sem.at[5 + 2 * g + m],
        )
        for g in range(GROUPS)
        for m in range(2)
    ]
    for load in loads[:2] + q_loads + loads[2:]:
        load.start()

    barrier = pltpu.get_barrier_semaphore()

    def greet(step, carry):
        pl.semaphore_signal(
            barrier, inc=1, device_id={"seq": lax.rem(me + step, n)}, device_id_type=MESH
        )
        return carry

    lax.fori_loop(1, n, greet, 0)

    side = 1 - 2 * lax.rem(me, 2)

    def ahead(step):
        return lax.rem(me + n * STRIDE + side * step * STRIDE, n)

    blocks_in = dest_ref.shape[0]
    back = pow(STRIDE, -1, n)
    lane = lax.broadcasted_iota(jnp.int32, (1, 2 * slots), 1)
    unit = lax.rem(lax.shift_right_logical(lane, 3), blocks_in)
    row = jnp.zeros((1, 2 * slots), jnp.int32)
    label = jnp.full((n, HD), -UNFILLED, jnp.int32)
    label_row = lax.broadcasted_iota(jnp.int32, (n, HD), 0)
    for u in range(blocks_in):
        slot = lax.rem((dest_ref[u] - me) * side * back + n * n, n)
        row = jnp.where(unit == u, slot * PAIR, row)
        label = jnp.where(label_row == slot, slot_ref[u] * UNIT, label)
    send_row[...] = row + (lane & (UNIT - 1)) + (lane // slots) * UNIT

    def label_copy(step):
        return pltpu.make_async_remote_copy(
            src_ref=labels.at[step], dst_ref=got_labels.at[step],
            send_sem=send_sem.at[0], recv_sem=recv_sem.at[0],
            device_id={"seq": ahead(step)}, device_id_type=MESH,
        )

    def kv_copy(g, step):
        rows = pl.ds(pl.multiple_of(step * PAIR, PAIR), PAIR)
        return pltpu.make_async_remote_copy(
            src_ref=pay_kv.at[g, rows], dst_ref=got_kv.at[g, rows],
            send_sem=send_sem.at[4 + g], recv_sem=recv_sem.at[4 + g],
            device_id={"seq": ahead(step)}, device_id_type=MESH,
        )

    def q_copy(g, step):
        rows = pl.ds(pl.multiple_of(step * PAIR, PAIR), PAIR)
        return pltpu.make_async_remote_copy(
            src_ref=pay_q.at[g, rows], dst_ref=got_q.at[g, rows],
            send_sem=send_sem.at[8 + g], recv_sem=recv_sem.at[8 + g],
            device_id={"seq": ahead(step)}, device_id_type=MESH,
        )

    def start_range(copy, low, high):
        def one(step, carry):
            copy(step).start()
            return carry

        lax.fori_loop(low, high, one, 0)

    def pick(base):
        rows = base + lax.broadcasted_iota(jnp.int32, (256, 2 * slots), 0)
        return jnp.where(rows == send_row[...], 1.0, 0.0).astype(BF16)

    def pack_kv(g, base):
        chosen = pick(base)
        for c in range(span // 256):
            pay_kv[g, pl.ds(base, 256), pl.ds(c * 256, 256)] = dot(
                chosen, kv_stack[:, pl.ds(g * span + c * 256, 256)]
            ).astype(BF16)

    for load in loads[:2]:
        load.wait()
    pack_kv(0, 0)
    pl.semaphore_wait(barrier, n - 1)
    group = 256 // PAIR
    kv_first = functools.partial(kv_copy, 0)
    kv_second = functools.partial(kv_copy, 1)
    start_range(kv_first, 1, group)
    for step in range(n):
        labels[step] = label[step : step + 1, :]
    start_range(label_copy, 1, n)
    for part in range(1, n // group):
        pack_kv(0, part * 256)
        start_range(kv_first, part * group, (part + 1) * group)

    def pack_later(step, carry):
        pack_kv(1, pl.multiple_of(step * 256, 256))
        return carry

    lax.fori_loop(0, n // group, pack_later, 0)
    start_range(kv_second, 1, (3 * n) // 8)

    for load in q_loads:
        load.wait()

    def pack_q(step, carry):
        base = pl.multiple_of(step * 256, 256)
        chosen = pick(base)
        for g in range(GROUPS):
            pay_q[g, pl.ds(base, 256)] = dot(chosen, q_stack[g]).astype(BF16)
        return carry

    lax.fori_loop(0, n // group, pack_q, 0)
    for g in range(GROUPS):
        got_kv[g, pl.ds(0, PAIR)] = pay_kv[g, pl.ds(0, PAIR)]
        got_q[g, pl.ds(0, PAIR)] = pay_q[g, pl.ds(0, PAIR)]
    got_labels[0] = labels[0]

    rest = pl.ds(PAIR, (n - 1) * PAIR)

    def all_labels():
        return pltpu.make_async_remote_copy(
            src_ref=labels.at[pl.ds(1, n - 1)], dst_ref=got_labels.at[pl.ds(1, n - 1)],
            send_sem=send_sem.at[0], recv_sem=recv_sem.at[0],
            device_id={"seq": lax.rem(me + 1, n)}, device_id_type=MESH,
        )

    def all_kv(g):
        return pltpu.make_async_remote_copy(
            src_ref=pay_kv.at[g, rest], dst_ref=got_kv.at[g, rest],
            send_sem=send_sem.at[4 + g], recv_sem=recv_sem.at[4 + g],
            device_id={"seq": lax.rem(me + 1, n)}, device_id_type=MESH,
        )

    def all_q(g):
        return pltpu.make_async_remote_copy(
            src_ref=pay_q.at[g, rest], dst_ref=got_q.at[g, rest],
            send_sem=send_sem.at[8 + g], recv_sem=recv_sem.at[8 + g],
            device_id={"seq": lax.rem(me + 1, n)}, device_id_type=MESH,
        )

    count = bound_ref.shape[0]
    across = lax.broadcasted_iota(jnp.int32, (1, HD), 1)
    down = lax.broadcasted_iota(jnp.int32, (count, HD), 0)
    line = jnp.full((1, HD), 2**30, jnp.int32)
    column = jnp.full((count, HD), 2**30, jnp.int32)
    for j in range(count):
        line = jnp.where(across == j, bound_ref[j], line)
        column = jnp.where(down == j, bound_ref[j], column)
    b_row[...] = line
    b_col[...] = column

    def clear(low, high):
        inside = (b_row[...] >= low) & (b_row[...] < high)
        found = jnp.sum(jnp.where(inside, 1.0, 0.0), axis=1, keepdims=True)
        return jnp.where(found == 0.0, 1.0, 0.0)

    def starts_upto(position):
        return jnp.sum(jnp.where(b_row[...] <= position, 1.0, 0.0), axis=1, keepdims=True)

    for c in range(chunks):
        base = me * length + c * CHUNK
        spot = base + lax.broadcasted_iota(jnp.int32, (CHUNK, HD), 0)
        count_col = jnp.sum(jnp.where(b_row[...] <= spot, 1.0, 0.0), axis=1, keepdims=True)
        spot_row = base + lax.broadcasted_iota(jnp.int32, (b_col.shape[0], CHUNK), 1)
        b_wide = jnp.concatenate([b_col[...]] * (CHUNK // HD), axis=1)
        count_row = jnp.sum(jnp.where(b_wide <= spot_row, 1.0, 0.0), axis=0, keepdims=True)
        gap = lax.broadcasted_iota(jnp.int32, (CHUNK, CHUNK), 0) - lax.broadcasted_iota(
            jnp.int32, (CHUNK, CHUNK), 1
        )
        mask[c] = jnp.where((gap >= 0) & (count_col == count_row), 1.0, 0.0)
        wide = jnp.broadcast_to(count_col, (CHUNK, HD))
        alive[c] = jnp.where(wide == starts_upto(base - 1), 1.0, 0.0)
        keep[c] = jnp.where(wide == starts_upto(base + CHUNK - 1), 1.0, 0.0)

    def decay_of(x):
        return jnp.exp(jnp.full((1, HD), x, F32))

    def decay_matrix(rate):
        gap = lax.broadcasted_iota(jnp.int32, (CHUNK, CHUNK), 0) - lax.broadcasted_iota(
            jnp.int32, (CHUNK, CHUNK), 1
        )
        return jnp.exp(-rate * jnp.maximum(gap, 0).astype(F32))

    def step_state(c, h, rate, state):
        rows = pl.ds(c * CHUNK, CHUNK)
        cols = pl.ds(pl.multiple_of(h * HD, HD), HD)
        spot = lax.broadcasted_iota(jnp.int32, (CHUNK, HD), 0).astype(F32)
        weight = jnp.exp(-rate * (CHUNK - 1.0 - spot)) * keep[c]
        fresh = fold(t_dot(k_all[rows, cols], two_terms(v_all[rows, cols].astype(F32) * weight)))
        whole = decay_of(-rate * CHUNK) * alive[c, CHUNK - 1 : CHUNK, :]
        return whole * state + fresh

    def local_part(c, h, decay):
        rows = pl.ds(c * CHUNK, CHUNK)
        cols = pl.ds(pl.multiple_of(h * HD, HD), HD)
        scores = dot_t(q_all[rows, cols], k_all[rows, cols])
        weights = (scores * (decay * mask[c])).astype(BF16)
        return dot(weights, v_all[rows, cols])

    for load in loads[2:]:
        load.wait()

    def resident_head(h, carry):
        rate = rate_ref[h]
        decay = decay_matrix(rate)
        cols = pl.ds(pl.multiple_of(h * HD, HD), HD)
        state = jnp.zeros((HD, HD), F32)
        for c in range(last):
            s_local[c, h] = state
            o_local[pl.ds(c * CHUNK, CHUNK), cols] = local_part(c, h, decay)
            state = step_state(c, h, rate, state)
        s_local[last, h] = state
        return carry

    lax.fori_loop(0, plane, resident_head, 0)

    all_labels().wait_recv()
    lane = lax.broadcasted_iota(jnp.int32, (1, HD), 1)
    owner = lax.shift_right_logical(lane, 4)
    pieces = []
    for c in range(n * PAIR // HD):
        piece = jnp.zeros((1, HD), jnp.int32)
        for o in range(HD // PAIR):
            piece = piece + jnp.where(owner == o, got_labels[c * (HD // PAIR) + o], 0)
        inner = (lane & (UNIT - 1)) + lax.shift_right_logical(lane & UNIT, 3) * slots
        pieces.append(piece + inner)
    for c, piece in enumerate(pieces):
        rows = lax.broadcasted_iota(jnp.int32, (2 * slots, HD), 0)
        place[:, pl.ds(c * HD, HD)] = jnp.where(rows == piece, 1.0, 0.0).astype(BF16)

    def arrange_kv(g):
        def one(step, carry):
            cols = pl.ds(pl.multiple_of(step * 256, 256), 256)
            home = pl.ds(pl.multiple_of(g * span + step * 256, 256), 256)
            whole = dot(place[...], got_kv[g, :, cols]).astype(BF16)
            k_all[pl.ds(resident, slots), home] = whole[:slots]
            v_all[pl.ds(resident, slots), home] = whole[slots:]
            return carry

        lax.fori_loop(0, span // 256, one, 0)

    def first_copy(g, step):
        mate = lax.rem(p + step, plane)
        return pltpu.make_async_remote_copy(
            src_ref=end.at[g * plane + mate], dst_ref=in1.at[g * plane + step],
            send_sem=send_sem.at[6 + g], recv_sem=recv_sem.at[6 + g],
            device_id={"seq": z * plane + mate}, device_id_type=MESH,
        )

    def third_copy(g, step):
        mate = lax.rem(p + step, plane)
        return pltpu.make_async_remote_copy(
            src_ref=out3.at[g * plane + mate], dst_ref=in3.at[g * plane + step],
            send_sem=send_sem.at[2 + g], recv_sem=recv_sem.at[2 + g],
            device_id={"seq": z * plane + mate}, device_id_type=MESH,
        )

    def second_copy(g, step):
        return pltpu.make_async_remote_copy(
            src_ref=total.at[g], dst_ref=in2.at[g * depth + step],
            send_sem=send2.at[g * depth + step], recv_sem=recv2.at[g * depth + step],
            device_id={"seq": lax.rem(me + step * plane, n)}, device_id_type=MESH,
        )

    def all_first(g):
        pieces = pl.ds(g * plane + 1, plane - 1)
        return pltpu.make_async_remote_copy(
            src_ref=end.at[pieces], dst_ref=in1.at[pieces],
            send_sem=send_sem.at[6 + g], recv_sem=recv_sem.at[6 + g],
            device_id={"seq": z * plane + lax.rem(p + 1, plane)}, device_id_type=MESH,
        )

    def all_third(g):
        pieces = pl.ds(g * plane + 1, plane - 1)
        return pltpu.make_async_remote_copy(
            src_ref=out3.at[pieces], dst_ref=in3.at[pieces],
            send_sem=send_sem.at[2 + g], recv_sem=recv_sem.at[2 + g],
            device_id={"seq": z * plane + lax.rem(p + 1, plane)}, device_id_type=MESH,
        )

    plane_rows = plane * length

    def ends(g):
        def one(i, carry):
            h = g * heads_in + i
            state = step_state(last, h, rate_ref[h], s_local[last, h])
            for m in range(GROUPS):
                end[h * GROUPS + m] = state[m * piece_rows : (m + 1) * piece_rows]
            return carry

        lax.fori_loop(0, heads_in, one, 0, unroll=2)
        start_range(functools.partial(first_copy, g), 1, plane)
        in1[g * plane] = end[g * plane + p]

    def totals(g, rate_p):
        all_first(g).wait_recv()
        state = jnp.zeros((piece_rows, HD), F32)
        for m in range(plane):
            shard = z * plane + m
            out3[g * plane + m] = state
            pass_on = decay_of(-rate_p * length) * clear(shard * length, (shard + 1) * length)
            state = pass_on * state + in1[g * plane + lax.rem(p - m + plane, plane)]
        total[g] = state.astype(BF16)
        for step in range(1, depth):
            @pl.when(z + step < depth)
            def _(step=step):
                second_copy(g, step).start()

    def prefixes(g, rate_p):
        before[...] = jnp.zeros((piece_rows, HD), F32)
        for step in range(1, depth):
            @pl.when(z - step >= 0)
            def _(step=step):
                second_copy(g, step).wait_recv()
                factor = decay_of(-rate_p * float(plane_rows * (step - 1))) * clear(
                    (z - step + 1) * plane_rows, z * plane_rows
                )
                before[...] = before[...] + factor * in2[g * depth + step].astype(F32)
        earlier = before[...]
        for m in range(plane):
            factor = decay_of(-rate_p * float(length * m)) * clear(
                z * plane_rows, z * plane_rows + m * length
            )
            out3[g * plane + m] = out3[g * plane + m] + factor * earlier
        start_range(functools.partial(third_copy, g), 1, plane)
        in3[g * plane] = out3[g * plane + p]

    def finish(c, h, rate, local):
        rows = pl.ds(c * CHUNK, CHUNK)
        cols = pl.ds(pl.multiple_of(h * HD, HD), HD)
        reach = decay_of(-rate * float(c * CHUNK))
        for m in range(c):
            reach = reach * alive[m, CHUNK - 1 : CHUNK, :]
        g = h // heads_in
        owner = (h - g * heads_in) * GROUPS
        carried = jnp.concatenate(
            [in3[g * plane + lax.rem(p - owner - m + plane, plane)] for m in range(GROUPS)], axis=0
        )
        carry = s_local[c, h] + reach * carried
        spot = lax.broadcasted_iota(jnp.int32, (CHUNK, HD), 0).astype(F32)
        into = jnp.exp(-rate * (spot + 1.0)) * alive[c]
        whole = local + into * fold(dot(q_all[rows, cols], two_terms(carry)))
        mean = jnp.sum(whole * whole, axis=1, keepdims=True) * (1.0 / HD)
        done[rows, cols] = (whole * lax.rsqrt(mean + 1e-06)).astype(BF16)

    def finish_resident(h, carry):
        rate = rate_ref[h]
        cols = pl.ds(pl.multiple_of(h * HD, HD), HD)
        for c in range(last):
            finish(c, h, rate, o_local[pl.ds(c * CHUNK, CHUNK), cols])
        return carry

    def finish_group(g):
        all_third(g).wait_recv()
        lax.fori_loop(g * heads_in, (g + 1) * heads_in, finish_resident, 0, unroll=2)

    def finish_admitted(h, carry):
        rate = rate_ref[h]
        finish(last, h, rate, local_part(last, h, decay_matrix(rate)))
        return carry

    def finish_new(g):
        all_q(g).wait_recv()
        whole = dot(place[...], got_q[g]).astype(BF16)
        for m in range(2):
            home = pl.ds(g * span + m * half, half)
            q_all[pl.ds(resident, slots), home] = whole[m * slots : (m + 1) * slots]
        lax.fori_loop(g * heads_in, (g + 1) * heads_in, finish_admitted, 0, unroll=4)

    rates = [rate_ref[g * heads_in + p // GROUPS] for g in range(GROUPS)]
    q_first = functools.partial(q_copy, 0)
    q_second = functools.partial(q_copy, 1)

    all_kv(0).wait_recv()
    arrange_kv(0)
    ends(0)
    start_range(kv_second, (3 * n) // 8, (5 * n) // 8)
    totals(0, rates[0])
    start_range(kv_second, (5 * n) // 8, (13 * n) // 16)
    prefixes(0, rates[0])
    start_range(kv_second, (13 * n) // 16, n)
    start_range(q_first, 1, n // 2)

    all_kv(1).wait_recv()
    arrange_kv(1)
    ends(1)
    start_range(q_first, n // 2, n)
    finish_group(0)
    totals(1, rates[1])
    start_range(q_second, 1, n // 2)
    prefixes(1, rates[1])
    start_range(q_second, n // 2, n)
    finish_new(0)
    finish_group(1)
    rows_in = pl.ds(0, resident)
    rows_new = pl.ds(resident, slots)
    store = pltpu.make_async_copy(done.at[rows_in], out.at[rows_in], out_sem.at[0])
    store.start()
    finish_new(1)
    store_new = pltpu.make_async_copy(done.at[rows_new], out.at[rows_new], out_sem.at[1])
    store_new.start()

    all_labels().wait_send()
    for g in range(GROUPS):
        all_kv(g).wait_send()
        all_q(g).wait_send()
        all_first(g).wait_send()
        all_third(g).wait_send()
        for step in range(1, depth):
            @pl.when(z + step < depth)
            def _(g=g, step=step):
                second_copy(g, step).wait_send()
    store.wait()
    store_new.wait()


def hand_over(parts, src, dst, hold, load_sem, store_sem):
    size = src.shape[0] // parts
    pieces = [pl.ds(i * size, size) for i in range(parts)]
    loads = [
        pltpu.make_async_copy(src.at[rows], hold.at[rows], load_sem.at[i])
        for i, rows in enumerate(pieces)
    ]
    stores = [
        pltpu.make_async_copy(hold.at[rows], dst.at[rows], store_sem.at[i])
        for i, rows in enumerate(pieces)
    ]
    for load in loads:
        load.start()
    for load, store in zip(loads, stores):
        load.wait()
        store.start()
    for store in stores:
        store.wait()


def body(q_res, k_res, v_res, q_new, k_new, v_new, admit_dest, admit_slot, boundaries, rate):
    n = lax.axis_size("seq")
    heads = rate.shape[0]
    columns = q_res.shape[1]
    resident, fresh = q_res.shape[0], q_new.shape[0]
    length = resident + fresh
    count = boundaries.shape[0]
    any_spec = pl.BlockSpec(memory_space=pl.ANY)
    smem = pl.BlockSpec(memory_space=pltpu.SMEM)
    chunks = length // CHUNK
    result = pl.pallas_call(
        functools.partial(kernel, n, heads),
        out_shape=jax.ShapeDtypeStruct((length, columns), BF16),
        in_specs=[any_spec] * 6 + [smem] * 4,
        out_specs=any_spec,
        scratch_shapes=[
            pltpu.VMEM((1, 2 * fresh), jnp.int32),
            pltpu.VMEM((n, 1, HD), jnp.int32),
            pltpu.VMEM((1, HD), jnp.int32),
            pltpu.VMEM((count, HD), jnp.int32),
            pltpu.VMEM((length, columns), BF16),
            pltpu.VMEM((length, columns), BF16),
            pltpu.VMEM((length, columns), BF16),
            pltpu.VMEM((2 * fresh, columns), BF16),
            pltpu.VMEM((GROUPS, 2 * fresh, columns // (2 * GROUPS)), BF16),
            pltpu.VMEM((GROUPS, n * PAIR, columns // GROUPS), BF16),
            pltpu.VMEM((GROUPS, n * PAIR, columns // (2 * GROUPS)), BF16),
            pltpu.VMEM((GROUPS, n * PAIR, columns // GROUPS), BF16),
            pltpu.VMEM((GROUPS, n * PAIR, columns // (2 * GROUPS)), BF16),
            pltpu.VMEM((n, 1, HD), jnp.int32),
            pltpu.VMEM((2 * fresh, n * PAIR), BF16),
            pltpu.VMEM((chunks, CHUNK, CHUNK), F32),
            pltpu.VMEM((chunks, CHUNK, HD), F32),
            pltpu.VMEM((chunks, CHUNK, HD), F32),
            pltpu.VMEM((resident, columns), F32),
            pltpu.VMEM((chunks, heads, HD, HD), F32),
            pltpu.VMEM((GROUPS * heads, HD // GROUPS, HD), F32),
            pltpu.VMEM((GROUPS * heads, HD // GROUPS, HD), F32),
            pltpu.VMEM((GROUPS, HD // GROUPS, HD), BF16),
            pltpu.VMEM((GROUPS * (n // heads), HD // GROUPS, HD), BF16),
            pltpu.VMEM((HD // GROUPS, HD), F32),
            pltpu.VMEM((GROUPS * heads, HD // GROUPS, HD), F32),
            pltpu.VMEM((GROUPS * heads, HD // GROUPS, HD), F32),
            pltpu.VMEM((length, columns), BF16),
            pltpu.SemaphoreType.DMA((5 + 2 * GROUPS,)),
            pltpu.SemaphoreType.DMA((4 + 3 * GROUPS,)),
            pltpu.SemaphoreType.DMA((4 + 3 * GROUPS,)),
            pltpu.SemaphoreType.DMA((GROUPS * (n // heads),)),
            pltpu.SemaphoreType.DMA((GROUPS * (n // heads),)),
            pltpu.SemaphoreType.DMA((2,)),
        ],
        compiler_params=pltpu.CompilerParams(
            collective_id=0, has_side_effects=True, vmem_limit_bytes=60 * 1024 * 1024
        ),
    )(q_res, k_res, v_res, q_new, k_new, v_new, admit_dest, admit_slot, boundaries, rate)
    parts = 8
    return pl.pallas_call(
        functools.partial(hand_over, parts),
        out_shape=jax.ShapeDtypeStruct((length, columns), BF16),
        in_specs=[any_spec],
        out_specs=any_spec,
        scratch_shapes=[
            pltpu.VMEM((length, columns), BF16),
            pltpu.SemaphoreType.DMA((parts,)),
            pltpu.SemaphoreType.DMA((parts,)),
        ],
        compiler_params=pltpu.CompilerParams(vmem_limit_bytes=60 * 1024 * 1024),
    )(result)


def solution(mesh):
    in_specs = (
        P("seq", "head"),
        P("seq", "head"),
        P("seq", "head"),
        P("seq", "head"),
        P("seq", "head"),
        P("seq", "head"),
        P("seq"),
        P("seq"),
        P(),
        P("head"),
    )
    out_specs = P("seq", "head")
    return jax.shard_map(body, mesh=mesh, in_specs=in_specs, out_specs=out_specs, check_vma=False)
```

```python
import functools

import jax
import jax.numpy as jnp
from jax import lax
from jax.experimental import pallas as pl
from jax.experimental.pallas import tpu as pltpu
from jax.sharding import PartitionSpec as P

MESH = pl.DeviceIdType.MESH
UNIT = 8
PAIR = 2 * UNIT
CHUNK = 256
HD = 128
F32 = jnp.float32
BF16 = jnp.bfloat16
UNFILLED = 4096
STRIDE = 37
GROUPS = 2


def dot(a, b):
    return jnp.dot(a, b, preferred_element_type=F32)


def dot_t(a, b):
    return lax.dot_general(a, b, (((1,), (1,)), ((), ())), preferred_element_type=F32)


def t_dot(a, b):
    return lax.dot_general(a, b, (((0,), (0,)), ((), ())), preferred_element_type=F32)


def two_terms(x):
    high = x.astype(BF16)
    low = (x - high.astype(F32)).astype(BF16)
    return jnp.concatenate([high, low], axis=1)


def fold(x):
    return x[:, :HD] + x[:, HD:]


def kernel(
    n, plane, q_res, k_res, v_res, q_new, k_new, v_new, dest_ref, slot_ref, bound_ref, rate_ref, out,
    send_row, labels, b_row, b_col,
    q_all, k_all, v_all, kv_stack, q_stack, pay_kv, pay_q, got_kv, got_q, got_labels, place,
    mask, alive, keep, o_local, s_local, end, in1, total, in2, before, out3, in3, done,
    load_sem, send_sem, recv_sem, send2, recv2, out_sem,
):
    me = lax.axis_index("seq")
    z, p = me // plane, lax.rem(me, plane)
    depth = n // plane
    resident = q_res.shape[0]
    length = resident + CHUNK
    chunks = length // CHUNK
    last = chunks - 1
    slots = CHUNK
    columns = q_res.shape[1]
    span = columns // GROUPS
    half = span // 2
    heads_in = plane // GROUPS
    piece_rows = HD // GROUPS

    barrier = pltpu.get_barrier_semaphore()

    def greet(step, carry):
        pl.semaphore_signal(
            barrier, inc=1, device_id={"seq": lax.rem(me + step, n)}, device_id_type=MESH
        )
        return carry

    lax.fori_loop(1, n, greet, 0, unroll=7)

    loads = [
        pltpu.make_async_copy(k_new, kv_stack.at[pl.ds(0, slots)], load_sem.at[0]),
        pltpu.make_async_copy(v_new, kv_stack.at[pl.ds(slots, slots)], load_sem.at[1]),
        pltpu.make_async_copy(q_res, q_all.at[pl.ds(0, resident)], load_sem.at[2]),
        pltpu.make_async_copy(k_res, k_all.at[pl.ds(0, resident)], load_sem.at[3]),
        pltpu.make_async_copy(v_res, v_all.at[pl.ds(0, resident)], load_sem.at[4]),
    ]
    q_loads = [
        pltpu.make_async_copy(
            q_new.at[:, pl.ds(g * span + m * half, half)],
            q_stack.at[g, pl.ds(m * slots, slots)],
            load_sem.at[5 + 2 * g + m],
        )
        for g in range(GROUPS)
        for m in range(2)
    ]
    for load in loads[:2] + q_loads + loads[2:]:
        load.start()

    side = 1 - 2 * lax.rem(me, 2)

    def ahead(step):
        return lax.rem(me + n * STRIDE + side * step * STRIDE, n)

    blocks_in = dest_ref.shape[0]
    back = pow(STRIDE, -1, n)
    lane = lax.broadcasted_iota(jnp.int32, (1, 2 * slots), 1)
    unit = lax.rem(lax.shift_right_logical(lane, 3), blocks_in)
    row = jnp.zeros((1, 2 * slots), jnp.int32)
    label = jnp.full((n, HD), -UNFILLED, jnp.int32)
    label_row = lax.broadcasted_iota(jnp.int32, (n, HD), 0)
    for u in range(blocks_in):
        slot = lax.rem((dest_ref[u] - me) * side * back + n * n, n)
        row = jnp.where(unit == u, slot * PAIR, row)
        label = jnp.where(label_row == slot, slot_ref[u] * UNIT, label)
    send_row[...] = row + (lane & (UNIT - 1)) + (lane // slots) * UNIT

    def label_copy(step):
        return pltpu.make_async_remote_copy(
            src_ref=labels.at[step], dst_ref=got_labels.at[step],
            send_sem=send_sem.at[0], recv_sem=recv_sem.at[0],
            device_id={"seq": ahead(step)}, device_id_type=MESH,
        )

    def kv_copy(g, step):
        rows = pl.ds(pl.multiple_of(step * PAIR, PAIR), PAIR)
        return pltpu.make_async_remote_copy(
            src_ref=pay_kv.at[g, rows], dst_ref=got_kv.at[g, rows],
            send_sem=send_sem.at[4 + g], recv_sem=recv_sem.at[4 + g],
            device_id={"seq": ahead(step)}, device_id_type=MESH,
        )

    def q_copy(g, step):
        rows = pl.ds(pl.multiple_of(step * PAIR, PAIR), PAIR)
        return pltpu.make_async_remote_copy(
            src_ref=pay_q.at[g, rows], dst_ref=got_q.at[g, rows],
            send_sem=send_sem.at[8 + g], recv_sem=recv_sem.at[8 + g],
            device_id={"seq": ahead(step)}, device_id_type=MESH,
        )

    def start_range(copy, low, high):
        def one(step, carry):
            copy(step).start()
            return carry

        lax.fori_loop(low, high, one, 0)

    def pick(base):
        rows = base + lax.broadcasted_iota(jnp.int32, (256, 2 * slots), 0)
        return jnp.where(rows == send_row[...], 1.0, 0.0).astype(BF16)

    def pack_kv(g, base):
        chosen = pick(base)
        for c in range(span // 256):
            pay_kv[g, pl.ds(base, 256), pl.ds(c * 256, 256)] = dot(
                chosen, kv_stack[:, pl.ds(g * span + c * 256, 256)]
            ).astype(BF16)

    for load in loads[:2]:
        load.wait()
    pack_kv(0, 0)
    pl.semaphore_wait(barrier, n - 1)
    group = 256 // PAIR
    kv_first = functools.partial(kv_copy, 0)
    kv_second = functools.partial(kv_copy, 1)
    start_range(kv_first, 1, group)
    for step in range(n):
        labels[step] = label[step : step + 1, :]
    start_range(label_copy, 1, n)
    for part in range(1, n // group):
        pack_kv(0, part * 256)
        start_range(kv_first, part * group, (part + 1) * group)

    def pack_later(step, carry):
        pack_kv(1, pl.multiple_of(step * 256, 256))
        return carry

    lax.fori_loop(0, n // group, pack_later, 0)
    start_range(kv_second, 1, (3 * n) // 4)

    for load in q_loads:
        load.wait()

    def pack_q(step, carry):
        base = pl.multiple_of(step * 256, 256)
        chosen = pick(base)
        for g in range(GROUPS):
            pay_q[g, pl.ds(base, 256)] = dot(chosen, q_stack[g]).astype(BF16)
        return carry

    lax.fori_loop(0, n // group, pack_q, 0)
    for g in range(GROUPS):
        got_kv[g, pl.ds(0, PAIR)] = pay_kv[g, pl.ds(0, PAIR)]
        got_q[g, pl.ds(0, PAIR)] = pay_q[g, pl.ds(0, PAIR)]
    got_labels[0] = labels[0]

    rest = pl.ds(PAIR, (n - 1) * PAIR)

    def all_labels():
        return pltpu.make_async_remote_copy(
            src_ref=labels.at[pl.ds(1, n - 1)], dst_ref=got_labels.at[pl.ds(1, n - 1)],
            send_sem=send_sem.at[0], recv_sem=recv_sem.at[0],
            device_id={"seq": lax.rem(me + 1, n)}, device_id_type=MESH,
        )

    def all_kv(g):
        return pltpu.make_async_remote_copy(
            src_ref=pay_kv.at[g, rest], dst_ref=got_kv.at[g, rest],
            send_sem=send_sem.at[4 + g], recv_sem=recv_sem.at[4 + g],
            device_id={"seq": lax.rem(me + 1, n)}, device_id_type=MESH,
        )

    def all_q(g):
        return pltpu.make_async_remote_copy(
            src_ref=pay_q.at[g, rest], dst_ref=got_q.at[g, rest],
            send_sem=send_sem.at[8 + g], recv_sem=recv_sem.at[8 + g],
            device_id={"seq": lax.rem(me + 1, n)}, device_id_type=MESH,
        )

    count = bound_ref.shape[0]
    across = lax.broadcasted_iota(jnp.int32, (1, HD), 1)
    down = lax.broadcasted_iota(jnp.int32, (count, HD), 0)
    line = jnp.full((1, HD), 2**30, jnp.int32)
    column = jnp.full((count, HD), 2**30, jnp.int32)
    for j in range(count):
        line = jnp.where(across == j, bound_ref[j], line)
        column = jnp.where(down == j, bound_ref[j], column)
    b_row[...] = line
    b_col[...] = column

    def clear(low, high):
        inside = (b_row[...] >= low) & (b_row[...] < high)
        found = jnp.sum(jnp.where(inside, 1.0, 0.0), axis=1, keepdims=True)
        return jnp.where(found == 0.0, 1.0, 0.0)

    def starts_upto(position):
        return jnp.sum(jnp.where(b_row[...] <= position, 1.0, 0.0), axis=1, keepdims=True)

    for c in range(chunks):
        base = me * length + c * CHUNK
        spot = base + lax.broadcasted_iota(jnp.int32, (CHUNK, HD), 0)
        count_col = jnp.sum(jnp.where(b_row[...] <= spot, 1.0, 0.0), axis=1, keepdims=True)
        spot_row = base + lax.broadcasted_iota(jnp.int32, (b_col.shape[0], CHUNK), 1)
        b_wide = jnp.concatenate([b_col[...]] * (CHUNK // HD), axis=1)
        count_row = jnp.sum(jnp.where(b_wide <= spot_row, 1.0, 0.0), axis=0, keepdims=True)
        gap = lax.broadcasted_iota(jnp.int32, (CHUNK, CHUNK), 0) - lax.broadcasted_iota(
            jnp.int32, (CHUNK, CHUNK), 1
        )
        mask[c] = jnp.where((gap >= 0) & (count_col == count_row), 1.0, 0.0)
        wide = jnp.broadcast_to(count_col, (CHUNK, HD))
        alive[c] = jnp.where(wide == starts_upto(base - 1), 1.0, 0.0)
        keep[c] = jnp.where(wide == starts_upto(base + CHUNK - 1), 1.0, 0.0)

    def decay_of(x):
        return jnp.exp(jnp.full((1, HD), x, F32))

    def decay_matrix(rate):
        gap = lax.broadcasted_iota(jnp.int32, (CHUNK, CHUNK), 0) - lax.broadcasted_iota(
            jnp.int32, (CHUNK, CHUNK), 1
        )
        return jnp.exp(-rate * jnp.maximum(gap, 0).astype(F32))

    def step_state(c, h, rate, state):
        rows = pl.ds(c * CHUNK, CHUNK)
        cols = pl.ds(pl.multiple_of(h * HD, HD), HD)
        spot = lax.broadcasted_iota(jnp.int32, (CHUNK, HD), 0).astype(F32)
        weight = jnp.exp(-rate * (CHUNK - 1.0 - spot)) * keep[c]
        fresh = fold(t_dot(k_all[rows, cols], two_terms(v_all[rows, cols].astype(F32) * weight)))
        whole = decay_of(-rate * CHUNK) * alive[c, CHUNK - 1 : CHUNK, :]
        return whole * state + fresh

    def local_part(c, h, decay):
        rows = pl.ds(c * CHUNK, CHUNK)
        cols = pl.ds(pl.multiple_of(h * HD, HD), HD)
        scores = dot_t(q_all[rows, cols], k_all[rows, cols])
        weights = (scores * (decay * mask[c])).astype(BF16)
        return dot(weights, v_all[rows, cols])

    for load in loads[2:]:
        load.wait()

    def resident_head(h, carry):
        rate = rate_ref[h]
        decay = decay_matrix(rate)
        cols = pl.ds(pl.multiple_of(h * HD, HD), HD)
        state = jnp.zeros((HD, HD), F32)
        for c in range(last):
            s_local[c, h] = state
            o_local[pl.ds(c * CHUNK, CHUNK), cols] = local_part(c, h, decay)
            state = step_state(c, h, rate, state)
        s_local[last, h] = state
        return carry

    lax.fori_loop(0, plane, resident_head, 0, unroll=2)

    all_labels().wait_recv()
    lane = lax.broadcasted_iota(jnp.int32, (1, HD), 1)
    owner = lax.shift_right_logical(lane, 4)
    pieces = []
    for c in range(n * PAIR // HD):
        piece = jnp.zeros((1, HD), jnp.int32)
        for o in range(HD // PAIR):
            piece = piece + jnp.where(owner == o, got_labels[c * (HD // PAIR) + o], 0)
        inner = (lane & (UNIT - 1)) + lax.shift_right_logical(lane & UNIT, 3) * slots
        pieces.append(piece + inner)
    for c, piece in enumerate(pieces):
        rows = lax.broadcasted_iota(jnp.int32, (2 * slots, HD), 0)
        place[:, pl.ds(c * HD, HD)] = jnp.where(rows == piece, 1.0, 0.0).astype(BF16)

    def arrange_kv(g):
        for step in range(span // 256):
            home = pl.ds(g * span + step * 256, 256)
            whole = dot(place[...], got_kv[g, :, pl.ds(step * 256, 256)]).astype(BF16)
            k_all[pl.ds(resident, slots), home] = whole[:slots]
            v_all[pl.ds(resident, slots), home] = whole[slots:]

    def first_copy(g, step):
        mate = lax.rem(p + step, plane)
        return pltpu.make_async_remote_copy(
            src_ref=end.at[g * plane + mate], dst_ref=in1.at[g * plane + step],
            send_sem=send_sem.at[6 + g], recv_sem=recv_sem.at[6 + g],
            device_id={"seq": z * plane + mate}, device_id_type=MESH,
        )

    def third_copy(g, step):
        mate = lax.rem(p + step, plane)
        return pltpu.make_async_remote_copy(
            src_ref=out3.at[g * plane + mate], dst_ref=in3.at[g * plane + step],
            send_sem=send_sem.at[2 + g], recv_sem=recv_sem.at[2 + g],
            device_id={"seq": z * plane + mate}, device_id_type=MESH,
        )

    def second_copy(g, step):
        return pltpu.make_async_remote_copy(
            src_ref=total.at[g], dst_ref=in2.at[g * depth + step],
            send_sem=send2.at[g * depth + step], recv_sem=recv2.at[g * depth + step],
            device_id={"seq": lax.rem(me + step * plane, n)}, device_id_type=MESH,
        )

    def all_first(g):
        pieces = pl.ds(g * plane + 1, plane - 1)
        return pltpu.make_async_remote_copy(
            src_ref=end.at[pieces], dst_ref=in1.at[pieces],
            send_sem=send_sem.at[6 + g], recv_sem=recv_sem.at[6 + g],
            device_id={"seq": z * plane + lax.rem(p + 1, plane)}, device_id_type=MESH,
        )

    def all_third(g):
        pieces = pl.ds(g * plane + 1, plane - 1)
        return pltpu.make_async_remote_copy(
            src_ref=out3.at[pieces], dst_ref=in3.at[pieces],
            send_sem=send_sem.at[2 + g], recv_sem=recv_sem.at[2 + g],
            device_id={"seq": z * plane + lax.rem(p + 1, plane)}, device_id_type=MESH,
        )

    plane_rows = plane * length

    def ends(g):
        def one(i, carry):
            h = g * heads_in + i
            state = step_state(last, h, rate_ref[h], s_local[last, h])
            for m in range(GROUPS):
                end[h * GROUPS + m] = state[m * piece_rows : (m + 1) * piece_rows]
            return carry

        lax.fori_loop(0, heads_in, one, 0, unroll=4)
        start_range(functools.partial(first_copy, g), 1, plane)
        in1[g * plane] = end[g * plane + p]

    def totals(g, rate_p):
        all_first(g).wait_recv()
        state = jnp.zeros((piece_rows, HD), F32)
        for m in range(plane):
            shard = z * plane + m
            out3[g * plane + m] = state
            pass_on = decay_of(-rate_p * length) * clear(shard * length, (shard + 1) * length)
            state = pass_on * state + in1[g * plane + lax.rem(p - m + plane, plane)]
        total[g] = state.astype(BF16)
        for step in range(1, depth):
            @pl.when(z + step < depth)
            def _(step=step):
                second_copy(g, step).start()

    def prefixes(g, rate_p):
        before[...] = jnp.zeros((piece_rows, HD), F32)
        for step in range(1, depth):
            @pl.when(z - step >= 0)
            def _(step=step):
                second_copy(g, step).wait_recv()
                factor = decay_of(-rate_p * float(plane_rows * (step - 1))) * clear(
                    (z - step + 1) * plane_rows, z * plane_rows
                )
                before[...] = before[...] + factor * in2[g * depth + step].astype(F32)
        earlier = before[...]
        for m in range(plane):
            factor = decay_of(-rate_p * float(length * m)) * clear(
                z * plane_rows, z * plane_rows + m * length
            )
            out3[g * plane + m] = out3[g * plane + m] + factor * earlier
        start_range(functools.partial(third_copy, g), 1, plane)
        in3[g * plane] = out3[g * plane + p]

    def finish(c, h, rate, local):
        rows = pl.ds(c * CHUNK, CHUNK)
        cols = pl.ds(pl.multiple_of(h * HD, HD), HD)
        reach = decay_of(-rate * float(c * CHUNK))
        for m in range(c):
            reach = reach * alive[m, CHUNK - 1 : CHUNK, :]
        g = h // heads_in
        owner = (h - g * heads_in) * GROUPS
        carried = jnp.concatenate(
            [in3[g * plane + lax.rem(p - owner - m + plane, plane)] for m in range(GROUPS)], axis=0
        )
        carry = s_local[c, h] + reach * carried
        spot = lax.broadcasted_iota(jnp.int32, (CHUNK, HD), 0).astype(F32)
        into = jnp.exp(-rate * (spot + 1.0)) * alive[c]
        whole = local + into * fold(dot(q_all[rows, cols], two_terms(carry)))
        mean = jnp.sum(whole * whole, axis=1, keepdims=True) * (1.0 / HD)
        done[rows, cols] = (whole * lax.rsqrt(mean + 1e-06)).astype(BF16)

    def finish_resident(h, carry):
        rate = rate_ref[h]
        cols = pl.ds(pl.multiple_of(h * HD, HD), HD)
        for c in range(last):
            finish(c, h, rate, o_local[pl.ds(c * CHUNK, CHUNK), cols])
        return carry

    def finish_group(g):
        all_third(g).wait_recv()
        lax.fori_loop(g * heads_in, (g + 1) * heads_in, finish_resident, 0, unroll=4)

    def finish_admitted(h, carry):
        rate = rate_ref[h]
        finish(last, h, rate, local_part(last, h, decay_matrix(rate)))
        return carry

    def finish_new(g):
        all_q(g).wait_recv()
        whole = dot(place[...], got_q[g]).astype(BF16)
        for m in range(2):
            home = pl.ds(g * span + m * half, half)
            q_all[pl.ds(resident, slots), home] = whole[m * slots : (m + 1) * slots]
        lax.fori_loop(g * heads_in, (g + 1) * heads_in, finish_admitted, 0, unroll=4)

    rates = [rate_ref[g * heads_in + p // GROUPS] for g in range(GROUPS)]
    q_first = functools.partial(q_copy, 0)
    q_second = functools.partial(q_copy, 1)

    all_kv(0).wait_recv()
    arrange_kv(0)
    ends(0)
    start_range(kv_second, (3 * n) // 4, n)
    totals(0, rates[0])
    start_range(q_first, 1, n // 2)
    prefixes(0, rates[0])
    start_range(q_first, n // 2, n)

    all_kv(1).wait_recv()
    arrange_kv(1)
    ends(1)
    start_range(q_second, 1, n // 2)
    finish_group(0)
    totals(1, rates[1])
    start_range(q_second, n // 2, n)
    prefixes(1, rates[1])
    finish_new(0)
    finish_group(1)
    rows_in = pl.ds(0, resident)
    rows_new = pl.ds(resident, slots)
    store = pltpu.make_async_copy(done.at[rows_in], out.at[rows_in], out_sem.at[0])
    store.start()
    finish_new(1)
    store_new = pltpu.make_async_copy(done.at[rows_new], out.at[rows_new], out_sem.at[1])
    store_new.start()

    all_labels().wait_send()
    for g in range(GROUPS):
        all_kv(g).wait_send()
        all_q(g).wait_send()
        all_first(g).wait_send()
        all_third(g).wait_send()
        for step in range(1, depth):
            @pl.when(z + step < depth)
            def _(g=g, step=step):
                second_copy(g, step).wait_send()
    store.wait()
    store_new.wait()


def hand_over(parts, src, dst, hold, load_sem, store_sem):
    size = src.shape[0] // parts
    pieces = [pl.ds(i * size, size) for i in range(parts)]
    loads = [
        pltpu.make_async_copy(src.at[rows], hold.at[rows], load_sem.at[i])
        for i, rows in enumerate(pieces)
    ]
    stores = [
        pltpu.make_async_copy(hold.at[rows], dst.at[rows], store_sem.at[i])
        for i, rows in enumerate(pieces)
    ]
    for load in loads:
        load.start()
    for load, store in zip(loads, stores):
        load.wait()
        store.start()
    for store in stores:
        store.wait()


def body(q_res, k_res, v_res, q_new, k_new, v_new, admit_dest, admit_slot, boundaries, rate):
    n = lax.axis_size("seq")
    heads = rate.shape[0]
    columns = q_res.shape[1]
    resident, fresh = q_res.shape[0], q_new.shape[0]
    length = resident + fresh
    count = boundaries.shape[0]
    any_spec = pl.BlockSpec(memory_space=pl.ANY)
    smem = pl.BlockSpec(memory_space=pltpu.SMEM)
    chunks = length // CHUNK
    result = pl.pallas_call(
        functools.partial(kernel, n, heads),
        out_shape=jax.ShapeDtypeStruct((length, columns), BF16),
        in_specs=[any_spec] * 6 + [smem] * 4,
        out_specs=any_spec,
        scratch_shapes=[
            pltpu.VMEM((1, 2 * fresh), jnp.int32),
            pltpu.VMEM((n, 1, HD), jnp.int32),
            pltpu.VMEM((1, HD), jnp.int32),
            pltpu.VMEM((count, HD), jnp.int32),
            pltpu.VMEM((length, columns), BF16),
            pltpu.VMEM((length, columns), BF16),
            pltpu.VMEM((length, columns), BF16),
            pltpu.VMEM((2 * fresh, columns), BF16),
            pltpu.VMEM((GROUPS, 2 * fresh, columns // (2 * GROUPS)), BF16),
            pltpu.VMEM((GROUPS, n * PAIR, columns // GROUPS), BF16),
            pltpu.VMEM((GROUPS, n * PAIR, columns // (2 * GROUPS)), BF16),
            pltpu.VMEM((GROUPS, n * PAIR, columns // GROUPS), BF16),
            pltpu.VMEM((GROUPS, n * PAIR, columns // (2 * GROUPS)), BF16),
            pltpu.VMEM((n, 1, HD), jnp.int32),
            pltpu.VMEM((2 * fresh, n * PAIR), BF16),
            pltpu.VMEM((chunks, CHUNK, CHUNK), F32),
            pltpu.VMEM((chunks, CHUNK, HD), F32),
            pltpu.VMEM((chunks, CHUNK, HD), F32),
            pltpu.VMEM((resident, columns), F32),
            pltpu.VMEM((chunks, heads, HD, HD), F32),
            pltpu.VMEM((GROUPS * heads, HD // GROUPS, HD), F32),
            pltpu.VMEM((GROUPS * heads, HD // GROUPS, HD), F32),
            pltpu.VMEM((GROUPS, HD // GROUPS, HD), BF16),
            pltpu.VMEM((GROUPS * (n // heads), HD // GROUPS, HD), BF16),
            pltpu.VMEM((HD // GROUPS, HD), F32),
            pltpu.VMEM((GROUPS * heads, HD // GROUPS, HD), F32),
            pltpu.VMEM((GROUPS * heads, HD // GROUPS, HD), F32),
            pltpu.VMEM((length, columns), BF16),
            pltpu.SemaphoreType.DMA((5 + 2 * GROUPS,)),
            pltpu.SemaphoreType.DMA((4 + 3 * GROUPS,)),
            pltpu.SemaphoreType.DMA((4 + 3 * GROUPS,)),
            pltpu.SemaphoreType.DMA((GROUPS * (n // heads),)),
            pltpu.SemaphoreType.DMA((GROUPS * (n // heads),)),
            pltpu.SemaphoreType.DMA((2,)),
        ],
        compiler_params=pltpu.CompilerParams(
            collective_id=0, has_side_effects=True, vmem_limit_bytes=60 * 1024 * 1024
        ),
    )(q_res, k_res, v_res, q_new, k_new, v_new, admit_dest, admit_slot, boundaries, rate)
    parts = 8
    return pl.pallas_call(
        functools.partial(hand_over, parts),
        out_shape=jax.ShapeDtypeStruct((length, columns), BF16),
        in_specs=[any_spec],
        out_specs=any_spec,
        scratch_shapes=[
            pltpu.VMEM((length, columns), BF16),
            pltpu.SemaphoreType.DMA((parts,)),
            pltpu.SemaphoreType.DMA((parts,)),
        ],
        compiler_params=pltpu.CompilerParams(vmem_limit_bytes=60 * 1024 * 1024),
    )(result)


def solution(mesh):
    in_specs = (
        P("seq", "head"),
        P("seq", "head"),
        P("seq", "head"),
        P("seq", "head"),
        P("seq", "head"),
        P("seq", "head"),
        P("seq"),
        P("seq"),
        P(),
        P("head"),
    )
    out_specs = P("seq", "head")
    return jax.shard_map(body, mesh=mesh, in_specs=in_specs, out_specs=out_specs, check_vma=False)
```

```python
import functools

import jax
import jax.numpy as jnp
from jax import lax
from jax.experimental import pallas as pl
from jax.experimental.pallas import tpu as pltpu
from jax.sharding import PartitionSpec as P

MESH = pl.DeviceIdType.MESH
UNIT = 8
PAIR = 2 * UNIT
CHUNK = 256
HD = 128
F32 = jnp.float32
BF16 = jnp.bfloat16
UNFILLED = 4096
STRIDE = 37
GROUPS = 2


def dot(a, b):
    return jnp.dot(a, b, preferred_element_type=F32)


def dot_t(a, b):
    return lax.dot_general(a, b, (((1,), (1,)), ((), ())), preferred_element_type=F32)


def t_dot(a, b):
    return lax.dot_general(a, b, (((0,), (0,)), ((), ())), preferred_element_type=F32)


def two_terms(x):
    high = x.astype(BF16)
    low = (x - high.astype(F32)).astype(BF16)
    return jnp.concatenate([high, low], axis=1)


def fold(x):
    return x[:, :HD] + x[:, HD:]


def kernel(
    n, plane, q_res, k_res, v_res, q_new, k_new, v_new, dest_ref, slot_ref, bound_ref, rate_ref, out,
    send_row, labels, b_row, b_col,
    q_all, k_all, v_all, kv_stack, q_stack, pay_kv, pay_q, got_kv, got_q, got_labels, place,
    mask, alive, keep, o_local, s_local, end, in1, total, in2, before, out3, in3, done, own_total, lower_sum, in4,
    load_sem, send_sem, recv_sem, send2, recv2, out_sem, send4, recv4,
):
    me = lax.axis_index("seq")
    z, p = me // plane, lax.rem(me, plane)
    depth = n // plane
    resident = q_res.shape[0]
    length = resident + CHUNK
    chunks = length // CHUNK
    last = chunks - 1
    slots = CHUNK
    columns = q_res.shape[1]
    span = columns // GROUPS
    half = span // 2
    heads_in = plane // GROUPS
    piece_rows = HD // GROUPS

    barrier = pltpu.get_barrier_semaphore()

    def greet(step, carry):
        pl.semaphore_signal(
            barrier, inc=1, device_id={"seq": lax.rem(me + step, n)}, device_id_type=MESH
        )
        return carry

    lax.fori_loop(1, n, greet, 0, unroll=7)

    loads = [
        pltpu.make_async_copy(k_new, kv_stack.at[pl.ds(0, slots)], load_sem.at[0]),
        pltpu.make_async_copy(v_new, kv_stack.at[pl.ds(slots, slots)], load_sem.at[1]),
        pltpu.make_async_copy(q_res, q_all.at[pl.ds(0, resident)], load_sem.at[2]),
        pltpu.make_async_copy(k_res, k_all.at[pl.ds(0, resident)], load_sem.at[3]),
        pltpu.make_async_copy(v_res, v_all.at[pl.ds(0, resident)], load_sem.at[4]),
    ]
    q_loads = [
        pltpu.make_async_copy(
            q_new.at[:, pl.ds(g * span + m * half, half)],
            q_stack.at[g, pl.ds(m * slots, slots)],
            load_sem.at[5 + 2 * g + m],
        )
        for g in range(GROUPS)
        for m in range(2)
    ]
    for load in loads[:2] + q_loads + loads[2:]:
        load.start()

    side = 1 - 2 * lax.rem(me, 2)

    def ahead(step):
        return lax.rem(me + n * STRIDE + side * step * STRIDE, n)

    blocks_in = dest_ref.shape[0]
    back = pow(STRIDE, -1, n)
    lane = lax.broadcasted_iota(jnp.int32, (1, 2 * slots), 1)
    unit = lax.rem(lax.shift_right_logical(lane, 3), blocks_in)
    row = jnp.zeros((1, 2 * slots), jnp.int32)
    label = jnp.full((n, HD), -UNFILLED, jnp.int32)
    label_row = lax.broadcasted_iota(jnp.int32, (n, HD), 0)
    for u in range(blocks_in):
        slot = lax.rem((dest_ref[u] - me) * side * back + n * n, n)
        row = jnp.where(unit == u, slot * PAIR, row)
        label = jnp.where(label_row == slot, slot_ref[u] * UNIT, label)
    send_row[...] = row + (lane & (UNIT - 1)) + (lane // slots) * UNIT

    def label_copy(step):
        return pltpu.make_async_remote_copy(
            src_ref=labels.at[step], dst_ref=got_labels.at[step],
            send_sem=send_sem.at[0], recv_sem=recv_sem.at[0],
            device_id={"seq": ahead(step)}, device_id_type=MESH,
        )

    def kv_copy(g, step):
        rows = pl.ds(pl.multiple_of(step * PAIR, PAIR), PAIR)
        return pltpu.make_async_remote_copy(
            src_ref=pay_kv.at[g, rows], dst_ref=got_kv.at[g, rows],
            send_sem=send_sem.at[4 + g], recv_sem=recv_sem.at[4 + g],
            device_id={"seq": ahead(step)}, device_id_type=MESH,
        )

    def q_copy(g, step):
        rows = pl.ds(pl.multiple_of(step * PAIR, PAIR), PAIR)
        return pltpu.make_async_remote_copy(
            src_ref=pay_q.at[g, rows], dst_ref=got_q.at[g, rows],
            send_sem=send_sem.at[8 + g], recv_sem=recv_sem.at[8 + g],
            device_id={"seq": ahead(step)}, device_id_type=MESH,
        )

    def start_range(copy, low, high):
        def one(step, carry):
            copy(step).start()
            return carry

        lax.fori_loop(low, high, one, 0)

    def pick(base):
        rows = base + lax.broadcasted_iota(jnp.int32, (256, 2 * slots), 0)
        return jnp.where(rows == send_row[...], 1.0, 0.0).astype(BF16)

    def pack_kv(g, base):
        chosen = pick(base)
        for c in range(span // 256):
            pay_kv[g, pl.ds(base, 256), pl.ds(c * 256, 256)] = dot(
                chosen, kv_stack[:, pl.ds(g * span + c * 256, 256)]
            ).astype(BF16)

    for load in loads[:2]:
        load.wait()
    pack_kv(0, 0)
    pl.semaphore_wait(barrier, n - 1)
    group = 256 // PAIR
    kv_first = functools.partial(kv_copy, 0)
    kv_second = functools.partial(kv_copy, 1)
    start_range(kv_first, 1, group)
    for step in range(n):
        labels[step] = label[step : step + 1, :]
    start_range(label_copy, 1, n)
    for part in range(1, n // group):
        pack_kv(0, part * 256)
        start_range(kv_first, part * group, (part + 1) * group)

    def pack_later(step, carry):
        pack_kv(1, pl.multiple_of(step * 256, 256))
        return carry

    lax.fori_loop(0, n // group, pack_later, 0)
    start_range(kv_second, 1, (3 * n) // 4)

    for load in q_loads:
        load.wait()

    def pack_q(step, carry):
        base = pl.multiple_of(step * 256, 256)
        chosen = pick(base)
        for g in range(GROUPS):
            pay_q[g, pl.ds(base, 256)] = dot(chosen, q_stack[g]).astype(BF16)
        return carry

    lax.fori_loop(0, n // group, pack_q, 0)
    for g in range(GROUPS):
        got_kv[g, pl.ds(0, PAIR)] = pay_kv[g, pl.ds(0, PAIR)]
        got_q[g, pl.ds(0, PAIR)] = pay_q[g, pl.ds(0, PAIR)]
    got_labels[0] = labels[0]

    rest = pl.ds(PAIR, (n - 1) * PAIR)

    def all_labels():
        return pltpu.make_async_remote_copy(
            src_ref=labels.at[pl.ds(1, n - 1)], dst_ref=got_labels.at[pl.ds(1, n - 1)],
            send_sem=send_sem.at[0], recv_sem=recv_sem.at[0],
            device_id={"seq": lax.rem(me + 1, n)}, device_id_type=MESH,
        )

    def all_kv(g):
        return pltpu.make_async_remote_copy(
            src_ref=pay_kv.at[g, rest], dst_ref=got_kv.at[g, rest],
            send_sem=send_sem.at[4 + g], recv_sem=recv_sem.at[4 + g],
            device_id={"seq": lax.rem(me + 1, n)}, device_id_type=MESH,
        )

    def all_q(g):
        return pltpu.make_async_remote_copy(
            src_ref=pay_q.at[g, rest], dst_ref=got_q.at[g, rest],
            send_sem=send_sem.at[8 + g], recv_sem=recv_sem.at[8 + g],
            device_id={"seq": lax.rem(me + 1, n)}, device_id_type=MESH,
        )

    count = bound_ref.shape[0]
    across = lax.broadcasted_iota(jnp.int32, (1, HD), 1)
    down = lax.broadcasted_iota(jnp.int32, (count, HD), 0)
    line = jnp.full((1, HD), 2**30, jnp.int32)
    column = jnp.full((count, HD), 2**30, jnp.int32)
    for j in range(count):
        line = jnp.where(across == j, bound_ref[j], line)
        column = jnp.where(down == j, bound_ref[j], column)
    b_row[...] = line
    b_col[...] = column

    def clear(low, high):
        inside = (b_row[...] >= low) & (b_row[...] < high)
        found = jnp.sum(jnp.where(inside, 1.0, 0.0), axis=1, keepdims=True)
        return jnp.where(found == 0.0, 1.0, 0.0)

    def starts_upto(position):
        return jnp.sum(jnp.where(b_row[...] <= position, 1.0, 0.0), axis=1, keepdims=True)

    for c in range(chunks):
        base = me * length + c * CHUNK
        spot = base + lax.broadcasted_iota(jnp.int32, (CHUNK, HD), 0)
        count_col = jnp.sum(jnp.where(b_row[...] <= spot, 1.0, 0.0), axis=1, keepdims=True)
        spot_row = base + lax.broadcasted_iota(jnp.int32, (b_col.shape[0], CHUNK), 1)
        b_wide = jnp.concatenate([b_col[...]] * (CHUNK // HD), axis=1)
        count_row = jnp.sum(jnp.where(b_wide <= spot_row, 1.0, 0.0), axis=0, keepdims=True)
        gap = lax.broadcasted_iota(jnp.int32, (CHUNK, CHUNK), 0) - lax.broadcasted_iota(
            jnp.int32, (CHUNK, CHUNK), 1
        )
        mask[c] = jnp.where((gap >= 0) & (count_col == count_row), 1.0, 0.0)
        wide = jnp.broadcast_to(count_col, (CHUNK, HD))
        alive[c] = jnp.where(wide == starts_upto(base - 1), 1.0, 0.0)
        keep[c] = jnp.where(wide == starts_upto(base + CHUNK - 1), 1.0, 0.0)

    def decay_of(x):
        return jnp.exp(jnp.full((1, HD), x, F32))

    def decay_matrix(rate):
        gap = lax.broadcasted_iota(jnp.int32, (CHUNK, CHUNK), 0) - lax.broadcasted_iota(
            jnp.int32, (CHUNK, CHUNK), 1
        )
        return jnp.exp(-rate * jnp.maximum(gap, 0).astype(F32))

    def step_state(c, h, rate, state):
        rows = pl.ds(c * CHUNK, CHUNK)
        cols = pl.ds(pl.multiple_of(h * HD, HD), HD)
        spot = lax.broadcasted_iota(jnp.int32, (CHUNK, HD), 0).astype(F32)
        weight = jnp.exp(-rate * (CHUNK - 1.0 - spot)) * keep[c]
        fresh = fold(t_dot(k_all[rows, cols], two_terms(v_all[rows, cols].astype(F32) * weight)))
        whole = decay_of(-rate * CHUNK) * alive[c, CHUNK - 1 : CHUNK, :]
        return whole * state + fresh

    def local_part(c, h, decay):
        rows = pl.ds(c * CHUNK, CHUNK)
        cols = pl.ds(pl.multiple_of(h * HD, HD), HD)
        scores = dot_t(q_all[rows, cols], k_all[rows, cols])
        weights = (scores * (decay * mask[c])).astype(BF16)
        return dot(weights, v_all[rows, cols])

    for load in loads[2:]:
        load.wait()

    def resident_head(h, carry):
        rate = rate_ref[h]
        decay = decay_matrix(rate)
        cols = pl.ds(pl.multiple_of(h * HD, HD), HD)
        state = jnp.zeros((HD, HD), F32)
        for c in range(last):
            s_local[c, h] = state
            o_local[pl.ds(c * CHUNK, CHUNK), cols] = local_part(c, h, decay)
            state = step_state(c, h, rate, state)
        s_local[last, h] = state
        return carry

    lax.fori_loop(0, plane, resident_head, 0, unroll=2)

    all_labels().wait_recv()
    lane = lax.broadcasted_iota(jnp.int32, (1, HD), 1)
    owner = lax.shift_right_logical(lane, 4)
    pieces = []
    for c in range(n * PAIR // HD):
        piece = jnp.zeros((1, HD), jnp.int32)
        for o in range(HD // PAIR):
            piece = piece + jnp.where(owner == o, got_labels[c * (HD // PAIR) + o], 0)
        inner = (lane & (UNIT - 1)) + lax.shift_right_logical(lane & UNIT, 3) * slots
        pieces.append(piece + inner)
    for c, piece in enumerate(pieces):
        rows = lax.broadcasted_iota(jnp.int32, (2 * slots, HD), 0)
        place[:, pl.ds(c * HD, HD)] = jnp.where(rows == piece, 1.0, 0.0).astype(BF16)

    def arrange_kv(g):
        for step in range(span // 256):
            home = pl.ds(g * span + step * 256, 256)
            whole = dot(place[...], got_kv[g, :, pl.ds(step * 256, 256)]).astype(BF16)
            k_all[pl.ds(resident, slots), home] = whole[:slots]
            v_all[pl.ds(resident, slots), home] = whole[slots:]

    side_z = depth // 2
    zl = lax.rem(z, side_z)

    def first_copy(g, step):
        mate = lax.rem(p + step, plane)
        return pltpu.make_async_remote_copy(
            src_ref=end.at[g * plane + mate], dst_ref=in1.at[g * plane + step],
            send_sem=send_sem.at[6 + g], recv_sem=recv_sem.at[6 + g],
            device_id={"seq": z * plane + mate}, device_id_type=MESH,
        )

    def third_copy(g, step):
        mate = lax.rem(p + step, plane)
        return pltpu.make_async_remote_copy(
            src_ref=out3.at[g * plane + mate], dst_ref=in3.at[g * plane + step],
            send_sem=send_sem.at[2 + g], recv_sem=recv_sem.at[2 + g],
            device_id={"seq": z * plane + mate}, device_id_type=MESH,
        )

    def second_copy(g, step):
        return pltpu.make_async_remote_copy(
            src_ref=total.at[g], dst_ref=in2.at[g * depth + step],
            send_sem=send2.at[g * depth + step], recv_sem=recv2.at[g * depth + step],
            device_id={"seq": (z - zl + lax.rem(zl + step, side_z)) * plane + p}, device_id_type=MESH,
        )

    def lower_copy(g, u):
        return pltpu.make_async_remote_copy(
            src_ref=lower_sum.at[g], dst_ref=in4.at[g],
            send_sem=send4.at[g * side_z + u], recv_sem=recv4.at[g],
            device_id={"seq": (side_z + u) * plane + p}, device_id_type=MESH,
        )

    def lower_sender(u):
        return side_z - 1 if 2 * u < side_z else 0

    def all_first(g):
        pieces = pl.ds(g * plane + 1, plane - 1)
        return pltpu.make_async_remote_copy(
            src_ref=end.at[pieces], dst_ref=in1.at[pieces],
            send_sem=send_sem.at[6 + g], recv_sem=recv_sem.at[6 + g],
            device_id={"seq": z * plane + lax.rem(p + 1, plane)}, device_id_type=MESH,
        )

    def all_third(g):
        pieces = pl.ds(g * plane + 1, plane - 1)
        return pltpu.make_async_remote_copy(
            src_ref=out3.at[pieces], dst_ref=in3.at[pieces],
            send_sem=send_sem.at[2 + g], recv_sem=recv_sem.at[2 + g],
            device_id={"seq": z * plane + lax.rem(p + 1, plane)}, device_id_type=MESH,
        )

    plane_rows = plane * length

    def ends(g):
        def one(i, carry):
            h = g * heads_in + i
            state = step_state(last, h, rate_ref[h], s_local[last, h])
            for m in range(GROUPS):
                end[h * GROUPS + m] = state[m * piece_rows : (m + 1) * piece_rows]
            return carry

        lax.fori_loop(0, heads_in, one, 0, unroll=4)
        start_range(functools.partial(first_copy, g), 1, plane)
        in1[g * plane] = end[g * plane + p]

    def totals(g, rate_p):
        all_first(g).wait_recv()
        state = jnp.zeros((piece_rows, HD), F32)
        for m in range(plane):
            shard = z * plane + m
            out3[g * plane + m] = state
            pass_on = decay_of(-rate_p * length) * clear(shard * length, (shard + 1) * length)
            state = pass_on * state + in1[g * plane + lax.rem(p - m + plane, plane)]
        total[g] = state.astype(BF16)
        own_total[g] = state
        for step in range(1, side_z):
            second_copy(g, step).start()

    def prefixes(g, rate_p):
        before[...] = jnp.zeros((piece_rows, HD), F32)
        for step in range(1, side_z):
            second_copy(g, step).wait_recv()
        for u in sorted({lower_sender(u): u for u in range(side_z)}.values()):
            @pl.when(z == lower_sender(u))
            def _(u=u):
                whole = jnp.zeros((piece_rows, HD), F32)
                for step in range(side_z):
                    source = lax.rem(z - step + side_z, side_z)
                    value = own_total[g] if step == 0 else in2[g * depth + step].astype(F32)
                    away = (plane_rows * (side_z - 1 - source)).astype(F32)
                    factor = decay_of(-rate_p * away) * clear(
                        (source + 1) * plane_rows, side_z * plane_rows
                    )
                    whole = whole + factor * value
                lower_sum[g] = whole
                for other in range(side_z):
                    if lower_sender(other) == lower_sender(u):
                        lower_copy(g, other).start()
        for step in range(1, side_z):
            @pl.when(zl - step >= 0)
            def _(step=step):
                factor = decay_of(-rate_p * float(plane_rows * (step - 1))) * clear(
                    (z - step + 1) * plane_rows, z * plane_rows
                )
                before[...] = before[...] + factor * in2[g * depth + step].astype(F32)

        @pl.when(z >= side_z)
        def _():
            lower_copy(g, 0).wait_recv()
            away = (plane_rows * zl).astype(F32)
            factor = decay_of(-rate_p * away) * clear(side_z * plane_rows, z * plane_rows)
            before[...] = before[...] + factor * in4[g]

        earlier = before[...]
        for m in range(plane):
            factor = decay_of(-rate_p * float(length * m)) * clear(
                z * plane_rows, z * plane_rows + m * length
            )
            out3[g * plane + m] = out3[g * plane + m] + factor * earlier
        start_range(functools.partial(third_copy, g), 1, plane)
        in3[g * plane] = out3[g * plane + p]

    def finish(c, h, rate, local):
        rows = pl.ds(c * CHUNK, CHUNK)
        cols = pl.ds(pl.multiple_of(h * HD, HD), HD)
        reach = decay_of(-rate * float(c * CHUNK))
        for m in range(c):
            reach = reach * alive[m, CHUNK - 1 : CHUNK, :]
        g = h // heads_in
        owner = (h - g * heads_in) * GROUPS
        carried = jnp.concatenate(
            [in3[g * plane + lax.rem(p - owner - m + plane, plane)] for m in range(GROUPS)], axis=0
        )
        carry = s_local[c, h] + reach * carried
        spot = lax.broadcasted_iota(jnp.int32, (CHUNK, HD), 0).astype(F32)
        into = jnp.exp(-rate * (spot + 1.0)) * alive[c]
        whole = local + into * fold(dot(q_all[rows, cols], two_terms(carry)))
        mean = jnp.sum(whole * whole, axis=1, keepdims=True) * (1.0 / HD)
        done[rows, cols] = (whole * lax.rsqrt(mean + 1e-06)).astype(BF16)

    def finish_resident(h, carry):
        rate = rate_ref[h]
        cols = pl.ds(pl.multiple_of(h * HD, HD), HD)
        for c in range(last):
            finish(c, h, rate, o_local[pl.ds(c * CHUNK, CHUNK), cols])
        return carry

    def finish_group(g):
        all_third(g).wait_recv()
        lax.fori_loop(g * heads_in, (g + 1) * heads_in, finish_resident, 0, unroll=4)

    def finish_admitted(h, carry):
        rate = rate_ref[h]
        finish(last, h, rate, local_part(last, h, decay_matrix(rate)))
        return carry

    def finish_new(g):
        all_q(g).wait_recv()
        whole = dot(place[...], got_q[g]).astype(BF16)
        for m in range(2):
            home = pl.ds(g * span + m * half, half)
            q_all[pl.ds(resident, slots), home] = whole[m * slots : (m + 1) * slots]
        lax.fori_loop(g * heads_in, (g + 1) * heads_in, finish_admitted, 0, unroll=4)

    rates = [rate_ref[g * heads_in + p // GROUPS] for g in range(GROUPS)]
    q_first = functools.partial(q_copy, 0)
    q_second = functools.partial(q_copy, 1)

    all_kv(0).wait_recv()
    arrange_kv(0)
    ends(0)
    start_range(kv_second, (3 * n) // 4, n)
    totals(0, rates[0])
    start_range(q_first, 1, n // 2)
    prefixes(0, rates[0])
    start_range(q_first, n // 2, n)

    all_kv(1).wait_recv()
    arrange_kv(1)
    ends(1)
    start_range(q_second, 1, n // 2)
    finish_group(0)
    totals(1, rates[1])
    start_range(q_second, n // 2, n)
    prefixes(1, rates[1])
    finish_new(0)
    finish_group(1)
    rows_in = pl.ds(0, resident)
    rows_new = pl.ds(resident, slots)
    store = pltpu.make_async_copy(done.at[rows_in], out.at[rows_in], out_sem.at[0])
    store.start()
    finish_new(1)
    store_new = pltpu.make_async_copy(done.at[rows_new], out.at[rows_new], out_sem.at[1])
    store_new.start()

    all_labels().wait_send()
    for g in range(GROUPS):
        all_kv(g).wait_send()
        all_q(g).wait_send()
        all_first(g).wait_send()
        all_third(g).wait_send()
        for step in range(1, side_z):
            second_copy(g, step).wait_send()
        for u in range(side_z):
            @pl.when(z == lower_sender(u))
            def _(g=g, u=u):
                lower_copy(g, u).wait_send()
    store.wait()
    store_new.wait()


def hand_over(parts, src, dst, hold, load_sem, store_sem):
    size = src.shape[0] // parts
    pieces = [pl.ds(i * size, size) for i in range(parts)]
    loads = [
        pltpu.make_async_copy(src.at[rows], hold.at[rows], load_sem.at[i])
        for i, rows in enumerate(pieces)
    ]
    stores = [
        pltpu.make_async_copy(hold.at[rows], dst.at[rows], store_sem.at[i])
        for i, rows in enumerate(pieces)
    ]
    for load in loads:
        load.start()
    for load, store in zip(loads, stores):
        load.wait()
        store.start()
    for store in stores:
        store.wait()


def body(q_res, k_res, v_res, q_new, k_new, v_new, admit_dest, admit_slot, boundaries, rate):
    n = lax.axis_size("seq")
    heads = rate.shape[0]
    columns = q_res.shape[1]
    resident, fresh = q_res.shape[0], q_new.shape[0]
    length = resident + fresh
    count = boundaries.shape[0]
    any_spec = pl.BlockSpec(memory_space=pl.ANY)
    smem = pl.BlockSpec(memory_space=pltpu.SMEM)
    chunks = length // CHUNK
    result = pl.pallas_call(
        functools.partial(kernel, n, heads),
        out_shape=jax.ShapeDtypeStruct((length, columns), BF16),
        in_specs=[any_spec] * 6 + [smem] * 4,
        out_specs=any_spec,
        scratch_shapes=[
            pltpu.VMEM((1, 2 * fresh), jnp.int32),
            pltpu.VMEM((n, 1, HD), jnp.int32),
            pltpu.VMEM((1, HD), jnp.int32),
            pltpu.VMEM((count, HD), jnp.int32),
            pltpu.VMEM((length, columns), BF16),
            pltpu.VMEM((length, columns), BF16),
            pltpu.VMEM((length, columns), BF16),
            pltpu.VMEM((2 * fresh, columns), BF16),
            pltpu.VMEM((GROUPS, 2 * fresh, columns // (2 * GROUPS)), BF16),
            pltpu.VMEM((GROUPS, n * PAIR, columns // GROUPS), BF16),
            pltpu.VMEM((GROUPS, n * PAIR, columns // (2 * GROUPS)), BF16),
            pltpu.VMEM((GROUPS, n * PAIR, columns // GROUPS), BF16),
            pltpu.VMEM((GROUPS, n * PAIR, columns // (2 * GROUPS)), BF16),
            pltpu.VMEM((n, 1, HD), jnp.int32),
            pltpu.VMEM((2 * fresh, n * PAIR), BF16),
            pltpu.VMEM((chunks, CHUNK, CHUNK), F32),
            pltpu.VMEM((chunks, CHUNK, HD), F32),
            pltpu.VMEM((chunks, CHUNK, HD), F32),
            pltpu.VMEM((resident, columns), F32),
            pltpu.VMEM((chunks, heads, HD, HD), F32),
            pltpu.VMEM((GROUPS * heads, HD // GROUPS, HD), F32),
            pltpu.VMEM((GROUPS * heads, HD // GROUPS, HD), F32),
            pltpu.VMEM((GROUPS, HD // GROUPS, HD), BF16),
            pltpu.VMEM((GROUPS * (n // heads), HD // GROUPS, HD), BF16),
            pltpu.VMEM((HD // GROUPS, HD), F32),
            pltpu.VMEM((GROUPS * heads, HD // GROUPS, HD), F32),
            pltpu.VMEM((GROUPS * heads, HD // GROUPS, HD), F32),
            pltpu.VMEM((length, columns), BF16),
            pltpu.VMEM((GROUPS, HD // GROUPS, HD), F32),
            pltpu.VMEM((GROUPS, HD // GROUPS, HD), F32),
            pltpu.VMEM((GROUPS, HD // GROUPS, HD), F32),
            pltpu.SemaphoreType.DMA((5 + 2 * GROUPS,)),
            pltpu.SemaphoreType.DMA((4 + 3 * GROUPS,)),
            pltpu.SemaphoreType.DMA((4 + 3 * GROUPS,)),
            pltpu.SemaphoreType.DMA((GROUPS * (n // heads),)),
            pltpu.SemaphoreType.DMA((GROUPS * (n // heads),)),
            pltpu.SemaphoreType.DMA((2,)),
            pltpu.SemaphoreType.DMA((GROUPS * (n // heads // 2),)),
            pltpu.SemaphoreType.DMA((GROUPS,)),
        ],
        compiler_params=pltpu.CompilerParams(
            collective_id=0, has_side_effects=True, vmem_limit_bytes=60 * 1024 * 1024
        ),
    )(q_res, k_res, v_res, q_new, k_new, v_new, admit_dest, admit_slot, boundaries, rate)
    parts = 8
    return pl.pallas_call(
        functools.partial(hand_over, parts),
        out_shape=jax.ShapeDtypeStruct((length, columns), BF16),
        in_specs=[any_spec],
        out_specs=any_spec,
        scratch_shapes=[
            pltpu.VMEM((length, columns), BF16),
            pltpu.SemaphoreType.DMA((parts,)),
            pltpu.SemaphoreType.DMA((parts,)),
        ],
        compiler_params=pltpu.CompilerParams(vmem_limit_bytes=60 * 1024 * 1024),
    )(result)


def solution(mesh):
    in_specs = (
        P("seq", "head"),
        P("seq", "head"),
        P("seq", "head"),
        P("seq", "head"),
        P("seq", "head"),
        P("seq", "head"),
        P("seq"),
        P("seq"),
        P(),
        P("head"),
    )
    out_specs = P("seq", "head")
    return jax.shard_map(body, mesh=mesh, in_specs=in_specs, out_specs=out_specs, check_vma=False)
```

```python
import functools

import jax
import jax.numpy as jnp
from jax import lax
from jax.experimental import pallas as pl
from jax.experimental.pallas import tpu as pltpu
from jax.sharding import PartitionSpec as P

MESH = pl.DeviceIdType.MESH
UNIT = 8
PAIR = 2 * UNIT
CHUNK = 256
HD = 128
F32 = jnp.float32
BF16 = jnp.bfloat16
UNFILLED = 4096
STRIDE = 37
GROUPS = 2


def dot(a, b):
    return jnp.dot(a, b, preferred_element_type=F32)


def dot_t(a, b):
    return lax.dot_general(a, b, (((1,), (1,)), ((), ())), preferred_element_type=F32)


def t_dot(a, b):
    return lax.dot_general(a, b, (((0,), (0,)), ((), ())), preferred_element_type=F32)


def two_terms(x):
    high = x.astype(BF16)
    low = (x - high.astype(F32)).astype(BF16)
    return jnp.concatenate([high, low], axis=1)


def fold(x):
    return x[:, :HD] + x[:, HD:]


def kernel(
    n, plane, q_res, k_res, v_res, q_new, k_new, v_new, dest_ref, slot_ref, bound_ref, rate_ref, out,
    send_row, labels, b_row, b_col,
    q_all, k_all, v_all, kv_stack, q_stack, pay_kv, pay_q, got_kv, got_q, got_labels, place,
    mask, alive, keep, o_local, s_local, end, in1, total, in2, before, out3, in3, done,
    load_sem, send_sem, recv_sem, send2, recv2, out_sem,
):
    me = lax.axis_index("seq")
    z, p = me // plane, lax.rem(me, plane)
    depth = n // plane
    resident = q_res.shape[0]
    length = resident + CHUNK
    chunks = length // CHUNK
    last = chunks - 1
    slots = CHUNK
    columns = q_res.shape[1]
    span = columns // GROUPS
    half = span // 2
    heads_in = plane // GROUPS
    piece_rows = HD // GROUPS

    barrier = pltpu.get_barrier_semaphore()

    def greet(step, carry):
        pl.semaphore_signal(
            barrier, inc=1, device_id={"seq": lax.rem(me + step, n)}, device_id_type=MESH
        )
        return carry

    lax.fori_loop(1, n, greet, 0, unroll=7)

    loads = [
        pltpu.make_async_copy(k_new, kv_stack.at[pl.ds(0, slots)], load_sem.at[0]),
        pltpu.make_async_copy(v_new, kv_stack.at[pl.ds(slots, slots)], load_sem.at[1]),
        pltpu.make_async_copy(q_res, q_all.at[pl.ds(0, resident)], load_sem.at[2]),
        pltpu.make_async_copy(k_res, k_all.at[pl.ds(0, resident)], load_sem.at[3]),
        pltpu.make_async_copy(v_res, v_all.at[pl.ds(0, resident)], load_sem.at[4]),
    ]
    q_loads = [
        pltpu.make_async_copy(
            q_new.at[:, pl.ds(g * span + m * half, half)],
            q_stack.at[g, pl.ds(m * slots, slots)],
            load_sem.at[5 + 2 * g + m],
        )
        for g in range(GROUPS)
        for m in range(2)
    ]
    for load in loads[:2] + q_loads + loads[2:]:
        load.start()

    side = 1 - 2 * lax.rem(me, 2)

    def ahead(step):
        return lax.rem(me + n * STRIDE + side * step * STRIDE, n)

    blocks_in = dest_ref.shape[0]
    back = pow(STRIDE, -1, n)
    lane = lax.broadcasted_iota(jnp.int32, (1, 2 * slots), 1)
    unit = lax.rem(lax.shift_right_logical(lane, 3), blocks_in)
    row = jnp.zeros((1, 2 * slots), jnp.int32)
    label = jnp.full((n, HD), -UNFILLED, jnp.int32)
    label_row = lax.broadcasted_iota(jnp.int32, (n, HD), 0)
    for u in range(blocks_in):
        slot = lax.rem((dest_ref[u] - me) * side * back + n * n, n)
        row = jnp.where(unit == u, slot * PAIR, row)
        label = jnp.where(label_row == slot, slot_ref[u] * UNIT, label)
    send_row[...] = row + (lane & (UNIT - 1)) + (lane // slots) * UNIT

    def label_copy(step):
        return pltpu.make_async_remote_copy(
            src_ref=labels.at[step], dst_ref=got_labels.at[step],
            send_sem=send_sem.at[0], recv_sem=recv_sem.at[0],
            device_id={"seq": ahead(step)}, device_id_type=MESH,
        )

    def kv_copy(g, step):
        rows = pl.ds(pl.multiple_of(step * PAIR, PAIR), PAIR)
        return pltpu.make_async_remote_copy(
            src_ref=pay_kv.at[g, rows], dst_ref=got_kv.at[g, rows],
            send_sem=send_sem.at[4 + g], recv_sem=recv_sem.at[4 + g],
            device_id={"seq": ahead(step)}, device_id_type=MESH,
        )

    def q_copy(g, step):
        rows = pl.ds(pl.multiple_of(step * PAIR, PAIR), PAIR)
        return pltpu.make_async_remote_copy(
            src_ref=pay_q.at[g, rows], dst_ref=got_q.at[g, rows],
            send_sem=send_sem.at[8 + g], recv_sem=recv_sem.at[8 + g],
            device_id={"seq": ahead(step)}, device_id_type=MESH,
        )

    def start_range(copy, low, high):
        def one(step, carry):
            copy(step).start()
            return carry

        lax.fori_loop(low, high, one, 0)

    def pick(base):
        rows = base + lax.broadcasted_iota(jnp.int32, (256, 2 * slots), 0)
        return jnp.where(rows == send_row[...], 1.0, 0.0).astype(BF16)

    def pack_kv(g, base):
        chosen = pick(base)
        for c in range(span // 256):
            pay_kv[g, pl.ds(base, 256), pl.ds(c * 256, 256)] = dot(
                chosen, kv_stack[:, pl.ds(g * span + c * 256, 256)]
            ).astype(BF16)

    for load in loads[:2]:
        load.wait()
    pack_kv(0, 0)
    pl.semaphore_wait(barrier, n - 1)
    group = 256 // PAIR
    kv_first = functools.partial(kv_copy, 0)
    kv_second = functools.partial(kv_copy, 1)
    start_range(kv_first, 1, group)
    for step in range(n):
        labels[step] = label[step : step + 1, :]
    start_range(label_copy, 1, n)
    for part in range(1, n // group):
        pack_kv(0, part * 256)
        start_range(kv_first, part * group, (part + 1) * group)

    def pack_later(step, carry):
        pack_kv(1, pl.multiple_of(step * 256, 256))
        return carry

    lax.fori_loop(0, n // group, pack_later, 0)
    start_range(kv_second, 1, (3 * n) // 4)

    for load in q_loads:
        load.wait()

    def pack_q(step, carry):
        base = pl.multiple_of(step * 256, 256)
        chosen = pick(base)
        for g in range(GROUPS):
            pay_q[g, pl.ds(base, 256)] = dot(chosen, q_stack[g]).astype(BF16)
        return carry

    lax.fori_loop(0, n // group, pack_q, 0)
    for g in range(GROUPS):
        got_kv[g, pl.ds(0, PAIR)] = pay_kv[g, pl.ds(0, PAIR)]
        got_q[g, pl.ds(0, PAIR)] = pay_q[g, pl.ds(0, PAIR)]
    got_labels[0] = labels[0]

    rest = pl.ds(PAIR, (n - 1) * PAIR)

    def all_labels():
        return pltpu.make_async_remote_copy(
            src_ref=labels.at[pl.ds(1, n - 1)], dst_ref=got_labels.at[pl.ds(1, n - 1)],
            send_sem=send_sem.at[0], recv_sem=recv_sem.at[0],
            device_id={"seq": lax.rem(me + 1, n)}, device_id_type=MESH,
        )

    def all_kv(g):
        return pltpu.make_async_remote_copy(
            src_ref=pay_kv.at[g, rest], dst_ref=got_kv.at[g, rest],
            send_sem=send_sem.at[4 + g], recv_sem=recv_sem.at[4 + g],
            device_id={"seq": lax.rem(me + 1, n)}, device_id_type=MESH,
        )

    def all_q(g):
        return pltpu.make_async_remote_copy(
            src_ref=pay_q.at[g, rest], dst_ref=got_q.at[g, rest],
            send_sem=send_sem.at[8 + g], recv_sem=recv_sem.at[8 + g],
            device_id={"seq": lax.rem(me + 1, n)}, device_id_type=MESH,
        )

    count = bound_ref.shape[0]
    across = lax.broadcasted_iota(jnp.int32, (1, HD), 1)
    down = lax.broadcasted_iota(jnp.int32, (count, HD), 0)
    line = jnp.full((1, HD), 2**30, jnp.int32)
    column = jnp.full((count, HD), 2**30, jnp.int32)
    for j in range(count):
        line = jnp.where(across == j, bound_ref[j], line)
        column = jnp.where(down == j, bound_ref[j], column)
    b_row[...] = line
    b_col[...] = column

    def clear(low, high):
        inside = (b_row[...] >= low) & (b_row[...] < high)
        found = jnp.sum(jnp.where(inside, 1.0, 0.0), axis=1, keepdims=True)
        return jnp.where(found == 0.0, 1.0, 0.0)

    def starts_upto(position):
        return jnp.sum(jnp.where(b_row[...] <= position, 1.0, 0.0), axis=1, keepdims=True)

    for c in range(chunks):
        base = me * length + c * CHUNK
        spot = base + lax.broadcasted_iota(jnp.int32, (CHUNK, HD), 0)
        count_col = jnp.sum(jnp.where(b_row[...] <= spot, 1.0, 0.0), axis=1, keepdims=True)
        spot_row = base + lax.broadcasted_iota(jnp.int32, (b_col.shape[0], CHUNK), 1)
        b_wide = jnp.concatenate([b_col[...]] * (CHUNK // HD), axis=1)
        count_row = jnp.sum(jnp.where(b_wide <= spot_row, 1.0, 0.0), axis=0, keepdims=True)
        gap = lax.broadcasted_iota(jnp.int32, (CHUNK, CHUNK), 0) - lax.broadcasted_iota(
            jnp.int32, (CHUNK, CHUNK), 1
        )
        mask[c] = jnp.where((gap >= 0) & (count_col == count_row), 1.0, 0.0)
        wide = jnp.broadcast_to(count_col, (CHUNK, HD))
        alive[c] = jnp.where(wide == starts_upto(base - 1), 1.0, 0.0)
        keep[c] = jnp.where(wide == starts_upto(base + CHUNK - 1), 1.0, 0.0)

    def decay_of(x):
        return jnp.exp(jnp.full((1, HD), x, F32))

    def decay_matrix(rate):
        gap = lax.broadcasted_iota(jnp.int32, (CHUNK, CHUNK), 0) - lax.broadcasted_iota(
            jnp.int32, (CHUNK, CHUNK), 1
        )
        return jnp.exp(-rate * jnp.maximum(gap, 0).astype(F32))

    def step_state(c, h, rate, state):
        rows = pl.ds(c * CHUNK, CHUNK)
        cols = pl.ds(pl.multiple_of(h * HD, HD), HD)
        spot = lax.broadcasted_iota(jnp.int32, (CHUNK, HD), 0).astype(F32)
        weight = jnp.exp(-rate * (CHUNK - 1.0 - spot)) * keep[c]
        fresh = fold(t_dot(k_all[rows, cols], two_terms(v_all[rows, cols].astype(F32) * weight)))
        whole = decay_of(-rate * CHUNK) * alive[c, CHUNK - 1 : CHUNK, :]
        return whole * state + fresh

    def local_part(c, h, decay):
        rows = pl.ds(c * CHUNK, CHUNK)
        cols = pl.ds(pl.multiple_of(h * HD, HD), HD)
        scores = dot_t(q_all[rows, cols], k_all[rows, cols])
        weights = (scores * (decay * mask[c])).astype(BF16)
        return dot(weights, v_all[rows, cols])

    for load in loads[2:]:
        load.wait()

    def resident_head(h, carry):
        rate = rate_ref[h]
        decay = decay_matrix(rate)
        cols = pl.ds(pl.multiple_of(h * HD, HD), HD)
        state = jnp.zeros((HD, HD), F32)
        for c in range(last):
            s_local[c, h] = state
            o_local[pl.ds(c * CHUNK, CHUNK), cols] = local_part(c, h, decay)
            state = step_state(c, h, rate, state)
        s_local[last, h] = state
        return carry

    lax.fori_loop(0, plane, resident_head, 0, unroll=2)

    all_labels().wait_recv()
    lane = lax.broadcasted_iota(jnp.int32, (1, HD), 1)
    owner = lax.shift_right_logical(lane, 4)
    pieces = []
    for c in range(n * PAIR // HD):
        piece = jnp.zeros((1, HD), jnp.int32)
        for o in range(HD // PAIR):
            piece = piece + jnp.where(owner == o, got_labels[c * (HD // PAIR) + o], 0)
        inner = (lane & (UNIT - 1)) + lax.shift_right_logical(lane & UNIT, 3) * slots
        pieces.append(piece + inner)
    for c, piece in enumerate(pieces):
        rows = lax.broadcasted_iota(jnp.int32, (2 * slots, HD), 0)
        place[:, pl.ds(c * HD, HD)] = jnp.where(rows == piece, 1.0, 0.0).astype(BF16)

    def arrange_kv(g):
        for step in range(span // 256):
            home = pl.ds(g * span + step * 256, 256)
            whole = dot(place[...], got_kv[g, :, pl.ds(step * 256, 256)]).astype(BF16)
            k_all[pl.ds(resident, slots), home] = whole[:slots]
            v_all[pl.ds(resident, slots), home] = whole[slots:]

    def first_copy(g, step):
        mate = lax.rem(p + step, plane)
        return pltpu.make_async_remote_copy(
            src_ref=end.at[g * plane + mate], dst_ref=in1.at[g * plane + step],
            send_sem=send_sem.at[6 + g], recv_sem=recv_sem.at[6 + g],
            device_id={"seq": z * plane + mate}, device_id_type=MESH,
        )

    def third_copy(g, step):
        mate = lax.rem(p + step, plane)
        return pltpu.make_async_remote_copy(
            src_ref=out3.at[g * plane + mate], dst_ref=in3.at[g * plane + step],
            send_sem=send_sem.at[2 + g], recv_sem=recv_sem.at[2 + g],
            device_id={"seq": z * plane + mate}, device_id_type=MESH,
        )

    def second_copy(g, step):
        return pltpu.make_async_remote_copy(
            src_ref=total.at[g], dst_ref=in2.at[g * depth + step],
            send_sem=send2.at[g * depth + step], recv_sem=recv2.at[g * depth + step],
            device_id={"seq": lax.rem(me + step * plane, n)}, device_id_type=MESH,
        )

    def all_first(g):
        pieces = pl.ds(g * plane + 1, plane - 1)
        return pltpu.make_async_remote_copy(
            src_ref=end.at[pieces], dst_ref=in1.at[pieces],
            send_sem=send_sem.at[6 + g], recv_sem=recv_sem.at[6 + g],
            device_id={"seq": z * plane + lax.rem(p + 1, plane)}, device_id_type=MESH,
        )

    def all_third(g):
        pieces = pl.ds(g * plane + 1, plane - 1)
        return pltpu.make_async_remote_copy(
            src_ref=out3.at[pieces], dst_ref=in3.at[pieces],
            send_sem=send_sem.at[2 + g], recv_sem=recv_sem.at[2 + g],
            device_id={"seq": z * plane + lax.rem(p + 1, plane)}, device_id_type=MESH,
        )

    plane_rows = plane * length

    def ends(g):
        def one(i, carry):
            h = g * heads_in + i
            state = step_state(last, h, rate_ref[h], s_local[last, h])
            for m in range(GROUPS):
                end[h * GROUPS + m] = state[m * piece_rows : (m + 1) * piece_rows]
            return carry

        lax.fori_loop(0, heads_in, one, 0, unroll=4)
        start_range(functools.partial(first_copy, g), 1, plane)
        in1[g * plane] = end[g * plane + p]

    def totals(g, rate_p):
        all_first(g).wait_recv()
        state = jnp.zeros((piece_rows, HD), F32)
        for m in range(plane):
            shard = z * plane + m
            out3[g * plane + m] = state
            pass_on = decay_of(-rate_p * length) * clear(shard * length, (shard + 1) * length)
            state = pass_on * state + in1[g * plane + lax.rem(p - m + plane, plane)]
        total[g] = state.astype(BF16)
        for step in range(1, depth):
            @pl.when(z + step < depth)
            def _(step=step):
                second_copy(g, step).start()

    def prefixes(g, rate_p):
        before[...] = jnp.zeros((piece_rows, HD), F32)
        for step in range(1, depth):
            @pl.when(z - step >= 0)
            def _(step=step):
                second_copy(g, step).wait_recv()
                factor = decay_of(-rate_p * float(plane_rows * (step - 1))) * clear(
                    (z - step + 1) * plane_rows, z * plane_rows
                )
                before[...] = before[...] + factor * in2[g * depth + step].astype(F32)
        earlier = before[...]
        for m in range(plane):
            factor = decay_of(-rate_p * float(length * m)) * clear(
                z * plane_rows, z * plane_rows + m * length
            )
            out3[g * plane + m] = out3[g * plane + m] + factor * earlier
        start_range(functools.partial(third_copy, g), 1, plane)
        in3[g * plane] = out3[g * plane + p]

    def finish(c, h, rate, local):
        rows = pl.ds(c * CHUNK, CHUNK)
        cols = pl.ds(pl.multiple_of(h * HD, HD), HD)
        reach = decay_of(-rate * float(c * CHUNK))
        for m in range(c):
            reach = reach * alive[m, CHUNK - 1 : CHUNK, :]
        g = h // heads_in
        owner = (h - g * heads_in) * GROUPS
        carried = jnp.concatenate(
            [in3[g * plane + lax.rem(p - owner - m + plane, plane)] for m in range(GROUPS)], axis=0
        )
        carry = s_local[c, h] + reach * carried
        spot = lax.broadcasted_iota(jnp.int32, (CHUNK, HD), 0).astype(F32)
        into = jnp.exp(-rate * (spot + 1.0)) * alive[c]
        whole = local + into * fold(dot(q_all[rows, cols], two_terms(carry)))
        mean = jnp.sum(whole * whole, axis=1, keepdims=True) * (1.0 / HD)
        done[rows, cols] = (whole * lax.rsqrt(mean + 1e-06)).astype(BF16)

    def finish_resident(h, carry):
        rate = rate_ref[h]
        cols = pl.ds(pl.multiple_of(h * HD, HD), HD)
        for c in range(last):
            finish(c, h, rate, o_local[pl.ds(c * CHUNK, CHUNK), cols])
        return carry

    def finish_heads(low, high):
        lax.fori_loop(low, high, finish_resident, 0, unroll=high - low)

    def finish_group(g):
        all_third(g).wait_recv()
        finish_heads(g * heads_in, (g + 1) * heads_in)

    def finish_admitted(h, carry):
        rate = rate_ref[h]
        finish(last, h, rate, local_part(last, h, decay_matrix(rate)))
        return carry

    def finish_new(g):
        all_q(g).wait_recv()
        whole = dot(place[...], got_q[g]).astype(BF16)
        for m in range(2):
            home = pl.ds(g * span + m * half, half)
            q_all[pl.ds(resident, slots), home] = whole[m * slots : (m + 1) * slots]
        lax.fori_loop(g * heads_in, (g + 1) * heads_in, finish_admitted, 0, unroll=4)

    rates = [rate_ref[g * heads_in + p // GROUPS] for g in range(GROUPS)]
    q_first = functools.partial(q_copy, 0)
    q_second = functools.partial(q_copy, 1)

    all_kv(0).wait_recv()
    arrange_kv(0)
    ends(0)
    start_range(kv_second, (3 * n) // 4, n)
    totals(0, rates[0])
    start_range(q_first, 1, n // 2)
    prefixes(0, rates[0])
    start_range(q_first, n // 2, n)

    all_kv(1).wait_recv()
    arrange_kv(1)
    ends(1)
    start_range(q_second, 1, n // 2)
    all_third(0).wait_recv()
    finish_heads(0, heads_in // 2)
    totals(1, rates[1])
    start_range(q_second, n // 2, n)
    finish_heads(heads_in // 2, heads_in)
    prefixes(1, rates[1])
    finish_new(0)
    finish_group(1)
    rows_in = pl.ds(0, resident)
    rows_new = pl.ds(resident, slots)
    store = pltpu.make_async_copy(done.at[rows_in], out.at[rows_in], out_sem.at[0])
    store.start()
    finish_new(1)
    store_new = pltpu.make_async_copy(done.at[rows_new], out.at[rows_new], out_sem.at[1])
    store_new.start()

    all_labels().wait_send()
    for g in range(GROUPS):
        all_kv(g).wait_send()
        all_q(g).wait_send()
        all_first(g).wait_send()
        all_third(g).wait_send()
        for step in range(1, depth):
            @pl.when(z + step < depth)
            def _(g=g, step=step):
                second_copy(g, step).wait_send()
    store.wait()
    store_new.wait()


def hand_over(parts, src, dst, hold, load_sem, store_sem):
    size = src.shape[0] // parts
    pieces = [pl.ds(i * size, size) for i in range(parts)]
    loads = [
        pltpu.make_async_copy(src.at[rows], hold.at[rows], load_sem.at[i])
        for i, rows in enumerate(pieces)
    ]
    stores = [
        pltpu.make_async_copy(hold.at[rows], dst.at[rows], store_sem.at[i])
        for i, rows in enumerate(pieces)
    ]
    for load in loads:
        load.start()
    for load, store in zip(loads, stores):
        load.wait()
        store.start()
    for store in stores:
        store.wait()


def body(q_res, k_res, v_res, q_new, k_new, v_new, admit_dest, admit_slot, boundaries, rate):
    n = lax.axis_size("seq")
    heads = rate.shape[0]
    columns = q_res.shape[1]
    resident, fresh = q_res.shape[0], q_new.shape[0]
    length = resident + fresh
    count = boundaries.shape[0]
    any_spec = pl.BlockSpec(memory_space=pl.ANY)
    smem = pl.BlockSpec(memory_space=pltpu.SMEM)
    chunks = length // CHUNK
    result = pl.pallas_call(
        functools.partial(kernel, n, heads),
        out_shape=jax.ShapeDtypeStruct((length, columns), BF16),
        in_specs=[any_spec] * 6 + [smem] * 4,
        out_specs=any_spec,
        scratch_shapes=[
            pltpu.VMEM((1, 2 * fresh), jnp.int32),
            pltpu.VMEM((n, 1, HD), jnp.int32),
            pltpu.VMEM((1, HD), jnp.int32),
            pltpu.VMEM((count, HD), jnp.int32),
            pltpu.VMEM((length, columns), BF16),
            pltpu.VMEM((length, columns), BF16),
            pltpu.VMEM((length, columns), BF16),
            pltpu.VMEM((2 * fresh, columns), BF16),
            pltpu.VMEM((GROUPS, 2 * fresh, columns // (2 * GROUPS)), BF16),
            pltpu.VMEM((GROUPS, n * PAIR, columns // GROUPS), BF16),
            pltpu.VMEM((GROUPS, n * PAIR, columns // (2 * GROUPS)), BF16),
            pltpu.VMEM((GROUPS, n * PAIR, columns // GROUPS), BF16),
            pltpu.VMEM((GROUPS, n * PAIR, columns // (2 * GROUPS)), BF16),
            pltpu.VMEM((n, 1, HD), jnp.int32),
            pltpu.VMEM((2 * fresh, n * PAIR), BF16),
            pltpu.VMEM((chunks, CHUNK, CHUNK), F32),
            pltpu.VMEM((chunks, CHUNK, HD), F32),
            pltpu.VMEM((chunks, CHUNK, HD), F32),
            pltpu.VMEM((resident, columns), F32),
            pltpu.VMEM((chunks, heads, HD, HD), F32),
            pltpu.VMEM((GROUPS * heads, HD // GROUPS, HD), F32),
            pltpu.VMEM((GROUPS * heads, HD // GROUPS, HD), F32),
            pltpu.VMEM((GROUPS, HD // GROUPS, HD), BF16),
            pltpu.VMEM((GROUPS * (n // heads), HD // GROUPS, HD), BF16),
            pltpu.VMEM((HD // GROUPS, HD), F32),
            pltpu.VMEM((GROUPS * heads, HD // GROUPS, HD), F32),
            pltpu.VMEM((GROUPS * heads, HD // GROUPS, HD), F32),
            pltpu.VMEM((length, columns), BF16),
            pltpu.SemaphoreType.DMA((5 + 2 * GROUPS,)),
            pltpu.SemaphoreType.DMA((4 + 3 * GROUPS,)),
            pltpu.SemaphoreType.DMA((4 + 3 * GROUPS,)),
            pltpu.SemaphoreType.DMA((GROUPS * (n // heads),)),
            pltpu.SemaphoreType.DMA((GROUPS * (n // heads),)),
            pltpu.SemaphoreType.DMA((2,)),
        ],
        compiler_params=pltpu.CompilerParams(
            collective_id=0, has_side_effects=True, vmem_limit_bytes=60 * 1024 * 1024
        ),
    )(q_res, k_res, v_res, q_new, k_new, v_new, admit_dest, admit_slot, boundaries, rate)
    parts = 8
    return pl.pallas_call(
        functools.partial(hand_over, parts),
        out_shape=jax.ShapeDtypeStruct((length, columns), BF16),
        in_specs=[any_spec],
        out_specs=any_spec,
        scratch_shapes=[
            pltpu.VMEM((length, columns), BF16),
            pltpu.SemaphoreType.DMA((parts,)),
            pltpu.SemaphoreType.DMA((parts,)),
        ],
        compiler_params=pltpu.CompilerParams(vmem_limit_bytes=60 * 1024 * 1024),
    )(result)


def solution(mesh):
    in_specs = (
        P("seq", "head"),
        P("seq", "head"),
        P("seq", "head"),
        P("seq", "head"),
        P("seq", "head"),
        P("seq", "head"),
        P("seq"),
        P("seq"),
        P(),
        P("head"),
    )
    out_specs = P("seq", "head")
    return jax.shard_map(body, mesh=mesh, in_specs=in_specs, out_specs=out_specs, check_vma=False)
```
